128 devices in a mesh: user: 16 (over x, y_lo, core), cand: 8 (over z, y_hi).
Axes of the slice: x: 4, y: 4 (y_hi: 2, y_lo: 2; y = y_hi * 2 + y_lo), z: 4, core: 2. Of those that a mesh axis runs over, the one named last changes fastest.
Arguments:
- pooled: bfloat16 [16, 32, 1024, 1024], P('user', None, 'cand'), may hold values from -6 to 6
- cand_feats: bfloat16 [65536, 1024], P(('user', 'cand')), may hold values from -6 to 6
- hist_len: int32 [32], P('user'), may hold values from 1 to 1024, 16384 in all
- cand_user: int32 [65536], P(('user', 'cand')), may hold values from 0 to 31, as said below
- w_in: bfloat16 [1024, 4096], replicated, may hold values from -0.1875 to 0.1875
- w_out: bfloat16 [1024, 1024], replicated, may hold values from -0.1875 to 0.1875
Outputs:
- hist_out: bfloat16 [32, 1024, 1024], P('user', 'cand')
- cand_out: bfloat16 [65536, 1024], P(('user', 'cand'))
The draws below stay inside these ranges and needn't reach their ends.
Inputs may be any that keep to these rules, and one draw needn't show every extreme that they name: `hist_len`: the lengths sum to 16384, and the longest is 1024. `cand_user`: candidate row r belongs to one of the 2 users numbered from (r // 4096) * 2 on.
All inputs are finite; a program needn't handle non-finite values. No bound on the sum of `hist_len` on one device may be relied on, other than what follows from the above.
Results may differ from the reference program's by a relative error of at most 0.022.
Values may be sent and summed in bfloat16 or wider, within the bound.
No kernel may reach another device: no remote copies, remote signals or barrier semaphores. Data moves between devices by JAX's collectives and lax.ppermute only.
A program may use at most 128 MiB of HBM per device.

```python
import math
import jax
import jax.numpy as jnp
import numpy as np
from jax import lax

D = 1024
H = 8
HD = 128
USERS_DEV = 2
HIST = 1024
CAND_DEV = 512
USERS = 32
TABLES = 16
CANDS = 65536
N_CAND = 8


def draw_cand_user(key, part):
    key = jax.random.fold_in(key, 11)
    rows = jnp.arange(CANDS, dtype=jnp.int32)
    group = rows // (CANDS // (USERS // USERS_DEV))
    pick = jax.random.randint(key, (CANDS,), 0, USERS_DEV, dtype=jnp.int32)
    return group * USERS_DEV + pick


def with_spikes(values, rng, source, target, parts, factor):
    def block_of(dim):
        return (jnp.arange(values.shape[dim]) // (values.shape[dim] // parts)).reshape((-1,) + (1,) * (values.ndim - 1 - dim))

    near = jax.random.permutation(rng, parts)[block_of(target)]
    second = (block_of(target) + parts // 2) % parts
    return jnp.where((block_of(source) == near) | (block_of(source) == second), factor * values, values)


def shard_levels(own_key, shape, split, smallest, largest):
    loudness, own = 1.0, jax.random.fold_in(own_key, 6)
    for axis_at, parts in split:
        heights = jnp.exp(jax.random.uniform(jax.random.fold_in(own, axis_at), (parts,), jnp.float32, smallest / len(split), largest / len(split)))
        loudness = loudness * jnp.repeat(heights, shape[axis_at] // parts).reshape([-1 if axis == axis_at else 1 for axis in range(len(shape))])
    return loudness


def split_up(amount, total, limit, lean):
    loads = [(1 << 20) // math.isqrt(rank ** lean) + 1 for rank in range(2, amount + 1)]
    rest, given = total - limit - (amount - 1), [1] * (amount - 1)
    while rest > 0:
        free = [i for i in range(amount - 1) if given[i] < limit]
        mass, remaining = sum([loads[i] for i in free]), rest
        for i in free:
            addition = min(limit - given[i], max(1, remaining * loads[i] // mass), rest)
            given[i] = given[i] + addition
            rest = rest - addition
    return np.array([limit] + given)


def uneven(own_key, number_of, total, reach, slope):
    if number_of == 2:
        one = jax.random.randint(own_key, (), max(1, total - reach), min(reach, total - 1) + 1)
        return jnp.stack([one, total - one])
    sizes = jnp.asarray(split_up(number_of, total, reach, slope), jnp.int32)
    couples = (number_of - 1) // 2
    source_of, sink = sizes[1:1 + 2 * couples:2], sizes[2:2 + 2 * couples:2]
    margin = jnp.minimum(source_of - 1, reach - sink)
    passed = jax.random.randint(jax.random.fold_in(own_key, 1), (couples,), 0, 1 << 20) % (margin + 1)
    sizes = sizes.at[1:1 + 2 * couples:2].set(source_of - passed).at[2:2 + 2 * couples:2].set(sink + passed)
    return sizes[jax.random.permutation(jax.random.fold_in(own_key, 2), number_of)]


def noise(key, extent, scale, reach, cuts=(), kind=jnp.bfloat16):
    factor_of = shard_levels(key, extent, cuts, -0.22, 0.18) if cuts else 1.0
    entries = jax.random.normal(key, extent, jnp.float32) * scale * factor_of
    return jnp.minimum(jnp.maximum(entries, -reach), reach).astype(kind)


def bell_draw_with(own_key, shape, deviation, limit, cuts, heavy, kind=jnp.bfloat16):
    entries = deviation * jax.random.normal(own_key, shape, jnp.float32)
    if cuts:
        entries = entries * shard_levels(own_key, shape, cuts, -0.22, 0.18)
    return jnp.clip(with_spikes(entries, jax.random.fold_in(own_key, 3), *heavy), -limit, limit).astype(kind)


def setup_inputs(seed: int = 0) -> dict:
    streams_of = jax.random.split(jax.random.key(seed), 7)
    return {
        "pooled": bell_draw_with(streams_of[0], (TABLES, USERS, HIST, D), 1.0, 6.0, ((0, 16), (2, 8)), (0, 1, 16, 2.0)),
        "cand_feats": noise(streams_of[1], (CANDS, D), 1.0, 6.0, ((0, 128),)),
        "hist_len": uneven(streams_of[2], USERS, USERS * HIST // 2, HIST, 2).astype(jnp.int32),
        "cand_user": draw_cand_user(jax.random.fold_in(streams_of[6], 71), 0),
        "w_in": noise(streams_of[4], (D, 4 * D), D ** -0.5, 0.1875),
        "w_out": noise(streams_of[5], (D, D), D ** -0.5, 0.1875),
    }


def layer_norm(rows):
    mean = lax.optimization_barrier(jnp.mean(rows, axis=-1, keepdims=True))
    centered = rows - mean
    var = lax.optimization_barrier(jnp.mean(centered * centered, axis=-1, keepdims=True))
    return centered * lax.rsqrt(var + 1e-05)

def project(feats, w_in):
    proj = jax.nn.silu(jnp.dot(feats, w_in, preferred_element_type=jnp.float32))
    width = w_in.shape[0]
    return tuple((proj[:, j * width:(j + 1) * width].astype(jnp.bfloat16) for j in range(4)))

def attend(queries, keys, values, mask):
    rows = queries.shape[0]
    nkeys = keys.shape[0]
    head_q = queries.reshape(rows, H, HD).astype(jnp.float32)
    head_k = keys.reshape(nkeys, H, HD).astype(jnp.float32)
    head_v = values.reshape(nkeys, H, HD).astype(jnp.float32)
    scores = jnp.einsum('qhd,khd->hqk', head_q, head_k) / jnp.sqrt(jnp.float32(HD))
    weights = jnp.where(mask[None], jax.nn.silu(scores), 0.0).astype(jnp.bfloat16)
    summed = jnp.einsum('hqk,khd->qhd', weights.astype(jnp.float32), head_v)
    return summed

def finish(summed, upart, feats, w_out):
    rows = summed.shape[0]
    mixed = (layer_norm(summed.reshape(rows, D)) * upart.astype(jnp.float32)).astype(jnp.bfloat16)
    return jnp.dot(mixed, w_out, preferred_element_type=jnp.float32) + feats.astype(jnp.float32)

def reference(pooled, cand_feats, hist_len, cand_user, w_in, w_out):
    positions = jnp.arange(HIST, dtype=jnp.int32)

    def hist_user(user):
        slab = lax.dynamic_index_in_dim(pooled, user, 1, keepdims=False)
        feats = layer_norm(lax.optimization_barrier(jnp.sum(slab, axis=0, dtype=jnp.float32))).astype(jnp.bfloat16)
        upart, vpart, qpart, kpart = project(feats, w_in)
        length = lax.dynamic_index_in_dim(hist_len, user, 0, keepdims=False)
        mask = (positions[None, :] <= positions[:, None]) & (positions[None, :] < length)
        result = finish(attend(qpart, kpart, vpart, mask), upart, feats, w_out)
        result = jnp.where(positions[:, None] < length, result, 0.0).astype(jnp.bfloat16)
        return (result, kpart, vpart)
    hist_out, keys, values = lax.map(hist_user, jnp.arange(USERS, dtype=jnp.int32))

    def cand_block(block):
        group = block // N_CAND
        feats_raw = lax.dynamic_slice_in_dim(cand_feats, (block * CAND_DEV).astype(jnp.int32), CAND_DEV, 0)
        owners = lax.dynamic_slice_in_dim(cand_user, (block * CAND_DEV).astype(jnp.int32), CAND_DEV, 0)
        first = (group * USERS_DEV).astype(jnp.int32)
        group_keys = lax.dynamic_slice_in_dim(keys, first, USERS_DEV, 0).reshape(USERS_DEV * HIST, D)
        group_values = lax.dynamic_slice_in_dim(values, first, USERS_DEV, 0).reshape(USERS_DEV * HIST, D)
        group_lens = lax.dynamic_slice_in_dim(hist_len, first, USERS_DEV, 0)
        flat = jnp.arange(USERS_DEV * HIST, dtype=jnp.int32)
        key_user = flat // HIST
        live = flat % HIST < group_lens[key_user]
        mask = (owners[:, None] == (first + key_user)[None, :]) & live[None, :]
        feats = layer_norm(feats_raw.astype(jnp.float32)).astype(jnp.bfloat16)
        upart, vpart, qpart, kpart = project(feats, w_in)
        summed = attend(qpart, group_keys, group_values, mask)
        own = (qpart.astype(jnp.float32) * kpart.astype(jnp.float32)).reshape(CAND_DEV, H, HD).sum(-1)
        own = jax.nn.silu(own / jnp.sqrt(jnp.float32(HD))).astype(jnp.bfloat16).astype(jnp.float32)
        summed = summed + own[:, :, None] * vpart.reshape(CAND_DEV, H, HD).astype(jnp.float32)
        return finish(summed, upart, feats, w_out).astype(jnp.bfloat16)
    cand_out = lax.map(cand_block, jnp.arange(CANDS // CAND_DEV, dtype=jnp.int32)).reshape(CANDS, D)
    return (hist_out, cand_out)
```

```python
import functools

import jax
import jax.numpy as jnp
from jax import lax
from jax.experimental import pallas as pl
from jax.experimental.pallas import tpu as pltpu
from jax.sharding import PartitionSpec as P

F32 = jnp.float32
BF16 = jnp.bfloat16
HEADS = 8
HD = 128
D = 1024
SLOTS = 128
ROWS = 512
NX, NZ = 4, 4
BLK = 128
WIDE = 256
STEPS = D // WIDE
HALF_SCALE = 0.5 / (HD**0.5)
VMEM = 56 * 1024 * 1024


def silu(v):
    half = v * 0.5
    return half + half * jnp.tanh(half)


def layer_norm(rows):
    mean = jnp.mean(rows, axis=-1, keepdims=True)
    centered = rows - mean
    var = jnp.mean(centered * centered, axis=-1, keepdims=True)
    return centered * lax.rsqrt(var + 1e-05)


def mm(a, b):
    return jnp.dot(a, b, preferred_element_type=F32)


def weights_of(queries, keys):
    s = lax.dot_general(queries, keys, (((1,), (1,)), ((), ())), preferred_element_type=F32)
    half = s * HALF_SCALE
    return half + half * jnp.tanh(half)


def cand_kernel(owner_ref, feats_ref, w_ref, xs_ref, u_ref, q_ref, a_ref, v_scr):
    step = pl.program_id(0)

    @pl.when(step == 0)
    def _():
        second = owner_ref[...].astype(F32)
        r_from = lax.broadcasted_iota(jnp.int32, (ROWS, ROWS), 0)
        r_to = lax.broadcasted_iota(jnp.int32, (ROWS, ROWS), 1)
        upper = jnp.where(r_from <= r_to, 1.0, 0.0).astype(BF16)
        ones_before = mm(jnp.broadcast_to(second, (8, ROWS)).astype(BF16), upper)[:1]
        index = lax.broadcasted_iota(jnp.int32, (1, ROWS), 1).astype(F32)
        n_first = ROWS - jnp.sum(second, axis=1, keepdims=True)
        place = jnp.where(second > 0.5, n_first + ones_before - 1.0, index - ones_before)
        onehot = jnp.where(r_from == place.astype(jnp.int32), 1.0, 0.0).astype(BF16)
        x = layer_norm(feats_ref[...].astype(F32)).astype(BF16)
        xs_ref[...] = mm(onehot, x).astype(BF16)

    proj = silu(mm(xs_ref[...], w_ref[...])).astype(BF16)

    @pl.when(step == 0)
    def _():
        u_ref[...] = proj

    @pl.when(step == 1)
    def _():
        v_scr[...] = proj

    @pl.when(step == 2)
    def _():
        q_ref[...] = proj

    @pl.when(step == 3)
    def _():
        prod = q_ref[...].astype(F32) * proj.astype(F32)
        for h in range(HEADS):
            cols = slice(h * HD, (h + 1) * HD)
            half = jnp.sum(prod[:, cols], axis=-1, keepdims=True) * HALF_SCALE
            own = (half + half * jnp.tanh(half)).astype(BF16).astype(F32)
            a_ref[:, cols] = own * v_scr[:, cols].astype(F32)


def cand_project(owner_row, feats, w_in):
    whole = lambda i: (0, 0)
    return pl.pallas_call(
        cand_kernel,
        grid=(4,),
        in_specs=[
            pl.BlockSpec((1, ROWS), whole),
            pl.BlockSpec((ROWS, D), whole),
            pl.BlockSpec((D, D), lambda i: (0, i)),
        ],
        out_specs=[pl.BlockSpec((ROWS, D), whole)] * 4,
        out_shape=[
            jax.ShapeDtypeStruct((ROWS, D), BF16),
            jax.ShapeDtypeStruct((ROWS, D), BF16),
            jax.ShapeDtypeStruct((ROWS, D), BF16),
            jax.ShapeDtypeStruct((ROWS, D), F32),
        ],
        scratch_shapes=[pltpu.VMEM((ROWS, D), BF16)],
        compiler_params=pltpu.CompilerParams(vmem_limit_bytes=VMEM),
        cost_estimate=pl.CostEstimate(
            flops=2 * ROWS * D * 4 * D, bytes_accessed=16 << 20, transcendentals=ROWS * 4 * D
        ),
        name="cand_project",
    )(owner_row, feats, w_in)


def attend_kernel(last, scal_ref, *refs):
    x_refs = refs[:4]
    wu_ref, wv_ref, wq_ref, wk_ref, wo_ref, q_ref, a_in_ref = refs[4:11]
    refs = refs[11:]
    if last:
        u_ref, xs_ref, owner_ref, hist_ref, out_ref, k_scr, v_scr, u_scr, ah_scr, a_ref = refs
    else:
        hist_ref, a_ref, k_scr, v_scr, u_scr, ah_scr = refs
    step = pl.program_id(0)
    length = scal_ref[0]
    row_lo = scal_ref[1]
    row_hi = scal_ref[2]
    my_off = scal_ref[3]
    cols = pl.ds(pl.multiple_of(step * WIDE, WIDE), WIDE)
    x_own = x_refs[0][0]
    row_iota = lax.broadcasted_iota(jnp.int32, (SLOTS, 1), 0)

    @pl.when(step == 0)
    def _():
        a_ref[...] = a_in_ref[...]

    for p in range(4):
        x = x_refs[p][...].reshape(2 * SLOTS, D)
        rows = slice(p * 2 * SLOTS, (p + 1) * 2 * SLOTS)
        k_scr[rows, :] = silu(mm(x, wk_ref[...])).astype(BF16)
        v = silu(mm(x, wv_ref[...])).astype(BF16)
        for e in range(2):
            piece = v[e * SLOTS : (e + 1) * SLOTS]
            off = scal_ref[4 + 2 * p + e]
            at = (2 * p + e) * SLOTS
            v_scr[at : at + SLOTS, :] = jnp.where(row_iota < length - off, piece, jnp.zeros_like(piece))

    u_scr[:, cols] = silu(mm(x_own, wu_ref[...])).astype(BF16)
    q_hist = silu(mm(x_own, wq_ref[...])).astype(BF16)
    ahead = lax.broadcasted_iota(jnp.int32, (SLOTS, SLOTS), 0) - lax.broadcasted_iota(
        jnp.int32, (SLOTS, SLOTS), 1
    )
    for h in range(WIDE // HD):
        hc = slice(h * HD, (h + 1) * HD)
        w = weights_of(q_hist[:, hc], k_scr[:, hc])
        parts = []
        for n in range(8):
            seen = ahead >= scal_ref[4 + n] - my_off
            parts.append(jnp.where(seen, w[:, n * SLOTS : (n + 1) * SLOTS], 0.0).astype(BF16))
        out_cols = pl.ds(pl.multiple_of(step * WIDE + h * HD, HD), HD)
        ah_scr[:, out_cols] = mm(jnp.concatenate(parts, axis=1), v_scr[:, hc])

    first_block = row_lo // BLK
    end_block = (row_hi + BLK - 1) // BLK

    @pl.loop(first_block, end_block)
    def _(blk):
        start = pl.multiple_of(blk * BLK, BLK)
        rows = pl.ds(start, BLK)
        index = start + lax.broadcasted_iota(jnp.int32, (BLK, 1), 0)
        mine = (index >= row_lo) & (index < row_hi)
        for h in range(WIDE // HD):
            hc = slice(h * HD, (h + 1) * HD)
            out_cols = pl.ds(pl.multiple_of(step * WIDE + h * HD, HD), HD)
            w = weights_of(q_ref[rows, out_cols], k_scr[:, hc]).astype(BF16)
            part = mm(w, v_scr[:, hc])
            a_ref[rows, out_cols] += jnp.where(mine, part, 0.0)

    @pl.when(step == STEPS - 1)
    def _():
        y = (layer_norm(ah_scr[...]) * u_scr[...].astype(F32)).astype(BF16)
        res = mm(y, wo_ref[...]) + x_own.astype(F32)
        hist_ref[...] = jnp.where(my_off + row_iota < length, res, 0.0).astype(BF16)
        if last:
            yc = (layer_norm(a_ref[...]) * u_ref[...].astype(F32)).astype(BF16)
            done = (mm(yc, wo_ref[...]) + xs_ref[...].astype(F32)).astype(BF16)
            r_row = lax.broadcasted_iota(jnp.int32, (ROWS, ROWS), 0)
            r_col = lax.broadcasted_iota(jnp.int32, (ROWS, ROWS), 1)
            second = owner_ref[...].astype(F32)
            lower = jnp.where(r_col <= r_row, 1.0, 0.0).astype(BF16)
            ones_before = mm(lower, jnp.broadcast_to(second, (ROWS, HD)).astype(BF16))[:, :1]
            index = lax.broadcasted_iota(jnp.int32, (ROWS, 1), 0).astype(F32)
            n_first = ROWS - jnp.sum(second, axis=0, keepdims=True)
            place = jnp.where(second > 0.5, n_first + ones_before - 1.0, index - ones_before)
            back = jnp.where(r_col == place.astype(jnp.int32), 1.0, 0.0).astype(BF16)
            out_ref[...] = mm(back, done).astype(BF16)


def attend(last, scal, pieces, w_in, w_out, q_cand, a_cand, extra):
    whole = lambda i, s: (0, 0)
    part = lambda n: pl.BlockSpec((D, WIDE), lambda i, s: (0, n * STEPS + i))
    rows_spec = pl.BlockSpec((ROWS, D), whole)
    in_specs = [pl.BlockSpec((2, SLOTS, D), lambda i, s: (0, 0, 0))] * 4
    in_specs += [part(0), part(1), part(2), part(3), pl.BlockSpec((D, D), whole)]
    in_specs += [rows_spec, rows_spec]
    hist_spec = pl.BlockSpec((SLOTS, D), whole)
    hist_shape = jax.ShapeDtypeStruct((SLOTS, D), BF16)
    scratch = [
        pltpu.VMEM((8 * SLOTS, WIDE), BF16),
        pltpu.VMEM((8 * SLOTS, WIDE), BF16),
        pltpu.VMEM((SLOTS, D), BF16),
        pltpu.VMEM((SLOTS, D), F32),
    ]
    if last:
        in_specs += [rows_spec, rows_spec, pl.BlockSpec((ROWS, 1), whole)]
        out_specs = [hist_spec, rows_spec]
        out_shape = [hist_shape, jax.ShapeDtypeStruct((ROWS, D), BF16)]
        scratch.append(pltpu.VMEM((ROWS, D), F32))
    else:
        out_specs = [hist_spec, rows_spec]
        out_shape = [hist_shape, jax.ShapeDtypeStruct((ROWS, D), F32)]
    return pl.pallas_call(
        functools.partial(attend_kernel, last),
        grid_spec=pltpu.PrefetchScalarGridSpec(
            num_scalar_prefetch=1,
            grid=(STEPS,),
            in_specs=in_specs,
            out_specs=out_specs,
            scratch_shapes=scratch,
        ),
        out_shape=out_shape,
        compiler_params=pltpu.CompilerParams(vmem_limit_bytes=VMEM),
        cost_estimate=pl.CostEstimate(
            flops=12 * 10**9, bytes_accessed=24 << 20, transcendentals=4 * 10**6
        ),
        name="attend_last" if last else "attend_first",
    )(scal, *pieces, w_in, w_in, w_in, w_in, w_out, q_cand, a_cand, *extra)


def user_at(x, y, core):
    return (x * 2 + y) * 2 + core


def user_perm(dx, dy, dcore):
    pairs = []
    for u in range(4 * NX):
        x, y, core = u >> 2, (u >> 1) & 1, u & 1
        pairs.append((u, user_at((x + dx) % NX, y ^ dy, core ^ dcore)))
    return pairs


def cand_perm(dz, dy):
    return [(c, (((c >> 1) + dz) % NZ) * 2 + ((c & 1) ^ dy)) for c in range(2 * NZ)]


def pick(array, at, axis):
    return lax.dynamic_index_in_dim(array, at, axis, keepdims=False)


def reduce_tables(view, x, y, core):
    with jax.named_scope("sum_core"):
        got = lax.ppermute(pick(view, 1 - core, 2), "user", user_perm(0, 0, 1))
        mine = pick(view, core, 2)
        toward = []
        for d in range(NX):
            to = lax.rem(x + d, NX)
            pair = pick(mine, to, 0).astype(F32) + pick(got, to, 0).astype(F32)
            toward.append(pair.astype(BF16))
    with jax.named_scope("sum_x"):
        arrived = [lax.ppermute(toward[d], "user", user_perm(d, 0, 0)) for d in (1, 3, 2)]
        total = toward[0].astype(F32)
        for got in arrived:
            total = total + got.astype(F32)
    with jax.named_scope("sum_y"):
        other = lax.ppermute(pick(total, 1 - y, 0).astype(BF16), "user", user_perm(0, 1, 0))
        return pick(total, y, 0) + other.astype(F32)


def local(pooled, cand_feats, hist_len, cand_user, w_in, w_out):
    user = lax.axis_index("user")
    cand = lax.axis_index("cand")
    x, y, core = user >> 2, (user >> 1) & 1, user & 1
    z, y_hi = cand >> 1, cand & 1
    owner = cand_user - 2 * user
    n_first = ROWS - jnp.sum(owner)
    xs, u_cand, q_cand, a_cand = cand_project(owner.reshape(1, ROWS), cand_feats, w_in)
    view = pooled.reshape(NX, 2, 2, 2, SLOTS, D)
    offsets = []
    for dz in (0, -1, 1, 2):
        for e in range(2):
            offsets.append(SLOTS * (((z + dz + NZ) % NZ) * 2 + (y_hi ^ e)))
    gathered = []
    for j in range(2):
        emb = reduce_tables(view[:, :, :, j], x, y, core)
        with jax.named_scope("gather"):
            own = layer_norm(emb).astype(BF16)
            near = lax.ppermute(own, "cand", cand_perm(0, 1))
            pair = jnp.stack([own, near])
            gathered.append(
                [pair] + [lax.ppermute(pair, "cand", cand_perm(dz, 0)) for dz in (1, -1, 2)]
            )
    outs = []
    for j in range(2):
        last = j == 1
        rows = [n_first, jnp.int32(ROWS)] if last else [jnp.int32(0), n_first]
        scal = jnp.stack([hist_len[j]] + rows + [cand * SLOTS] + offsets).astype(jnp.int32)
        extra = (u_cand, xs, owner.reshape(ROWS, 1)) if last else ()
        out, a_cand = attend(last, scal, gathered[j], w_in, w_out, q_cand, a_cand, extra)
        outs.append(out)
    return jnp.stack(outs), a_cand


def solution(mesh):
    placed = (
        P("user", None, "cand", None),
        P(("user", "cand"), None),
        P("user"),
        P(("user", "cand")),
        P(),
        P(),
    )
    return jax.shard_map(
        local,
        mesh=mesh,
        in_specs=placed,
        out_specs=(P("user", "cand", None), P(("user", "cand"), None)),
        check_vma=False,
    )
```

```python
import functools

import jax
import jax.numpy as jnp
from jax import lax
from jax.experimental import pallas as pl
from jax.experimental.pallas import tpu as pltpu
from jax.sharding import PartitionSpec as P

F32 = jnp.float32
BF16 = jnp.bfloat16
HEADS = 8
HD = 128
D = 1024
SLOTS = 128
ROWS = 512
NX, NZ = 4, 4
WINDOW = 320
HALF_SCALE = 0.5 / (HD**0.5)
VMEM = 48 * 1024 * 1024
SHIFTS = (0, -1, 1, 2)


def silu(v):
    half = v * 0.5
    return half + half * jnp.tanh(half)


def layer_norm(rows):
    mean = jnp.mean(rows, axis=-1, keepdims=True)
    centered = rows - mean
    var = jnp.mean(centered * centered, axis=-1, keepdims=True)
    return centered * lax.rsqrt(var + 1e-05)


def mm(a, b):
    return jnp.dot(a, b, preferred_element_type=F32)


def weights_of(queries, keys):
    s = lax.dot_general(queries, keys, (((1,), (1,)), ((), ())), preferred_element_type=F32)
    half = s * HALF_SCALE
    return half + half * jnp.tanh(half)


def cand_kernel(owner_ref, feats_ref, w_ref, xs_ref, u_ref, q_ref, a_ref, v_scr):
    step = pl.program_id(0)

    @pl.when(step == 0)
    def _():
        second = owner_ref[...].astype(F32)
        r_from = lax.broadcasted_iota(jnp.int32, (ROWS, ROWS), 0)
        r_to = lax.broadcasted_iota(jnp.int32, (ROWS, ROWS), 1)
        upper = jnp.where(r_from <= r_to, 1.0, 0.0).astype(BF16)
        ones_before = mm(jnp.broadcast_to(second, (8, ROWS)).astype(BF16), upper)[:1]
        index = lax.broadcasted_iota(jnp.int32, (1, ROWS), 1).astype(F32)
        n_first = ROWS - jnp.sum(second, axis=1, keepdims=True)
        place = jnp.where(second > 0.5, n_first + ones_before - 1.0, index - ones_before)
        onehot = jnp.where(r_from == place.astype(jnp.int32), 1.0, 0.0).astype(BF16)
        x = layer_norm(feats_ref[...].astype(F32)).astype(BF16)
        xs_ref[...] = mm(onehot, x).astype(BF16)

    proj = silu(mm(xs_ref[...], w_ref[...])).astype(BF16)

    @pl.when(step == 0)
    def _():
        u_ref[...] = proj

    @pl.when(step == 1)
    def _():
        v_scr[...] = proj

    @pl.when(step == 2)
    def _():
        q_ref[...] = proj

    @pl.when(step == 3)
    def _():
        prod = q_ref[...].astype(F32) * proj.astype(F32)
        for h in range(HEADS):
            cols = slice(h * HD, (h + 1) * HD)
            half = jnp.sum(prod[:, cols], axis=-1, keepdims=True) * HALF_SCALE
            own = (half + half * jnp.tanh(half)).astype(BF16).astype(F32)
            a_ref[:, cols] = own * v_scr[:, cols].astype(F32)


def cand_project(owner_row, feats, w_in):
    whole = lambda i: (0, 0)
    return pl.pallas_call(
        cand_kernel,
        grid=(4,),
        in_specs=[
            pl.BlockSpec((1, ROWS), whole),
            pl.BlockSpec((ROWS, D), whole),
            pl.BlockSpec((D, D), lambda i: (0, i)),
        ],
        out_specs=[pl.BlockSpec((ROWS, D), whole)] * 4,
        out_shape=[
            jax.ShapeDtypeStruct((ROWS, D), BF16),
            jax.ShapeDtypeStruct((ROWS, D), BF16),
            jax.ShapeDtypeStruct((ROWS, D), BF16),
            jax.ShapeDtypeStruct((ROWS, D), F32),
        ],
        scratch_shapes=[pltpu.VMEM((ROWS, D), BF16)],
        compiler_params=pltpu.CompilerParams(vmem_limit_bytes=VMEM),
        cost_estimate=pl.CostEstimate(
            flops=10**6, bytes_accessed=1 << 16, transcendentals=0
        ),
        name="cand_project",
    )(owner_row, feats, w_in)


def absorb_kernel(plan, scal_ref, *refs):
    width, users, first, final = plan["width"], plan["users"], plan["first"], plan["final"]
    refs = list(refs)
    take = lambda n: [refs.pop(0) for _ in range(n)]
    keys = [(user, shift, e, ref) for (user, shift, es), ref in zip(plan["items"], take(len(plan["items"]))) for e in es]
    wk_ref, wv_ref, q_ref, a_in_ref = take(4)
    if first:
        wu_ref, wq_ref = take(2)
        own_ref = dict(zip(users, take(len(users))))
    else:
        qh_in = dict(zip(users, take(len(users))))
        ah_in = dict(zip(users, take(len(users))))
    if final:
        uh_in = dict(zip(users, take(len(users))))
        xh_in = dict(zip(users, take(len(users))))
        u_ref, xs_ref, owner_ref, wo_ref = take(4)
        hist_ref, cand_ref, a_ref = take(3)
        ah_ref = dict(zip(users, take(len(users))))
    else:
        (a_ref,) = take(1)
        ah_ref = dict(zip(users, take(len(users))))
        if first:
            qh_out = dict(zip(users, take(len(users))))
            uh_out = dict(zip(users, take(len(users))))
    step = pl.program_id(0)
    base = pl.multiple_of(step * width, width) if final else 0
    at = lambda lo, n: pl.ds(pl.multiple_of(base + lo, HD), n)
    row_iota = lax.broadcasted_iota(jnp.int32, (SLOTS, 1), 0)
    ahead = lax.broadcasted_iota(jnp.int32, (SLOTS, SLOTS), 0) - lax.broadcasted_iota(
        jnp.int32, (SLOTS, SLOTS), 1
    )
    a_ref[:, at(0, width)] = a_in_ref[...]
    for user in users:
        length = scal_ref[user, 0]
        row_lo = scal_ref[user, 1]
        row_hi = scal_ref[user, 2]
        my_off = scal_ref[user, 3]
        if first:
            x_own = own_ref[user][...]
            q_hist = silu(mm(x_own, wq_ref[...])).astype(BF16)
            qh_out[user][...] = q_hist
            uh_out[user][...] = silu(mm(x_own, wu_ref[...])).astype(BF16)
            ah_ref[user][:, at(0, width)] = jnp.zeros((SLOTS, width), F32)
        else:
            q_hist = qh_in[user][...]
            ah_ref[user][:, at(0, width)] = ah_in[user][...]
        mine_keys = [(shift, e, ref) for (u, shift, e, ref) in keys if u == user]
        blocks = []
        for n in range(0, len(mine_keys), 2):
            two = mine_keys[n : n + 2]
            x = jnp.concatenate([ref[min(e, ref.shape[0] - 1)] for _, e, ref in two], axis=0)
            k = silu(mm(x, wk_ref[...])).astype(BF16)
            v = silu(mm(x, wv_ref[...])).astype(BF16)
            parts = []
            offs = [scal_ref[user, 4 + 2 * SHIFTS.index(shift) + e] for shift, e, _ in two]
            for i, off in enumerate(offs):
                piece = v[i * SLOTS : (i + 1) * SLOTS]
                parts.append(jnp.where(row_iota < length - off, piece, jnp.zeros_like(piece)))
            blocks.append((k, jnp.concatenate(parts, axis=0), offs))

        def attend(start, count):
            rows = pl.ds(start, count)
            index = start + lax.broadcasted_iota(jnp.int32, (count, 1), 0)
            mine = (index >= row_lo) & (index < row_hi)
            for h in range(width // HD):
                hc = slice(h * HD, (h + 1) * HD)
                q = jnp.concatenate([q_ref[rows, hc], q_hist[:, hc]], axis=0)
                total = None
                for k, v, offs in blocks:
                    w = weights_of(q, k[:, hc])
                    parts = []
                    for i, off in enumerate(offs):
                        part = w[count:, i * SLOTS : (i + 1) * SLOTS]
                        parts.append(jnp.where(ahead >= off - my_off, part, 0.0).astype(BF16))
                    w = jnp.concatenate([w[:count].astype(BF16), jnp.concatenate(parts, axis=1)], axis=0)
                    pv = mm(w, v[:, hc])
                    total = pv if total is None else total + pv
                a_ref[rows, at(h * HD, HD)] += jnp.where(mine, total[:count], 0.0)
                ah_ref[user][:, at(h * HD, HD)] += total[count:]

        start = jnp.minimum((row_lo // 16) * 16, ROWS - WINDOW)
        narrow = row_hi <= start + WINDOW

        @pl.when(narrow)
        def _():
            attend(pl.multiple_of(start, 16), WINDOW)

        @pl.when(jnp.logical_not(narrow))
        def _():
            attend(0, ROWS)

    if final:

        @pl.when(step == D // width - 1)
        def _():
            for user in users:
                y = (layer_norm(ah_ref[user][...]) * uh_in[user][...].astype(F32)).astype(BF16)
                res = mm(y, wo_ref[...]) + xh_in[user][...].astype(F32)
                keep = scal_ref[user, 3] + row_iota < scal_ref[user, 0]
                hist_ref[user] = jnp.where(keep, res, 0.0).astype(BF16)
            yc = (layer_norm(a_ref[...]) * u_ref[...].astype(F32)).astype(BF16)
            done = (mm(yc, wo_ref[...]) + xs_ref[...].astype(F32)).astype(BF16)
            r_row = lax.broadcasted_iota(jnp.int32, (ROWS, ROWS), 0)
            r_col = lax.broadcasted_iota(jnp.int32, (ROWS, ROWS), 1)
            second = owner_ref[...].astype(F32)
            lower = jnp.where(r_col <= r_row, 1.0, 0.0).astype(BF16)
            ones_before = mm(lower, jnp.broadcast_to(second, (ROWS, HD)).astype(BF16))[:, :1]
            index = lax.broadcasted_iota(jnp.int32, (ROWS, 1), 0).astype(F32)
            n_first = ROWS - jnp.sum(second, axis=0, keepdims=True)
            place = jnp.where(second > 0.5, n_first + ones_before - 1.0, index - ones_before)
            back = jnp.where(r_col == place.astype(jnp.int32), 1.0, 0.0).astype(BF16)
            cand_ref[...] = mm(back, done).astype(BF16)


def absorb(name, scal, items, w_in, q_cand, a_cand, width=512, first=None, state=None, final=None):
    steps = D // width
    users = tuple(sorted({item[0] for item in items}))
    plan = dict(items=tuple(item[:3] for item in items), users=users, width=width, first=first is not None, final=final is not None)
    whole = lambda i, s: (0, 0)
    col = lambda rows: pl.BlockSpec((rows, width), lambda i, s: (0, i))
    part = lambda n: pl.BlockSpec((D, width), lambda i, s: (0, n * steps + i))
    full = lambda *shape: pl.BlockSpec(shape, lambda i, s: (0,) * len(shape))
    args, in_specs = [], []

    def give(array, spec):
        args.append(array)
        in_specs.append(spec)

    for item in items:
        give(item[3], full(*item[3].shape))
    give(w_in, part(3))
    give(w_in, part(1))
    give(q_cand, col(ROWS))
    give(a_cand, col(ROWS))
    if first is not None:
        give(w_in, part(0))
        give(w_in, part(2))
        for user in users:
            give(first[user], full(SLOTS, D))
    else:
        for user in users:
            give(state[user][0], col(SLOTS))
        for user in users:
            give(state[user][2], col(SLOTS))
    scratch = []
    if final is not None:
        for user in users:
            give(state[user][1], full(SLOTS, D))
        for user in users:
            give(final["own"][user], full(SLOTS, D))
        give(final["u"], full(ROWS, D))
        give(final["xs"], full(ROWS, D))
        give(final["owner"], full(ROWS, 1))
        give(final["w_out"], full(D, D))
        out_specs = [full(len(users), SLOTS, D), full(ROWS, D)]
        out_shape = [
            jax.ShapeDtypeStruct((len(users), SLOTS, D), BF16),
            jax.ShapeDtypeStruct((ROWS, D), BF16),
        ]
        scratch = [pltpu.VMEM((ROWS, D), F32)] + [pltpu.VMEM((SLOTS, D), F32)] * len(users)
    else:
        out_specs = [col(ROWS)] + [col(SLOTS)] * len(users)
        out_shape = [jax.ShapeDtypeStruct((ROWS, D), F32)]
        out_shape += [jax.ShapeDtypeStruct((SLOTS, D), F32)] * len(users)
        if first is not None:
            out_specs += [col(SLOTS)] * (2 * len(users))
            out_shape += [jax.ShapeDtypeStruct((SLOTS, D), BF16)] * (2 * len(users))
    outs = pl.pallas_call(
        functools.partial(absorb_kernel, plan),
        grid_spec=pltpu.PrefetchScalarGridSpec(
            num_scalar_prefetch=1,
            grid=(steps,),
            in_specs=in_specs,
            out_specs=out_specs,
            scratch_shapes=scratch,
        ),
        out_shape=out_shape,
        compiler_params=pltpu.CompilerParams(vmem_limit_bytes=VMEM),
        cost_estimate=pl.CostEstimate(
            flops=10**6, bytes_accessed=1 << 16, transcendentals=0
        ),
        name=name,
    )(scal, *args)
    if final is not None:
        return outs
    n = len(users)
    new = {}
    for i, user in enumerate(users):
        if first is not None:
            new[user] = (outs[1 + n + i], outs[1 + 2 * n + i], outs[1 + i])
        else:
            new[user] = (state[user][0], state[user][1], outs[1 + i])
    return outs[0], new


def user_perm(dx, dy, dcore):
    pairs = []
    for u in range(4 * NX):
        x, y, core = u >> 2, (u >> 1) & 1, u & 1
        pairs.append((u, (((x + dx) % NX) * 2 + (y ^ dy)) * 2 + (core ^ dcore)))
    return pairs


def cand_perm(dz, dy):
    return [(c, (((c >> 1) + dz) % NZ) * 2 + ((c & 1) ^ dy)) for c in range(2 * NZ)]


def to_user(array, dx, dy, dcore):
    return lax.ppermute(array, "user", user_perm(dx, dy, dcore))


def to_cand(array, dz, dy):
    return lax.ppermute(array, "cand", cand_perm(dz, dy))


def after(value, *others):
    return lax.optimization_barrier((value, others))[0]


def local(pooled, cand_feats, hist_len, cand_user, w_in, w_out):
    user = lax.axis_index("user")
    cand = lax.axis_index("cand")
    x, y, core = user >> 2, (user >> 1) & 1, user & 1
    z, y_hi = cand >> 1, cand & 1
    owner = cand_user - 2 * user
    n_first = ROWS - jnp.sum(owner)
    offsets = [SLOTS * (((z + dz + NZ) % NZ) * 2 + (y_hi ^ e)) for dz in SHIFTS for e in range(2)]
    scal = jnp.stack(
        [
            jnp.stack([hist_len[0], 0 * user, n_first, cand * SLOTS] + offsets),
            jnp.stack([hist_len[1], n_first, 0 * user + ROWS, cand * SLOTS] + offsets),
        ]
    ).astype(jnp.int32)

    tables = pooled.reshape(NX, 2, 2, 2, SLOTS, D)

    def block(j, core_at, x_at=None, y_at=None):
        at = (0 if x_at is None else x_at, 0 if y_at is None else y_at, core_at, j, 0, 0)
        size = (NX if x_at is None else 1, 2 if y_at is None else 1, 1, 1, SLOTS, D)
        return lax.dynamic_slice(tables, at, size).reshape(size[0], size[1], SLOTS, D)

    def share(got, x_at=None, y_at=None):
        at = (0 if x_at is None else x_at, 0 if y_at is None else y_at, 0, 0)
        size = (NX if x_at is None else 1, 2 if y_at is None else 1, SLOTS, D)
        return lax.dynamic_slice(got, at, size)

    hop = [lax.rem(x + d, NX) for d in range(NX)]
    with jax.named_scope("sum_core"):
        got0 = to_user(block(0, 1 - core), 0, 0, 1)
        got1 = to_user(block(1, 1 - core), 0, 0, 1)
    with jax.named_scope("sum_x_first"):
        away = [
            (block(0, core, x_at=hop[d]).astype(F32) + share(got0, x_at=hop[d]).astype(F32)).astype(BF16)[0]
            for d in range(NX)
        ]
        x0 = [to_user(away[d], d, 0, 0) for d in (1, 3, 2)]
    with jax.named_scope("sum_y_second"):
        got1 = after(got1, away)
        over = (block(1, core, y_at=1 - y).astype(F32) + share(got1, y_at=1 - y).astype(F32)).astype(BF16)
        y1 = to_user(over, 0, 1, 0)
    owner_row = after(owner.reshape(1, ROWS), over)
    xs, u_cand, q_cand, a_cand = cand_project(owner_row, cand_feats, w_in)
    with jax.named_scope("sum_x_first"):
        x0 = after(x0, xs)
        total0 = away[0].astype(F32)
        for got in x0:
            total0 = total0 + got.astype(F32)
        y0 = to_user(lax.dynamic_index_in_dim(total0, 1 - y, 0, False).astype(BF16), 0, 1, 0)
        mine0 = lax.dynamic_index_in_dim(total0, y, 0, False)
    with jax.named_scope("sum_y_second"):
        y1 = after(y1, mine0)
        away1 = []
        for d in range(NX):
            part = (
                block(1, core, x_at=hop[d], y_at=y).astype(F32)
                + share(got1, x_at=hop[d], y_at=y).astype(F32)
            )[0, 0]
            part = part + share(y1, x_at=hop[d], y_at=0).astype(F32)[0, 0]
            away1.append(part if d == 0 else part.astype(BF16))
        x1 = [to_user(away1[d], d, 0, 0) for d in (1, 3, 2)]
    with jax.named_scope("gather"):
        y0 = after(y0, away1)
        own0 = layer_norm(mine0 + y0.astype(F32)).astype(BF16)
        pair0 = jnp.stack([own0, to_cand(own0, 0, 1)])
        z0 = {-1: to_cand(pair0, 1, 0), 1: to_cand(pair0, -1, 0)}
        x1 = after(x1, pair0)
        total1 = away1[0]
        for got in x1:
            total1 = total1 + got.astype(F32)
        own1 = layer_norm(total1).astype(BF16)
        near1 = to_cand(own1, 0, 1)
    both = (0, 1)
    put = functools.partial(absorb, scal=scal, w_in=w_in, q_cand=q_cand)
    a_cand, state0 = put(
        "own_first", items=[(0, 0, both, after(pair0, own1))], a_cand=a_cand, first={0: own0}
    )
    with jax.named_scope("gather"):
        pair1 = jnp.stack([own1, after(near1, a_cand)])
        z1 = {-1: to_cand(pair1, 1, 0), 1: to_cand(pair1, -1, 0)}
    a_cand, state1 = put("own_second", items=[(1, 0, both, pair1)], a_cand=a_cand, first={1: own1})
    with jax.named_scope("gather"):
        z0 = after(z0, a_cand)
        far0 = [to_cand(z0[-1][:1], 1, 0), to_cand(z0[1][1:], -1, 0)]
    a_cand, state0 = put(
        "side_first",
        items=[(0, -1, both, z0[-1]), (0, 1, both, z0[1])],
        a_cand=a_cand,
        state=state0,
    )
    with jax.named_scope("gather"):
        z1 = after(z1, a_cand)
        far1 = [to_cand(z1[-1][:1], 1, 0), to_cand(z1[1][1:], -1, 0)]
    a_cand, state1 = put(
        "side_second",
        items=[(1, -1, both, z1[-1]), (1, 1, both, z1[1])],
        a_cand=a_cand,
        state=state1,
    )
    return put(
        "far_finish",
        items=[(0, 2, (0,), far0[0]), (0, 2, (1,), far0[1]), (1, 2, (0,), far1[0]), (1, 2, (1,), far1[1])],
        a_cand=a_cand,
        state={**state0, **state1},
        final=dict(
            own={0: own0, 1: own1}, u=u_cand, xs=xs, owner=owner.reshape(ROWS, 1), w_out=w_out
        ),
    )


def solution(mesh):
    placed = (
        P("user", None, "cand", None),
        P(("user", "cand"), None),
        P("user"),
        P(("user", "cand")),
        P(),
        P(),
    )
    return jax.shard_map(
        local,
        mesh=mesh,
        in_specs=placed,
        out_specs=(P("user", "cand", None), P(("user", "cand"), None)),
        check_vma=False,
    )
```

```python
import functools

import jax
import jax.numpy as jnp
from jax import lax
from jax.experimental import pallas as pl
from jax.experimental.pallas import tpu as pltpu
from jax.sharding import PartitionSpec as P

F32 = jnp.float32
BF16 = jnp.bfloat16
HEADS = 8
HD = 128
D = 1024
SLOTS = 128
ROWS = 512
NX, NZ = 4, 4
WINDOW = 320
HALF_SCALE = 0.5 / (HD**0.5)
VMEM = 20 * 1024 * 1024
GROUP = 512
SHIFTS = (0, -1, 1, 2)


def silu(v):
    half = v * 0.5
    return half + half * jnp.tanh(half)


def layer_norm(rows):
    mean = jnp.mean(rows, axis=-1, keepdims=True)
    centered = rows - mean
    var = jnp.mean(centered * centered, axis=-1, keepdims=True)
    return centered * lax.rsqrt(var + 1e-05)


def mm(a, b):
    return jnp.dot(a, b, preferred_element_type=F32)


def weights_of(queries, keys):
    s = lax.dot_general(queries, keys, (((1,), (1,)), ((), ())), preferred_element_type=F32)
    half = s * HALF_SCALE
    return half + half * jnp.tanh(half)


def in_vmem(array):
    return pltpu.with_memory_space_constraint(array, pltpu.VMEM)


def kernel_call(body, name, arrays, out_shape, scratch, scalars=None, aliases=None):
    vmem = pl.BlockSpec(memory_space=pltpu.VMEM)
    in_specs, args = [vmem] * len(arrays), [in_vmem(array) for array in arrays]
    if scalars is not None:
        in_specs = [pl.BlockSpec(memory_space=pltpu.SMEM)] + in_specs
        args = [scalars] + args
    return pl.pallas_call(
        body,
        in_specs=in_specs,
        out_specs=[vmem] * len(out_shape),
        out_shape=out_shape,
        scratch_shapes=scratch,
        input_output_aliases=aliases or {},
        compiler_params=pltpu.CompilerParams(vmem_limit_bytes=VMEM),
        cost_estimate=pl.CostEstimate(flops=10**6, bytes_accessed=1 << 16, transcendentals=0),
        name=name,
    )(*args)


def cand_kernel(owner_ref, feats_ref, w_ref, xs_ref, u_ref, q_ref, a_ref):
    second = owner_ref[...].astype(F32)
    r_from = lax.broadcasted_iota(jnp.int32, (ROWS, ROWS), 0)
    r_to = lax.broadcasted_iota(jnp.int32, (ROWS, ROWS), 1)
    upper = jnp.where(r_from <= r_to, 1.0, 0.0).astype(BF16)
    ones_before = mm(jnp.broadcast_to(second, (8, ROWS)).astype(BF16), upper)[:1]
    index = lax.broadcasted_iota(jnp.int32, (1, ROWS), 1).astype(F32)
    n_first = ROWS - jnp.sum(second, axis=1, keepdims=True)
    place = jnp.where(second > 0.5, n_first + ones_before - 1.0, index - ones_before)
    onehot = jnp.where(r_from == place.astype(jnp.int32), 1.0, 0.0).astype(BF16)
    x = layer_norm(feats_ref[...].astype(F32)).astype(BF16)
    xs_ref[...] = mm(onehot, x).astype(BF16)

    @pl.loop(0, D // GROUP)
    def _(g):
        cols = lambda n: pl.ds(pl.multiple_of(n * D + g * GROUP, GROUP), GROUP)
        u, v, q, k = (silu(mm(xs_ref[...], w_ref[:, cols(n)])).astype(BF16) for n in range(4))
        u_ref[:, cols(0)] = u
        q_ref[:, cols(0)] = q
        prod = q.astype(F32) * k.astype(F32)
        for h in range(GROUP // HD):
            hc = slice(h * HD, (h + 1) * HD)
            half = jnp.sum(prod[:, hc], axis=-1, keepdims=True) * HALF_SCALE
            own = (half + half * jnp.tanh(half)).astype(BF16).astype(F32)
            out_cols = pl.ds(pl.multiple_of(g * GROUP + h * HD, HD), HD)
            a_ref[:, out_cols] = own * v[:, hc].astype(F32)


def cand_project(owner_row, feats, w_in):
    rows = jax.ShapeDtypeStruct((ROWS, D), BF16)
    out_shape = [rows, rows, rows, jax.ShapeDtypeStruct((ROWS, D), F32)]
    return kernel_call(cand_kernel, "cand_project", [owner_row, feats, w_in], out_shape, [])


def absorb_kernel(plan, scal_ref, *refs):
    users, first, final = plan["users"], plan["first"], plan["final"]
    refs = list(refs)
    take = lambda n: [refs.pop(0) for _ in range(n)]
    keys = [(user, shift, e, ref) for (user, shift, es), ref in zip(plan["items"], take(len(plan["items"]))) for e in es]
    w_ref, q_ref, a_ref = take(3)
    if first:
        own_ref = dict(zip(users, take(len(users))))
    else:
        qh_ref = dict(zip(users, take(len(users))))
        ah_ref = dict(zip(users, take(len(users))))
    if final:
        uh_ref = dict(zip(users, take(len(users))))
        xh_ref = dict(zip(users, take(len(users))))
        u_ref, xs_ref, owner_ref, wo_ref = take(4)
        hist_ref, cand_ref = take(2)
    else:
        take(1)
        if first:
            ah_ref = dict(zip(users, take(len(users))))
            qh_ref = dict(zip(users, take(len(users))))
            uh_ref = dict(zip(users, take(len(users))))
        else:
            take(len(users))
    k_scr, v_scr = take(2)
    if final:
        (y_scr,) = take(1)
    row_iota = lax.broadcasted_iota(jnp.int32, (SLOTS, 1), 0)
    ahead = lax.broadcasted_iota(jnp.int32, (SLOTS, SLOTS), 0) - lax.broadcasted_iota(
        jnp.int32, (SLOTS, SLOTS), 1
    )
    for user in users:
        length = scal_ref[user, 0]
        row_lo = scal_ref[user, 1]
        row_hi = scal_ref[user, 2]
        my_off = scal_ref[user, 3]
        mine_keys = [(shift, e, ref) for (u, shift, e, ref) in keys if u == user]
        offs = [scal_ref[user, 4 + 2 * SHIFTS.index(shift) + e] for shift, e, _ in mine_keys]
        n_keys = SLOTS * len(offs)

        @pl.loop(0, D // GROUP)
        def _(g):
            cols = lambda n: pl.ds(pl.multiple_of(n * D + g * GROUP, GROUP), GROUP)
            if first:
                x_own = own_ref[user][...]
                qh_ref[user][:, cols(0)] = silu(mm(x_own, w_ref[:, cols(2)])).astype(BF16)
                uh_ref[user][:, cols(0)] = silu(mm(x_own, w_ref[:, cols(0)])).astype(BF16)
                ah_ref[user][:, cols(0)] = jnp.zeros((SLOTS, GROUP), F32)
            x = jnp.concatenate([ref[min(e, ref.shape[0] - 1)] for _, e, ref in mine_keys], axis=0)
            k_scr[:n_keys, :] = silu(mm(x, w_ref[:, cols(3)])).astype(BF16)
            v = silu(mm(x, w_ref[:, cols(1)])).astype(BF16)
            for i, off in enumerate(offs):
                piece = v[i * SLOTS : (i + 1) * SLOTS]
                piece = jnp.where(row_iota < length - off, piece, jnp.zeros_like(piece))
                v_scr[i * SLOTS : (i + 1) * SLOTS, :] = piece

            def attend(start, count):
                rows = pl.ds(start, count)
                index = start + lax.broadcasted_iota(jnp.int32, (count, 1), 0)
                mine = (index >= row_lo) & (index < row_hi)
                for h in range(GROUP // HD):
                    hc = slice(h * HD, (h + 1) * HD)
                    oc = pl.ds(pl.multiple_of(g * GROUP + h * HD, HD), HD)
                    q = jnp.concatenate([q_ref[rows, oc], qh_ref[user][:, oc]], axis=0)
                    total = None
                    for n in range(0, n_keys, 2 * SLOTS):
                        w = weights_of(q, k_scr[n : n + 2 * SLOTS, hc])
                        parts = []
                        for i in range(2):
                            part = w[count:, i * SLOTS : (i + 1) * SLOTS]
                            seen = ahead >= offs[n // SLOTS + i] - my_off
                            parts.append(jnp.where(seen, part, 0.0).astype(BF16))
                        w = jnp.concatenate([w[:count].astype(BF16), jnp.concatenate(parts, axis=1)], axis=0)
                        pv = mm(w, v_scr[n : n + 2 * SLOTS, hc])
                        total = pv if total is None else total + pv
                    a_ref[rows, oc] += jnp.where(mine, total[:count], 0.0)
                    ah_ref[user][:, oc] += total[count:]

            start = jnp.minimum((row_lo // 16) * 16, ROWS - WINDOW)
            narrow = row_hi <= start + WINDOW

            @pl.when(narrow)
            def _():
                attend(pl.multiple_of(start, 16), WINDOW)

            @pl.when(jnp.logical_not(narrow))
            def _():
                attend(0, ROWS)

    if final:
        n_hist = SLOTS * len(users)
        for i, user in enumerate(users):
            y = layer_norm(ah_ref[user][...]) * uh_ref[user][...].astype(F32)
            y_scr[i * SLOTS : (i + 1) * SLOTS, :] = y.astype(BF16)

        @pl.loop(0, ROWS // SLOTS)
        def _(n):
            rows = pl.ds(pl.multiple_of(n * SLOTS, SLOTS), SLOTS)
            y = layer_norm(a_ref[rows, :]) * u_ref[rows, :].astype(F32)
            y_scr[pl.ds(pl.multiple_of(n_hist + n * SLOTS, SLOTS), SLOTS), :] = y.astype(BF16)

        r_row = lax.broadcasted_iota(jnp.int32, (ROWS, ROWS), 0)
        r_col = lax.broadcasted_iota(jnp.int32, (ROWS, ROWS), 1)
        second = owner_ref[...].astype(F32)
        lower = jnp.where(r_col <= r_row, 1.0, 0.0).astype(BF16)
        ones_before = mm(lower, jnp.broadcast_to(second, (ROWS, HD)).astype(BF16))[:, :1]
        index = lax.broadcasted_iota(jnp.int32, (ROWS, 1), 0).astype(F32)
        n_first = ROWS - jnp.sum(second, axis=0, keepdims=True)
        place = jnp.where(second > 0.5, n_first + ones_before - 1.0, index - ones_before)
        back = jnp.where(r_col == place.astype(jnp.int32), 1.0, 0.0).astype(BF16)

        @pl.loop(0, D // GROUP)
        def _(g):
            cols = pl.ds(pl.multiple_of(g * GROUP, GROUP), GROUP)
            res = mm(y_scr[...], wo_ref[:, cols])
            for i, user in enumerate(users):
                out = res[i * SLOTS : (i + 1) * SLOTS] + xh_ref[user][:, cols].astype(F32)
                keep = scal_ref[user, 3] + row_iota < scal_ref[user, 0]
                hist_ref[user, :, cols] = jnp.where(keep, out, 0.0).astype(BF16)
            done = (res[n_hist:] + xs_ref[:, cols].astype(F32)).astype(BF16)
            cand_ref[:, cols] = mm(back, done).astype(BF16)


def absorb(name, scal, items, w_in, q_cand, a_cand, first=None, state=None, final=None):
    users = tuple(sorted({item[0] for item in items}))
    plan = dict(items=tuple(item[:3] for item in items), users=users, first=first is not None, final=final is not None)
    arrays = [item[3] for item in items] + [w_in, q_cand, a_cand]
    n = len(users)
    a_at = len(arrays)
    sums = jax.ShapeDtypeStruct((SLOTS, D), F32)
    rows = jax.ShapeDtypeStruct((SLOTS, D), BF16)
    most = max(sum(len(item[2]) for item in items if item[0] == user) for user in users)
    scratch = [pltpu.VMEM((most * SLOTS, GROUP), BF16)] * 2
    out_shape = [jax.ShapeDtypeStruct((ROWS, D), F32)]
    aliases = {a_at: 0}
    if first is not None:
        arrays += [first[user] for user in users]
        out_shape += [sums] * n + [rows] * (2 * n)
    else:
        arrays += [state[user][0] for user in users]
        aliases.update({len(arrays) + 1 + i: 1 + i for i in range(n)})
        arrays += [state[user][2] for user in users]
        out_shape += [sums] * n
    if final is not None:
        arrays += [state[user][1] for user in users]
        arrays += [final["own"][user] for user in users]
        arrays += [final["u"], final["xs"], final["owner"], final["w_out"]]
        out_shape = [jax.ShapeDtypeStruct((n, SLOTS, D), BF16), jax.ShapeDtypeStruct((ROWS, D), BF16)]
        aliases = {}
        scratch.append(pltpu.VMEM((n * SLOTS + ROWS, D), BF16))
    outs = kernel_call(
        functools.partial(absorb_kernel, plan), name, arrays, out_shape, scratch, scal, aliases
    )
    if final is not None:
        return outs
    new = {}
    for i, user in enumerate(users):
        if first is not None:
            new[user] = (outs[1 + n + i], outs[1 + 2 * n + i], outs[1 + i])
        else:
            new[user] = (state[user][0], state[user][1], outs[1 + i])
    return outs[0], new


def user_perm(dx, dy, dcore):
    pairs = []
    for u in range(4 * NX):
        x, y, core = u >> 2, (u >> 1) & 1, u & 1
        pairs.append((u, (((x + dx) % NX) * 2 + (y ^ dy)) * 2 + (core ^ dcore)))
    return pairs


def cand_perm(dz, dy):
    return [(c, (((c >> 1) + dz) % NZ) * 2 + ((c & 1) ^ dy)) for c in range(2 * NZ)]


def to_user(array, dx, dy, dcore):
    return lax.ppermute(array, "user", user_perm(dx, dy, dcore))


def to_cand(array, dz, dy):
    return lax.ppermute(array, "cand", cand_perm(dz, dy))


def after(value, *others):
    return lax.optimization_barrier((value, others))[0]


def local(pooled, cand_feats, hist_len, cand_user, w_in, w_out):
    user = lax.axis_index("user")
    cand = lax.axis_index("cand")
    x, y, core = user >> 2, (user >> 1) & 1, user & 1
    z, y_hi = cand >> 1, cand & 1
    owner = cand_user - 2 * user
    n_first = ROWS - jnp.sum(owner)
    offsets = [SLOTS * (((z + dz + NZ) % NZ) * 2 + (y_hi ^ e)) for dz in SHIFTS for e in range(2)]
    scal = jnp.stack(
        [
            jnp.stack([hist_len[0], 0 * user, n_first, cand * SLOTS] + offsets),
            jnp.stack([hist_len[1], n_first, 0 * user + ROWS, cand * SLOTS] + offsets),
        ]
    ).astype(jnp.int32)

    tables = pooled.reshape(NX, 2, 2, 2, SLOTS, D)

    def block(j, core_at, x_at=None, y_at=None):
        at = (0 if x_at is None else x_at, 0 if y_at is None else y_at, core_at, j, 0, 0)
        size = (NX if x_at is None else 1, 2 if y_at is None else 1, 1, 1, SLOTS, D)
        return lax.dynamic_slice(tables, at, size).reshape(size[0], size[1], SLOTS, D)

    def share(got, x_at=None, y_at=None):
        at = (0 if x_at is None else x_at, 0 if y_at is None else y_at, 0, 0)
        size = (NX if x_at is None else 1, 2 if y_at is None else 1, SLOTS, D)
        return lax.dynamic_slice(got, at, size)

    hop = [lax.rem(x + d, NX) for d in range(NX)]
    with jax.named_scope("sum_core"):
        pack0 = block(0, 1 - core)
        got0 = to_user(pack0, 0, 0, 1)
        tables = after(tables, pack0)
        got1 = to_user(block(1, 1 - core), 0, 0, 1)
    with jax.named_scope("sum_x_first"):
        away = [
            (block(0, core, x_at=hop[d]).astype(F32) + share(got0, x_at=hop[d]).astype(F32)).astype(BF16)[0]
            for d in range(NX)
        ]
        x0 = [to_user(away[d], d, 0, 0) for d in (1, 3, 2)]
    with jax.named_scope("sum_y_second"):
        got1 = after(got1, away)
        over = (block(1, core, y_at=1 - y).astype(F32) + share(got1, y_at=1 - y).astype(F32)).astype(BF16)
        y1 = to_user(over, 0, 1, 0)
    owner_row = after(owner.reshape(1, ROWS), over)
    xs, u_cand, q_cand, a_cand = cand_project(owner_row, cand_feats, w_in)
    with jax.named_scope("sum_x_first"):
        x0 = after(x0, xs)
        total0 = away[0].astype(F32)
        for got in x0:
            total0 = total0 + got.astype(F32)
        y0 = to_user(lax.dynamic_index_in_dim(total0, 1 - y, 0, False).astype(BF16), 0, 1, 0)
        mine0 = lax.dynamic_index_in_dim(total0, y, 0, False)
    with jax.named_scope("sum_y_second"):
        y1 = after(y1, mine0)
        away1 = []
        for d in range(NX):
            part = (
                block(1, core, x_at=hop[d], y_at=y).astype(F32)
                + share(got1, x_at=hop[d], y_at=y).astype(F32)
            )[0, 0]
            part = part + share(y1, x_at=hop[d], y_at=0).astype(F32)[0, 0]
            away1.append(part if d == 0 else part.astype(BF16))
        x1 = [to_user(away1[d], d, 0, 0) for d in (1, 3, 2)]
    with jax.named_scope("gather"):
        y0 = after(y0, away1)
        own0 = layer_norm(mine0 + y0.astype(F32)).astype(BF16)
        pair0 = jnp.stack([own0, to_cand(own0, 0, 1)])
        z0 = {-1: to_cand(pair0, 1, 0), 1: to_cand(pair0, -1, 0)}
    both = (0, 1)
    put = functools.partial(absorb, scal=scal, w_in=w_in, q_cand=q_cand)
    a_cand, state0 = put("own_first", items=[(0, 0, both, pair0)], a_cand=a_cand, first={0: own0})
    with jax.named_scope("gather"):
        x1 = after(x1, a_cand)
        total1 = away1[0]
        for got in x1:
            total1 = total1 + got.astype(F32)
        own1 = layer_norm(total1).astype(BF16)
        near1 = to_cand(own1, 0, 1)
        z0 = after(z0, own1)
        ends0 = [z0[-1][:1], z0[1][1:]]
        far0 = [to_cand(ends0[0], 1, 0), to_cand(ends0[1], -1, 0)]
        pair1 = jnp.stack([own1, after(near1, ends0)])
        z1 = {-1: to_cand(pair1, 1, 0), 1: to_cand(pair1, -1, 0)}
    a_cand, state0 = put(
        "side_first",
        items=[(0, -1, both, z0[-1]), (0, 1, both, z0[1])],
        a_cand=after(a_cand, pair1),
        state=state0,
    )
    a_cand, state1 = put("own_second", items=[(1, 0, both, pair1)], a_cand=a_cand, first={1: own1})
    with jax.named_scope("gather"):
        z1 = after(z1, a_cand)
        ends1 = [z1[-1][:1], z1[1][1:]]
        far1 = [to_cand(ends1[0], 1, 0), to_cand(ends1[1], -1, 0)]
    a_cand, state1 = put(
        "side_second",
        items=[(1, -1, both, z1[-1]), (1, 1, both, z1[1])],
        a_cand=after(a_cand, ends1),
        state=state1,
    )
    return put(
        "far_finish",
        items=[(0, 2, (0,), far0[0]), (0, 2, (1,), far0[1]), (1, 2, (0,), far1[0]), (1, 2, (1,), far1[1])],
        a_cand=a_cand,
        state={**state0, **state1},
        final=dict(
            own={0: own0, 1: own1}, u=u_cand, xs=xs, owner=owner.reshape(ROWS, 1), w_out=w_out
        ),
    )


def solution(mesh):
    placed = (
        P("user", None, "cand", None),
        P(("user", "cand"), None),
        P("user"),
        P(("user", "cand")),
        P(),
        P(),
    )
    return jax.shard_map(
        local,
        mesh=mesh,
        in_specs=placed,
        out_specs=(P("user", "cand", None), P(("user", "cand"), None)),
        check_vma=False,
    )
```

```python
import functools

import jax
import jax.numpy as jnp
from jax import lax
from jax.experimental import pallas as pl
from jax.experimental.pallas import tpu as pltpu
from jax.sharding import PartitionSpec as P

F32 = jnp.float32
BF16 = jnp.bfloat16
HEADS = 8
HD = 128
D = 1024
SLOTS = 128
ROWS = 512
NX, NZ = 4, 4
WINDOW = 320
HALF_SCALE = 0.5 / (HD**0.5)
VMEM = 40 * 1024 * 1024
GROUP = 512
STEPS = D // GROUP
SHIFTS = (0, -1, 1, 2)


def silu(v):
    half = v * 0.5
    return half + half * jnp.tanh(half)


def layer_norm(rows):
    mean = jnp.mean(rows, axis=-1, keepdims=True)
    centered = rows - mean
    var = jnp.mean(centered * centered, axis=-1, keepdims=True)
    return centered * lax.rsqrt(var + 1e-05)


def mm(a, b):
    return jnp.dot(a, b, preferred_element_type=F32)


def weights_of(queries, keys):
    s = lax.dot_general(queries, keys, (((1,), (1,)), ((), ())), preferred_element_type=F32)
    half = s * HALF_SCALE
    return half + half * jnp.tanh(half)


def after(value, *others):
    return lax.optimization_barrier((value, others))[0]


def in_hbm(array):
    return pltpu.with_memory_space_constraint(array, pltpu.HBM)


def cost():
    return pl.CostEstimate(flops=10**6, bytes_accessed=1 << 16, transcendentals=0)


def pack_kernel(scal_ref, tables_ref, out_ref, sems):
    copies = []
    for x in range(NX):
        for y in range(2):
            n = 2 * x + y
            copies.append(
                pltpu.make_async_copy(
                    tables_ref.at[x, y, scal_ref[0], scal_ref[1]], out_ref.at[x, y], sems.at[n]
                )
            )
    for copy in copies:
        copy.start()
    for copy in copies:
        copy.wait()


def pack(tables, core_at, j):
    return pl.pallas_call(
        pack_kernel,
        in_specs=[pl.BlockSpec(memory_space=pltpu.SMEM), pl.BlockSpec(memory_space=pltpu.HBM)],
        out_specs=pl.BlockSpec(memory_space=pltpu.HBM),
        out_shape=jax.ShapeDtypeStruct((NX, 2, SLOTS, D), BF16),
        scratch_shapes=[pltpu.SemaphoreType.DMA((2 * NX,))],
        compiler_params=pltpu.CompilerParams(vmem_limit_bytes=VMEM),
        cost_estimate=cost(),
        name="pack",
    )(jnp.stack([core_at, jnp.int32(j)]).astype(jnp.int32), in_hbm(tables))


def add_up(name, scal, grid, parts, outs):
    def body(scal_ref, *refs):
        ins, out_refs = refs[: len(parts)], refs[len(parts) :]
        for (_, dtype, _, _, members), out_ref in zip(outs, out_refs):
            total = None
            for n in members:
                value = ins[n][...].astype(F32)
                value = value.reshape(value.shape[-2:])
                total = value if total is None else total + value
            if dtype == "norm":
                total, dtype = layer_norm(total), BF16
            out_ref[...] = total.astype(dtype).reshape(out_ref.shape)

    return pl.pallas_call(
        body,
        grid_spec=pltpu.PrefetchScalarGridSpec(
            num_scalar_prefetch=1,
            grid=grid,
            in_specs=[pl.BlockSpec(block, index) for _, block, index in parts],
            out_specs=[pl.BlockSpec(block, index) for _, _, block, index, _ in outs],
        ),
        out_shape=[
            jax.ShapeDtypeStruct(shape, BF16 if dtype == "norm" else dtype)
            for shape, dtype, _, _, _ in outs
        ],
        compiler_params=pltpu.CompilerParams(vmem_limit_bytes=VMEM),
        cost_estimate=cost(),
        name=name,
    )(scal, *(in_hbm(array) if array.ndim == 6 else array for array, _, _ in parts))


def over_y(scal, tables, got):
    block = (1, 1, 1, 1, SLOTS, D)
    return add_up(
        "over_y",
        scal,
        (NX,),
        [
            (tables, block, lambda i, s: (i, 1 - s[1], s[2], 1, 0, 0)),
            (got, (1, 1, SLOTS, D), lambda i, s: (i, 1 - s[1], 0, 0)),
        ],
        [((NX, SLOTS, D), BF16, (1, SLOTS, D), lambda i, s: (i, 0, 0), (0, 1))],
    )[0]


def away_x(scal, tables, got):
    half = SLOTS // 2
    parts, outs = [], []
    for d in range(NX):
        parts.append(
            (
                tables,
                (1, 1, 1, 1, half, D),
                lambda i, s, d=d: ((s[0] + d) % NX, i // 2, s[2], 0, i % 2, 0),
            )
        )
        parts.append((got, (1, 1, half, D), lambda i, s, d=d: ((s[0] + d) % NX, i // 2, i % 2, 0)))
        outs.append(
            ((2, SLOTS, D), BF16, (1, half, D), lambda i, s: (i // 2, i % 2, 0), (2 * d, 2 * d + 1))
        )
    return add_up("away_x", scal, (4,), parts, outs)


def join_x(scal, away, arrived):
    half = SLOTS // 2
    arrays = [away] + list(arrived)
    parts = [(a, (1, half, D), lambda i, s: (s[1], i, 0)) for a in arrays]
    parts += [(a, (1, half, D), lambda i, s: (1 - s[1], i, 0)) for a in arrays]
    out = lambda dtype, members: ((SLOTS, D), dtype, (half, D), lambda i, s: (i, 0), members)
    return add_up("join_x", scal, (2,), parts, [out(F32, (0, 1, 2, 3)), out(BF16, (4, 5, 6, 7))])


def join_y(scal, tables, got, arrived):
    half = SLOTS // 2
    parts, outs = [], []
    for d in range(NX):
        at = lambda s, d=d: (s[0] + d) % NX
        parts.append(
            (tables, (1, 1, 1, 1, half, D), lambda i, s, at=at: (at(s), s[1], s[2], 1, i, 0))
        )
        parts.append((got, (1, 1, half, D), lambda i, s, at=at: (at(s), s[1], i, 0)))
        parts.append((arrived, (1, half, D), lambda i, s, at=at: (at(s), i, 0)))
        outs.append(
            (
                (SLOTS, D),
                F32 if d == 0 else BF16,
                (half, D),
                lambda i, s: (i, 0),
                (3 * d, 3 * d + 1, 3 * d + 2),
            )
        )
    return add_up("join_y", scal, (2,), parts, outs)


def norm_sum(scal, arrays):
    half = SLOTS // 2
    parts = [(a, (half, D), lambda i, s: (i, 0)) for a in arrays]
    return add_up(
        "norm_sum",
        scal,
        (2,),
        parts,
        [((SLOTS, D), "norm", (half, D), lambda i, s: (i, 0), tuple(range(len(arrays))))],
    )[0]


class Fetch:
    def __init__(self, sems):
        self.sems, self.count, self.pending = sems, 0, {}

    def start(self, key, src, dst):
        copy = pltpu.make_async_copy(src, dst, self.sems.at[self.count])
        copy.start()
        self.count += 1
        self.pending.setdefault(key, []).append(copy)

    def wait(self, *keys):
        for key in keys:
            for copy in self.pending.pop(key, ()):
                copy.wait()


def cand_kernel(owner_ref, feats_hbm, w_hbm, *refs):
    outs, (xs_ref, u_ref, q_ref, a_ref), (feats_ref, w_ref, sems, out_sems) = refs[:4], refs[4:8], refs[8:]
    stores = []
    for g in range(STEPS):
        cols = slice(g * GROUP, (g + 1) * GROUP)
        for n, ref in enumerate((u_ref, q_ref, a_ref)):
            stores.append(
                pltpu.make_async_copy(
                    ref.at[:, cols], outs[1 + n].at[:, cols], out_sems.at[3 * g + n]
                )
            )
    stores.append(pltpu.make_async_copy(xs_ref, outs[0], out_sems.at[3 * STEPS]))
    fetch = Fetch(sems)
    fetch.start("feats", feats_hbm, feats_ref)
    for g in range(STEPS):
        for n in range(4):
            at = n * D + g * GROUP
            fetch.start(g, w_hbm.at[:, at : at + GROUP], w_ref.at[4 * g + n])
    second = owner_ref[...].astype(F32)
    r_from = lax.broadcasted_iota(jnp.int32, (ROWS, ROWS), 0)
    r_to = lax.broadcasted_iota(jnp.int32, (ROWS, ROWS), 1)
    upper = jnp.where(r_from <= r_to, 1.0, 0.0).astype(BF16)
    ones_before = mm(jnp.broadcast_to(second, (8, ROWS)).astype(BF16), upper)[:1]
    index = lax.broadcasted_iota(jnp.int32, (1, ROWS), 1).astype(F32)
    n_first = ROWS - jnp.sum(second, axis=1, keepdims=True)
    place = jnp.where(second > 0.5, n_first + ones_before - 1.0, index - ones_before)
    onehot = jnp.where(r_from == place.astype(jnp.int32), 1.0, 0.0).astype(BF16)
    fetch.wait("feats")
    x = layer_norm(feats_ref[...].astype(F32)).astype(BF16)
    xs_ref[...] = mm(onehot, x).astype(BF16)
    stores[-1].start()
    fetch.wait(0)

    @pl.loop(0, STEPS)
    def _(g):
        @pl.when(g == STEPS - 1)
        def _():
            fetch.wait(*range(1, STEPS))
            for copy in stores[: 3 * (STEPS - 1)]:
                copy.start()

        cols = pl.ds(pl.multiple_of(g * GROUP, GROUP), GROUP)
        u, v, q, k = (silu(mm(xs_ref[...], w_ref[4 * g + n])).astype(BF16) for n in range(4))
        u_ref[:, cols] = u
        q_ref[:, cols] = q
        prod = q.astype(F32) * k.astype(F32)
        for h in range(GROUP // HD):
            hc = slice(h * HD, (h + 1) * HD)
            half = jnp.sum(prod[:, hc], axis=-1, keepdims=True) * HALF_SCALE
            own = (half + half * jnp.tanh(half)).astype(BF16).astype(F32)
            out_cols = pl.ds(pl.multiple_of(g * GROUP + h * HD, HD), HD)
            a_ref[:, out_cols] = own * v[:, hc].astype(F32)

    for copy in stores[3 * (STEPS - 1) : -1]:
        copy.start()
    for copy in stores:
        copy.wait()


def cand_project(owner_row, feats, w_in):
    rows = pltpu.HBM((ROWS, D), BF16)
    vmem, hbm = pl.BlockSpec(memory_space=pltpu.VMEM), pl.BlockSpec(memory_space=pltpu.HBM)
    return pl.pallas_call(
        cand_kernel,
        in_specs=[vmem, hbm, hbm],
        out_specs=[hbm] * 4,
        out_shape=[rows, rows, rows, pltpu.HBM((ROWS, D), F32)],
        scratch_shapes=[pltpu.VMEM((ROWS, D), BF16)] * 3
        + [
            pltpu.VMEM((ROWS, D), F32),
            pltpu.VMEM((ROWS, D), BF16),
            pltpu.VMEM((4 * STEPS, D, GROUP), BF16),
            pltpu.SemaphoreType.DMA((1 + 4 * STEPS,)),
            pltpu.SemaphoreType.DMA((1 + 3 * STEPS,)),
        ],
        compiler_params=pltpu.CompilerParams(vmem_limit_bytes=VMEM),
        cost_estimate=cost(),
        name="cand_project",
    )(owner_row, in_hbm(feats), in_hbm(w_in))


def absorb_kernel(plan, scal_ref, *refs):
    items, first, final = plan["items"], plan["first"], plan["final"]
    users = sorted({user for user, _ in items})
    refs = list(refs)
    names = plan["names"]
    hbm = dict(zip(names, refs[: len(names)]))
    refs = refs[len(names) :]
    outs = dict(zip(plan["outs"], refs[: len(plan["outs"])]))
    refs = refs[len(plan["outs"]) :]
    vm = dict(zip(plan["held"], refs[: len(plan["held"])]))
    refs = refs[len(plan["held"]) :]
    made = dict(zip(plan["made"], refs[: len(plan["made"])]))
    refs = refs[len(plan["made"]) :]
    w_ref, k_scr, v_scr = refs[:3]
    sems, out_sems = refs[-2:]
    fetch = Fetch(sems)
    kinds = (3, 1, 2, 0) if first else (3, 1)
    fetch.start("x", hbm["x0"], vm["x0"])
    for g in range(STEPS):
        for n in kinds:
            at = n * D + g * GROUP
            fetch.start(("w", g), hbm["w_in"].at[:, at : at + GROUP], w_ref.at[4 * g + n])
        if g == 0:
            for name in names:
                if name not in ("x0", "w_in") and name in vm:
                    key = "late" if name in ("w_out", "u", "xs", "uh0", "uh1", "xh0", "xh1") else "x"
                    fetch.start(key, hbm[name], vm[name])
    if first:
        ah = {user: made["ah%d" % user] for user in users}
        qh = {user: made["qh%d" % user] for user in users}
        uh = {user: made["uh%d" % user] for user in users}
    else:
        ah = {user: vm["ah%d" % user] for user in (0, 1) if "ah%d" % user in vm}
        qh = {user: vm["qh%d" % user] for user in users}
    a_ref, q_ref = vm["a"], vm["q"]
    row_iota = lax.broadcasted_iota(jnp.int32, (SLOTS, 1), 0)
    ahead = lax.broadcasted_iota(jnp.int32, (SLOTS, SLOTS), 0) - lax.broadcasted_iota(
        jnp.int32, (SLOTS, SLOTS), 1
    )
    fetch.wait("x", ("w", 0))
    halves, wholes = [], []
    for name, out in outs.items():
        src = made[name] if name in made else vm[name]
        if name in ("a", "cand"):
            for g in range(STEPS):
                cols = slice(g * GROUP, (g + 1) * GROUP)
                halves.append(pltpu.make_async_copy(src.at[:, cols], out.at[:, cols], out_sems.at[g]))
        else:
            wholes.append(pltpu.make_async_copy(src, out, out_sems.at[STEPS + len(wholes)]))

    @pl.loop(0, STEPS)
    def _(g):
        @pl.when(g == STEPS - 1)
        def _():
            fetch.wait(*(("w", n) for n in range(1, STEPS)))
            if not final:
                for copy in halves[: STEPS - 1]:
                    copy.start()

        cols = pl.ds(pl.multiple_of(g * GROUP, GROUP), GROUP)
        wk, wv = w_ref[4 * g + 3], w_ref[4 * g + 1]
        for user in users:
            length = scal_ref[user, 0]
            row_lo = scal_ref[user, 1]
            row_hi = scal_ref[user, 2]
            my_off = scal_ref[user, 3]
            mine_items = [(n, shift) for n, (u, shift) in enumerate(items) if u == user]
            offs = [scal_ref[user, 4 + 2 * SHIFTS.index(shift) + e] for _, shift in mine_items for e in (0, 1)]
            n_keys = SLOTS * len(offs)
            if first:
                x_own = vm["x%d" % mine_items[0][0]][0]
                qh[user][:, cols] = silu(mm(x_own, w_ref[4 * g + 2])).astype(BF16)
                uh[user][:, cols] = silu(mm(x_own, w_ref[4 * g])).astype(BF16)
                ah[user][:, cols] = jnp.zeros((SLOTS, GROUP), F32)
            x = jnp.concatenate([vm["x%d" % n][...].reshape(2 * SLOTS, D) for n, _ in mine_items], axis=0)
            k_scr[:n_keys, :] = silu(mm(x, wk)).astype(BF16)
            v = silu(mm(x, wv)).astype(BF16)
            for i, off in enumerate(offs):
                piece = v[i * SLOTS : (i + 1) * SLOTS]
                piece = jnp.where(row_iota < length - off, piece, jnp.zeros_like(piece))
                v_scr[i * SLOTS : (i + 1) * SLOTS, :] = piece

            def attend(start, count):
                rows = pl.ds(start, count)
                index = start + lax.broadcasted_iota(jnp.int32, (count, 1), 0)
                mine = (index >= row_lo) & (index < row_hi)
                for h in range(GROUP // HD):
                    hc = slice(h * HD, (h + 1) * HD)
                    oc = pl.ds(pl.multiple_of(g * GROUP + h * HD, HD), HD)
                    q = jnp.concatenate([q_ref[rows, oc], qh[user][:, oc]], axis=0)
                    total = None
                    for n in range(0, n_keys, 2 * SLOTS):
                        w = weights_of(q, k_scr[n : n + 2 * SLOTS, hc])
                        parts = []
                        for i in range(2):
                            part = w[count:, i * SLOTS : (i + 1) * SLOTS]
                            seen = ahead >= offs[n // SLOTS + i] - my_off
                            parts.append(jnp.where(seen, part, 0.0).astype(BF16))
                        w = jnp.concatenate([w[:count].astype(BF16), jnp.concatenate(parts, axis=1)], axis=0)
                        pv = mm(w, v_scr[n : n + 2 * SLOTS, hc])
                        total = pv if total is None else total + pv
                    a_ref[rows, oc] += jnp.where(mine, total[:count], 0.0)
                    ah[user][:, oc] += total[count:]

            start = jnp.minimum((row_lo // 16) * 16, ROWS - WINDOW)
            narrow = row_hi <= start + WINDOW

            @pl.when(narrow)
            def _():
                attend(pl.multiple_of(start, 16), WINDOW)

            @pl.when(jnp.logical_not(narrow))
            def _():
                attend(0, ROWS)

    if not final:
        for copy in halves[STEPS - 1 :] + wholes:
            copy.start()
        for copy in halves + wholes:
            copy.wait()
        return
    y_scr = refs[3]
    owner_ref = vm["owner"]
    r_row = lax.broadcasted_iota(jnp.int32, (ROWS, ROWS), 0)
    r_col = lax.broadcasted_iota(jnp.int32, (ROWS, ROWS), 1)
    second = owner_ref[...].astype(F32)
    lower = jnp.where(r_col <= r_row, 1.0, 0.0).astype(BF16)
    ones_before = mm(lower, jnp.broadcast_to(second, (ROWS, HD)).astype(BF16))[:, :1]
    index = lax.broadcasted_iota(jnp.int32, (ROWS, 1), 0).astype(F32)
    n_first = ROWS - jnp.sum(second, axis=0, keepdims=True)
    place = jnp.where(second > 0.5, n_first + ones_before - 1.0, index - ones_before)
    back = jnp.where(r_col == place.astype(jnp.int32), 1.0, 0.0).astype(BF16)
    fetch.wait("late")
    for user in (0, 1):
        y = layer_norm(ah[user][...]) * vm["uh%d" % user][...].astype(F32)
        y_scr[user * SLOTS : (user + 1) * SLOTS, :] = y.astype(BF16)
    for n in range(0, ROWS, SLOTS):
        rows = slice(n, n + SLOTS)
        y = layer_norm(a_ref[rows, :]) * vm["u"][rows, :].astype(F32)
        y_scr[2 * SLOTS + n : 3 * SLOTS + n, :] = y.astype(BF16)

    @pl.loop(0, STEPS)
    def _(g):
        @pl.when(g == STEPS - 1)
        def _():
            for copy in halves[: STEPS - 1]:
                copy.start()

        cols = pl.ds(pl.multiple_of(g * GROUP, GROUP), GROUP)
        res = mm(y_scr[...], vm["w_out"][:, cols])
        for user in (0, 1):
            out = res[user * SLOTS : (user + 1) * SLOTS] + vm["xh%d" % user][:, cols].astype(F32)
            keep = scal_ref[user, 3] + row_iota < scal_ref[user, 0]
            made["hist"][user, :, cols] = jnp.where(keep, out, 0.0).astype(BF16)
        done = (res[2 * SLOTS :] + vm["xs"][:, cols].astype(F32)).astype(BF16)
        made["cand"][:, cols] = mm(back, done).astype(BF16)

    for copy in halves[STEPS - 1 :] + wholes:
        copy.start()
    for copy in halves + wholes:
        copy.wait()


def absorb(name, scal, items, w_in, q_cand, a_cand, first=False, state=None, final=None):
    users = sorted({item[0] for item in items})
    args = {"x%d" % n: item[2] for n, item in enumerate(items)}
    args.update(w_in=w_in, q=q_cand, a=a_cand)
    outs = {}
    sums, rows = pltpu.HBM((SLOTS, D), F32), pltpu.HBM((SLOTS, D), BF16)
    hbm, anywhere = pl.BlockSpec(memory_space=pltpu.HBM), pl.BlockSpec(memory_space=pl.ANY)
    if not first:
        for user in users:
            args["qh%d" % user] = state[user][0]
        for user in (0, 1) if final else users:
            args["ah%d" % user] = state[user][2]
    extra = []
    if final is not None:
        for user in (0, 1):
            args["uh%d" % user] = state[user][1]
            args["xh%d" % user] = final["own"][user]
        args.update({n: final[n] for n in ("u", "xs", "w_out", "owner")})
        outs = dict(
            hist=jax.ShapeDtypeStruct((2, SLOTS, D), BF16), cand=jax.ShapeDtypeStruct((ROWS, D), BF16)
        )
        extra = [pltpu.VMEM((2 * SLOTS + ROWS, D), BF16)]
    else:
        outs["a"] = pltpu.HBM((ROWS, D), F32)
        for user in users:
            outs["ah%d" % user] = sums
            if first:
                outs["qh%d" % user] = rows
                outs["uh%d" % user] = rows
    names = list(args)
    held = [n for n in names if n != "w_in"]
    most = max(sum(1 for item in items if item[0] == user) for user in users)
    plan = dict(
        items=tuple(item[:2] for item in items),
        first=first,
        final=final is not None,
        names=names,
        outs=list(outs),
        held=held,
        made=[n for n in outs if n not in held],
    )
    results = pl.pallas_call(
        functools.partial(absorb_kernel, plan),
        in_specs=[pl.BlockSpec(memory_space=pltpu.SMEM)]
        + [anywhere if n.startswith("x") and n != "xs" else hbm for n in names],
        out_specs=[hbm] * len(outs),
        out_shape=list(outs.values()),
        scratch_shapes=[pltpu.VMEM(args[n].shape, args[n].dtype) for n in held]
        + [pltpu.VMEM(outs[n].shape, outs[n].dtype) for n in plan["made"]]
        + [pltpu.VMEM((4 * STEPS, D, GROUP), BF16)]
        + [pltpu.VMEM((2 * most * SLOTS, GROUP), BF16)] * 2
        + extra
        + [pltpu.SemaphoreType.DMA((len(names) + 4 * STEPS,)), pltpu.SemaphoreType.DMA((STEPS + len(outs),))],
        compiler_params=pltpu.CompilerParams(vmem_limit_bytes=VMEM),
        cost_estimate=cost(),
        name=name,
    )(scal, *(args[n] if n.startswith("x") and n != "xs" else in_hbm(args[n]) for n in names))
    if final is not None:
        return results
    results = dict(zip(outs, results))
    new = dict(state or {})
    for user in users:
        if first:
            new[user] = tuple(results[n + str(user)] for n in ("qh", "uh", "ah"))
        else:
            new[user] = (state[user][0], state[user][1], results["ah%d" % user])
    return results["a"], new


def user_perm(dx, dy, dcore):
    pairs = []
    for u in range(4 * NX):
        x, y, core = u >> 2, (u >> 1) & 1, u & 1
        pairs.append((u, (((x + dx) % NX) * 2 + (y ^ dy)) * 2 + (core ^ dcore)))
    return pairs


def cand_perm(dz, dy):
    return [(c, (((c >> 1) + dz) % NZ) * 2 + ((c & 1) ^ dy)) for c in range(2 * NZ)]


def to_user(array, dx, dy, dcore):
    return lax.ppermute(array, "user", user_perm(dx, dy, dcore))


def to_cand(array, dz, dy):
    return lax.ppermute(array, "cand", cand_perm(dz, dy))


def local(pooled, cand_feats, hist_len, cand_user, w_in, w_out):
    user = lax.axis_index("user")
    cand = lax.axis_index("cand")
    x, y, core = user >> 2, (user >> 1) & 1, user & 1
    z, y_hi = cand >> 1, cand & 1
    owner = cand_user - 2 * user
    n_first = ROWS - jnp.sum(owner)
    offsets = [SLOTS * (((z + dz + NZ) % NZ) * 2 + (y_hi ^ e)) for dz in SHIFTS for e in range(2)]
    scal = jnp.stack(
        [
            jnp.stack([hist_len[0], 0 * user, n_first, cand * SLOTS] + offsets),
            jnp.stack([hist_len[1], n_first, 0 * user + ROWS, cand * SLOTS] + offsets),
        ]
    ).astype(jnp.int32)

    tables = pooled.reshape(NX, 2, 2, 2, SLOTS, D)
    place = jnp.stack([x, y, core]).astype(jnp.int32)
    with jax.named_scope("sum_core"):
        pack1 = pack(tables, 1 - core, 1)
        got1 = to_user(pack1, 0, 0, 1)
        pack0 = pack(after(tables, pack1), 1 - core, 0)
        got0 = to_user(pack0, 0, 0, 1)
    with jax.named_scope("sum_y_second"):
        over1 = over_y(place, tables, after(got1, pack0))
        y1 = to_user(over1, 0, 1, 0)
    with jax.named_scope("sum_x_first"):
        away0 = away_x(place, tables, after(got0, over1))
        x0 = [to_user(away0[d], d, 0, 0) for d in (1, 3, 2)]
    xs, u_cand, q_cand, a_cand = cand_project(after(owner.reshape(1, ROWS), away0), cand_feats, w_in)
    with jax.named_scope("sum_y_second"):
        away1 = join_y(place, tables, got1, after(y1, xs))
        x1 = [to_user(away1[d], d, 0, 0) for d in (1, 3, 2)]
    with jax.named_scope("sum_x_first"):
        mine0, over0 = join_x(place, away0[0], after(x0, away1))
        y0 = to_user(over0, 0, 1, 0)
    with jax.named_scope("gather"):
        own0 = norm_sum(place, [mine0, y0])
        near0 = to_cand(own0, 0, 1)
        own1 = norm_sum(place, [away1[0]] + after(x1, own0))
        near1 = to_cand(own1, 0, 1)
        pair0 = jnp.stack([own0, after(near0, own1)])
        z0 = {-1: to_cand(pair0, 1, 0), 1: to_cand(pair0, -1, 0)}
        pair1 = jnp.stack([own1, after(near1, pair0)])
        z1 = {-1: to_cand(pair1, 1, 0), 1: to_cand(pair1, -1, 0)}
    put = functools.partial(absorb, scal=scal, w_in=w_in, q_cand=q_cand)
    a_cand, state = put("own_pairs", items=[(0, 0, pair0), (1, 0, pair1)], a_cand=a_cand, first=True)
    with jax.named_scope("gather"):
        z0 = after(z0, a_cand)
        far0 = to_cand(z0[-1], 1, 0)
    a_cand, state = put(
        "side_first", items=[(0, -1, z0[-1]), (0, 1, z0[1])], a_cand=a_cand, state=state
    )
    with jax.named_scope("gather"):
        z1 = after(z1, a_cand)
        far1 = to_cand(z1[1], -1, 0)
    a_cand, state = put(
        "side_second",
        items=[(1, -1, z1[-1]), (1, 1, z1[1]), (0, 2, far0)],
        a_cand=a_cand,
        state=state,
    )
    return put(
        "far_finish",
        items=[(1, 2, far1)],
        a_cand=a_cand,
        state=state,
        final=dict(
            own={0: own0, 1: own1}, u=u_cand, xs=xs, owner=owner.reshape(ROWS, 1), w_out=w_out
        ),
    )


def solution(mesh):
    placed = (
        P("user", None, "cand", None),
        P(("user", "cand"), None),
        P("user"),
        P(("user", "cand")),
        P(),
        P(),
    )
    return jax.shard_map(
        local,
        mesh=mesh,
        in_specs=placed,
        out_specs=(P("user", "cand", None), P(("user", "cand"), None)),
        check_vma=False,
    )
```

```python
import functools

import jax
import jax.numpy as jnp
from jax import lax
from jax.experimental import pallas as pl
from jax.experimental.pallas import tpu as pltpu
from jax.sharding import PartitionSpec as P

F32 = jnp.float32
BF16 = jnp.bfloat16
HEADS = 8
HD = 128
D = 1024
SLOTS = 128
ROWS = 512
NX, NZ = 4, 4
WINDOW = 320
HALF_SCALE = 0.5 / (HD**0.5)
VMEM = 20 * 1024 * 1024
GROUP = 512
SHIFTS = (0, -1, 1, 2)


def silu(v):
    half = v * 0.5
    return half + half * jnp.tanh(half)


def layer_norm(rows):
    mean = jnp.mean(rows, axis=-1, keepdims=True)
    centered = rows - mean
    var = jnp.mean(centered * centered, axis=-1, keepdims=True)
    return centered * lax.rsqrt(var + 1e-05)


def mm(a, b):
    return jnp.dot(a, b, preferred_element_type=F32)


def weights_of(queries, keys):
    s = lax.dot_general(queries, keys, (((1,), (1,)), ((), ())), preferred_element_type=F32)
    half = s * HALF_SCALE
    return half + half * jnp.tanh(half)


def after(value, *others):
    return lax.optimization_barrier((value, others))[0]


def in_hbm(array):
    return pltpu.with_memory_space_constraint(array, pltpu.HBM)


def cost():
    return pl.CostEstimate(flops=10**6, bytes_accessed=1 << 16, transcendentals=0)


def block_sums(name, scal, arrays, shapes, sums, hbm=True):
    loads = [part for _, _, parts, _ in sums for part in parts]

    def body(scal_ref, *refs):
        ins, refs = refs[: len(arrays)], refs[len(arrays) :]
        outs, refs = refs[: len(shapes)], refs[len(shapes) :]
        bufs, refs = refs[: len(loads)], refs[len(loads) :]
        res, (in_sems, out_sems) = refs[: len(sums)], refs[len(sums) :]
        copies = []
        for n, (at, index) in enumerate(loads):
            lead = index(scal_ref)
            src = ins[at].at[lead] if lead else ins[at]
            copies.append(pltpu.make_async_copy(src, bufs[n], in_sems.at[n]))
            copies[-1].start()
        stores, used = [], 0
        for n, (out, lead, parts, norm) in enumerate(sums):
            total = None
            for k in range(used, used + len(parts)):
                copies[k].wait()
                value = bufs[k][...].astype(F32)
                total = value if total is None else total + value
            used += len(parts)
            res[n][...] = (layer_norm(total) if norm else total).astype(res[n].dtype)
            dst = outs[out].at[lead] if lead else outs[out]
            stores.append(pltpu.make_async_copy(res[n], dst, out_sems.at[n]))
            stores[-1].start()
        for store in stores:
            store.wait()

    spec = pl.BlockSpec(memory_space=pltpu.HBM)
    return pl.pallas_call(
        body,
        in_specs=[pl.BlockSpec(memory_space=pltpu.SMEM)]
        + [spec if a.ndim == 6 else pl.BlockSpec(memory_space=pl.ANY) for a in arrays],
        out_specs=[spec if hbm else pl.BlockSpec(memory_space=pl.ANY)] * len(shapes),
        out_shape=[(pltpu.HBM if hbm else jax.ShapeDtypeStruct)(shape, dtype) for shape, dtype in shapes],
        scratch_shapes=[pltpu.VMEM((SLOTS, D), arrays[at].dtype) for at, _ in loads]
        + [pltpu.VMEM((SLOTS, D), shapes[out][1]) for out, _, _, _ in sums]
        + [pltpu.SemaphoreType.DMA((len(loads),)), pltpu.SemaphoreType.DMA((len(sums),))],
        compiler_params=pltpu.CompilerParams(vmem_limit_bytes=VMEM),
        cost_estimate=cost(),
        name=name,
    )(scal, *(in_hbm(a) if a.ndim == 6 else a for a in arrays))


def pack(place, tables, j):
    sums = [
        (0, (x, y), [(0, lambda s, x=x, y=y: (x, y, 1 - s[2], j))], False)
        for x in range(NX)
        for y in range(2)
    ]
    return block_sums("pack", place, [tables], [((NX, 2, SLOTS, D), BF16)], sums)[0]


def over_y(place, tables, got):
    sums = [
        (
            0,
            (x,),
            [(0, lambda s, x=x: (x, 1 - s[1], s[2], 1)), (1, lambda s, x=x: (x, 1 - s[1]))],
            False,
        )
        for x in range(NX)
    ]
    return block_sums("over_y", place, [tables, got], [((NX, SLOTS, D), BF16)], sums)[0]


def away_x(place, tables, got):
    sums = []
    for d in (1, 3, 2, 0):
        for y in range(2):
            at = lambda s, d=d: lax.rem(s[0] + d, NX)
            parts = [
                (0, lambda s, at=at, y=y: (at(s), y, s[2], 0)),
                (1, lambda s, at=at, y=y: (at(s), y)),
            ]
            sums.append((d, (y,), parts, False))
    return block_sums("away_x", place, [tables, got], [((2, SLOTS, D), BF16)] * NX, sums)


def join_x(place, away, arrived):
    arrays = [away] + list(arrived)
    sums = [
        (1, (), [(n, lambda s: (1 - s[1],)) for n in range(NX)], False),
        (0, (), [(n, lambda s: (s[1],)) for n in range(NX)], False),
    ]
    return block_sums("join_x", place, arrays, [((SLOTS, D), F32), ((SLOTS, D), BF16)], sums, False)


def join_y(place, tables, got, arrived):
    sums = []
    for d in (1, 3, 2, 0):
        at = lambda s, d=d: lax.rem(s[0] + d, NX)
        parts = [
            (0, lambda s, at=at: (at(s), s[1], s[2], 1)),
            (1, lambda s, at=at: (at(s), s[1])),
            (2, lambda s, at=at: (at(s),)),
        ]
        sums.append((d, (), parts, False))
    shapes = [((SLOTS, D), F32 if d == 0 else BF16) for d in range(NX)]
    return block_sums("join_y", place, [tables, got, arrived], shapes, sums)


def norm_sum(place, arrays):
    parts = [(n, lambda s: ()) for n in range(len(arrays))]
    return block_sums("norm_sum", place, arrays, [((SLOTS, D), BF16)], [(0, (), parts, True)], False)[0]


def join_pair(place, own, near):
    sums = [(0, (n,), [(n, lambda s: ())], False) for n in range(2)]
    return block_sums("join_pair", place, [own, near], [((2, SLOTS, D), BF16)], sums, False)[0]


def in_vmem(array):
    return pltpu.with_memory_space_constraint(array, pltpu.VMEM)


def kernel_call(body, name, arrays, out_shape, scratch, scalars=None, aliases=None):
    vmem = pl.BlockSpec(memory_space=pltpu.VMEM)
    in_specs, args = [vmem] * len(arrays), [in_vmem(array) for array in arrays]
    if scalars is not None:
        in_specs = [pl.BlockSpec(memory_space=pltpu.SMEM)] + in_specs
        args = [scalars] + args
    return pl.pallas_call(
        body,
        in_specs=in_specs,
        out_specs=[vmem] * len(out_shape),
        out_shape=out_shape,
        scratch_shapes=scratch,
        input_output_aliases=aliases or {},
        compiler_params=pltpu.CompilerParams(vmem_limit_bytes=VMEM),
        cost_estimate=cost(),
        name=name,
    )(*args)


def cand_kernel(owner_ref, feats_ref, w_ref, xs_ref, u_ref, q_ref, back_ref, a_ref):
    second = owner_ref[...].astype(F32)
    r_from = lax.broadcasted_iota(jnp.int32, (ROWS, ROWS), 0)
    r_to = lax.broadcasted_iota(jnp.int32, (ROWS, ROWS), 1)
    upper = jnp.where(r_from <= r_to, 1.0, 0.0).astype(BF16)
    ones_before = mm(jnp.broadcast_to(second, (8, ROWS)).astype(BF16), upper)[:1]
    index = lax.broadcasted_iota(jnp.int32, (1, ROWS), 1).astype(F32)
    n_first = ROWS - jnp.sum(second, axis=1, keepdims=True)
    place = jnp.where(second > 0.5, n_first + ones_before - 1.0, index - ones_before)
    onehot = jnp.where(r_from == place.astype(jnp.int32), 1.0, 0.0)
    back_ref[...] = onehot.T.astype(BF16)
    onehot = onehot.astype(BF16)
    x = layer_norm(feats_ref[...].astype(F32)).astype(BF16)
    xs_ref[...] = mm(onehot, x).astype(BF16)

    @pl.loop(0, D // GROUP)
    def _(g):
        cols = lambda n: pl.ds(pl.multiple_of(n * D + g * GROUP, GROUP), GROUP)
        u, v, q, k = (silu(mm(xs_ref[...], w_ref[:, cols(n)])).astype(BF16) for n in range(4))
        u_ref[:, cols(0)] = u
        q_ref[:, cols(0)] = q
        prod = q.astype(F32) * k.astype(F32)
        for h in range(GROUP // HD):
            hc = slice(h * HD, (h + 1) * HD)
            half = jnp.sum(prod[:, hc], axis=-1, keepdims=True) * HALF_SCALE
            own = (half + half * jnp.tanh(half)).astype(BF16).astype(F32)
            out_cols = pl.ds(pl.multiple_of(g * GROUP + h * HD, HD), HD)
            a_ref[:, out_cols] = own * v[:, hc].astype(F32)


def cand_project(owner_row, feats, w_in):
    rows = jax.ShapeDtypeStruct((ROWS, D), BF16)
    out_shape = [rows, rows, rows, jax.ShapeDtypeStruct((ROWS, ROWS), BF16), jax.ShapeDtypeStruct((ROWS, D), F32)]
    return kernel_call(cand_kernel, "cand_project", [owner_row, feats, w_in], out_shape, [])


def absorb_kernel(plan, scal_ref, *refs):
    users, every, first, final = plan["users"], plan["every"], plan["first"], plan["final"]
    refs = list(refs)
    take = lambda n: [refs.pop(0) for _ in range(n)]
    keys = [(user, shift, e, ref) for (user, shift, es), ref in zip(plan["items"], take(len(plan["items"]))) for e in es]
    w_ref, q_ref, a_ref = take(3)
    if first:
        own_ref = dict(zip(users, take(len(users))))
    else:
        qh_ref = dict(zip(users, take(len(users))))
        ah_ref = dict(zip(every, take(len(every))))
    if final:
        uh_ref = dict(zip(every, take(len(every))))
        xh_ref = dict(zip(every, take(len(every))))
        u_ref, xs_ref, back_ref, wo_ref = take(4)
        hist_ref, cand_ref = take(2)
    else:
        take(1)
        if first:
            ah_ref = dict(zip(users, take(len(users))))
            qh_ref = dict(zip(users, take(len(users))))
            uh_ref = dict(zip(users, take(len(users))))
        else:
            take(len(users))
    k_scr, v_scr = take(2)
    if final:
        (y_scr,) = take(1)
    row_iota = lax.broadcasted_iota(jnp.int32, (SLOTS, 1), 0)
    ahead = lax.broadcasted_iota(jnp.int32, (SLOTS, SLOTS), 0) - lax.broadcasted_iota(
        jnp.int32, (SLOTS, SLOTS), 1
    )
    for user in users:
        length = scal_ref[user, 0]
        row_lo = scal_ref[user, 1]
        row_hi = scal_ref[user, 2]
        my_off = scal_ref[user, 3]
        mine_keys = [(shift, e, ref) for (u, shift, e, ref) in keys if u == user]
        offs = [scal_ref[user, 4 + 2 * SHIFTS.index(shift) + e] for shift, e, _ in mine_keys]
        n_keys = SLOTS * len(offs)

        @pl.loop(0, D // GROUP)
        def _(g):
            cols = lambda n: pl.ds(pl.multiple_of(n * D + g * GROUP, GROUP), GROUP)
            if first:
                x_own = own_ref[user][...]
                qh_ref[user][:, cols(0)] = silu(mm(x_own, w_ref[:, cols(2)])).astype(BF16)
                uh_ref[user][:, cols(0)] = silu(mm(x_own, w_ref[:, cols(0)])).astype(BF16)
                ah_ref[user][:, cols(0)] = jnp.zeros((SLOTS, GROUP), F32)
            x = jnp.concatenate([ref[min(e, ref.shape[0] - 1)] for _, e, ref in mine_keys], axis=0)
            k_scr[:n_keys, :] = silu(mm(x, w_ref[:, cols(3)])).astype(BF16)
            v = silu(mm(x, w_ref[:, cols(1)])).astype(BF16)
            for i, off in enumerate(offs):
                piece = v[i * SLOTS : (i + 1) * SLOTS]
                piece = jnp.where(row_iota < length - off, piece, jnp.zeros_like(piece))
                v_scr[i * SLOTS : (i + 1) * SLOTS, :] = piece

            def attend(start, count):
                rows = pl.ds(start, count)
                index = start + lax.broadcasted_iota(jnp.int32, (count, 1), 0)
                mine = (index >= row_lo) & (index < row_hi)
                for h in range(GROUP // HD):
                    hc = slice(h * HD, (h + 1) * HD)
                    oc = pl.ds(pl.multiple_of(g * GROUP + h * HD, HD), HD)
                    q = jnp.concatenate([q_ref[rows, oc], qh_ref[user][:, oc]], axis=0)
                    total = None
                    for n in range(0, n_keys, 2 * SLOTS):
                        w = weights_of(q, k_scr[n : n + 2 * SLOTS, hc])
                        parts = []
                        for i in range(2):
                            part = w[count:, i * SLOTS : (i + 1) * SLOTS]
                            seen = ahead >= offs[n // SLOTS + i] - my_off
                            parts.append(jnp.where(seen, part, 0.0).astype(BF16))
                        w = jnp.concatenate([w[:count].astype(BF16), jnp.concatenate(parts, axis=1)], axis=0)
                        pv = mm(w, v_scr[n : n + 2 * SLOTS, hc])
                        total = pv if total is None else total + pv
                    a_ref[rows, oc] += jnp.where(mine, total[:count], 0.0)
                    ah_ref[user][:, oc] += total[count:]

            start = jnp.minimum((row_lo // 16) * 16, ROWS - WINDOW)
            narrow = row_hi <= start + WINDOW

            @pl.when(narrow)
            def _():
                attend(pl.multiple_of(start, 16), WINDOW)

            @pl.when(jnp.logical_not(narrow))
            def _():
                attend(0, ROWS)

    if final:
        n_hist = SLOTS * len(every)
        for i, user in enumerate(every):
            y = layer_norm(ah_ref[user][...]) * uh_ref[user][...].astype(F32)
            y_scr[i * SLOTS : (i + 1) * SLOTS, :] = y.astype(BF16)

        @pl.loop(0, ROWS // SLOTS)
        def _(n):
            rows = pl.ds(pl.multiple_of(n * SLOTS, SLOTS), SLOTS)
            y = layer_norm(a_ref[rows, :]) * u_ref[rows, :].astype(F32)
            y_scr[pl.ds(pl.multiple_of(n_hist + n * SLOTS, SLOTS), SLOTS), :] = y.astype(BF16)

        @pl.loop(0, D // GROUP)
        def _(g):
            cols = pl.ds(pl.multiple_of(g * GROUP, GROUP), GROUP)
            res = mm(y_scr[...], wo_ref[:, cols])
            for i, user in enumerate(every):
                out = res[i * SLOTS : (i + 1) * SLOTS] + xh_ref[user][:, cols].astype(F32)
                keep = scal_ref[user, 3] + row_iota < scal_ref[user, 0]
                hist_ref[user, :, cols] = jnp.where(keep, out, 0.0).astype(BF16)
            done = (res[n_hist:] + xs_ref[:, cols].astype(F32)).astype(BF16)
            cand_ref[:, cols] = mm(back_ref[...], done).astype(BF16)


def absorb(name, scal, items, w_in, q_cand, a_cand, first=None, state=None, final=None):
    users = tuple(sorted({item[0] for item in items}))
    every = (0, 1) if final is not None else users
    plan = dict(items=tuple(item[:3] for item in items), users=users, every=every, first=first is not None, final=final is not None)
    arrays = [item[3] for item in items] + [w_in, q_cand, a_cand]
    n = len(users)
    a_at = len(arrays)
    sums = jax.ShapeDtypeStruct((SLOTS, D), F32)
    rows = jax.ShapeDtypeStruct((SLOTS, D), BF16)
    most = max(sum(len(item[2]) for item in items if item[0] == user) for user in users)
    scratch = [pltpu.VMEM((most * SLOTS, GROUP), BF16)] * 2
    out_shape = [jax.ShapeDtypeStruct((ROWS, D), F32)]
    aliases = {a_at: 0}
    if first is not None:
        arrays += [first[user] for user in users]
        out_shape += [sums] * n + [rows] * (2 * n)
    else:
        arrays += [state[user][0] for user in users]
        aliases.update({len(arrays) + 1 + i: 1 + i for i in range(n)})
        arrays += [state[user][2] for user in every]
        out_shape += [sums] * n
    if final is not None:
        arrays += [state[user][1] for user in every]
        arrays += [final["own"][user] for user in every]
        arrays += [final["u"], final["xs"], final["back"], final["w_out"]]
        out_shape = [jax.ShapeDtypeStruct((2, SLOTS, D), BF16), jax.ShapeDtypeStruct((ROWS, D), BF16)]
        aliases = {}
        scratch.append(pltpu.VMEM((2 * SLOTS + ROWS, D), BF16))
    outs = kernel_call(
        functools.partial(absorb_kernel, plan), name, arrays, out_shape, scratch, scal, aliases
    )
    if final is not None:
        return outs
    new = dict(state or {})
    for i, user in enumerate(users):
        if first is not None:
            new[user] = (outs[1 + n + i], outs[1 + 2 * n + i], outs[1 + i])
        else:
            new[user] = (state[user][0], state[user][1], outs[1 + i])
    return outs[0], new


def user_perm(dx, dy, dcore):
    pairs = []
    for u in range(4 * NX):
        x, y, core = u >> 2, (u >> 1) & 1, u & 1
        pairs.append((u, (((x + dx) % NX) * 2 + (y ^ dy)) * 2 + (core ^ dcore)))
    return pairs


def cand_perm(dz, dy):
    return [(c, (((c >> 1) + dz) % NZ) * 2 + ((c & 1) ^ dy)) for c in range(2 * NZ)]


def to_user(array, dx, dy, dcore):
    return lax.ppermute(array, "user", user_perm(dx, dy, dcore))


def to_cand(array, dz, dy):
    return lax.ppermute(array, "cand", cand_perm(dz, dy))


def local(pooled, cand_feats, hist_len, cand_user, w_in, w_out):
    user = lax.axis_index("user")
    cand = lax.axis_index("cand")
    x, y, core = user >> 2, (user >> 1) & 1, user & 1
    z, y_hi = cand >> 1, cand & 1
    owner = cand_user - 2 * user
    n_first = ROWS - jnp.sum(owner)
    offsets = [SLOTS * (((z + dz + NZ) % NZ) * 2 + (y_hi ^ e)) for dz in SHIFTS for e in range(2)]
    scal = jnp.stack(
        [
            jnp.stack([hist_len[0], 0 * user, n_first, cand * SLOTS] + offsets),
            jnp.stack([hist_len[1], n_first, 0 * user + ROWS, cand * SLOTS] + offsets),
        ]
    ).astype(jnp.int32)

    tables = pooled.reshape(NX, 2, 2, 2, SLOTS, D)
    place = jnp.stack([x, y, core]).astype(jnp.int32)
    with jax.named_scope("sum_core"):
        pack1 = pack(place, tables, 1)
        got1 = to_user(pack1, 0, 0, 1)
        pack0 = pack(place, after(tables, pack1), 0)
        got0 = to_user(pack0, 0, 0, 1)
    with jax.named_scope("sum_y_second"):
        over1 = over_y(place, tables, after(got1, pack0))
        y1 = to_user(over1, 0, 1, 0)
    with jax.named_scope("sum_x_first"):
        away0 = away_x(place, tables, after(got0, over1))
        x0 = [to_user(away0[d], d, 0, 0) for d in (1, 3, 2)]
    owner_row, scal = after((owner.reshape(1, ROWS), scal), away0)
    xs, u_cand, q_cand, back, a_cand = cand_project(owner_row, cand_feats, w_in)
    with jax.named_scope("sum_y_second"):
        away1 = join_y(place, tables, got1, after(y1, xs, scal))
        x1 = [to_user(away1[d], d, 0, 0) for d in (1, 3, 2)]
    with jax.named_scope("sum_x_first"):
        mine0, over0 = join_x(place, away0[0], after(x0, away1))
        y0 = to_user(over0, 0, 1, 0)
    with jax.named_scope("gather"):
        own1 = norm_sum(place, [away1[0]] + after(x1, mine0))
        near1 = to_cand(own1, 0, 1)
        own0 = norm_sum(place, [mine0, after(y0, own1)])
        near0 = to_cand(own0, 0, 1)
        pair1 = join_pair(place, own1, after(near1, own0))
        z1 = {-1: to_cand(pair1, 1, 0), 1: to_cand(pair1, -1, 0)}
        pair0 = join_pair(place, own0, after(near0, pair1))
        z0 = {-1: to_cand(pair0, 1, 0), 1: to_cand(pair0, -1, 0)}
    both = (0, 1)
    put = functools.partial(absorb, scal=scal, w_in=w_in, q_cand=q_cand)
    a_cand, state = put(
        "own_pairs",
        items=[(1, 0, both, pair1), (0, 0, both, pair0)],
        a_cand=a_cand,
        first={0: own0, 1: own1},
    )
    with jax.named_scope("gather"):
        z1 = after(z1, a_cand)
        far1 = to_cand(z1[1], -1, 0)
    a_cand, state = put(
        "side_second",
        items=[(1, -1, both, z1[-1]), (1, 1, both, z1[1])],
        a_cand=a_cand,
        state=state,
    )
    with jax.named_scope("gather"):
        z0 = after(z0, a_cand)
        far0 = to_cand(z0[-1], 1, 0)
    a_cand, state = put(
        "side_first",
        items=[(0, -1, both, z0[-1]), (0, 1, both, z0[1]), (1, 2, both, far1)],
        a_cand=a_cand,
        state=state,
    )
    return put(
        "far_finish",
        items=[(0, 2, both, far0)],
        a_cand=a_cand,
        state=state,
        final=dict(own={0: own0, 1: own1}, u=u_cand, xs=xs, back=back, w_out=w_out),
    )


def solution(mesh):
    placed = (
        P("user", None, "cand", None),
        P(("user", "cand"), None),
        P("user"),
        P(("user", "cand")),
        P(),
        P(),
    )
    return jax.shard_map(
        local,
        mesh=mesh,
        in_specs=placed,
        out_specs=(P("user", "cand", None), P(("user", "cand"), None)),
        check_vma=False,
    )
```

```python
import functools

import jax
import jax.numpy as jnp
from jax import lax
from jax.experimental import pallas as pl
from jax.experimental.pallas import tpu as pltpu
from jax.sharding import PartitionSpec as P

F32 = jnp.float32
BF16 = jnp.bfloat16
HEADS = 8
HD = 128
D = 1024
SLOTS = 128
ROWS = 512
NX, NZ = 4, 4
WINDOW = 320
HALF_SCALE = 0.5 / (HD**0.5)
VMEM = 20 * 1024 * 1024
GROUP = 512
SHIFTS = (0, -1, 1, 2)


def silu(v):
    half = v * 0.5
    return half + half * jnp.tanh(half)


def layer_norm(rows):
    mean = jnp.mean(rows, axis=-1, keepdims=True)
    centered = rows - mean
    var = jnp.mean(centered * centered, axis=-1, keepdims=True)
    return centered * lax.rsqrt(var + 1e-05)


def mm(a, b):
    return jnp.dot(a, b, preferred_element_type=F32)


def weights_of(queries, keys):
    s = lax.dot_general(queries, keys, (((1,), (1,)), ((), ())), preferred_element_type=F32)
    half = s * HALF_SCALE
    return half + half * jnp.tanh(half)


def after(value, *others):
    return lax.optimization_barrier((value, others))[0]


def in_hbm(array):
    return pltpu.with_memory_space_constraint(array, pltpu.HBM)


def cost():
    return pl.CostEstimate(flops=10**6, bytes_accessed=1 << 16, transcendentals=0)


def block_sums(name, scal, arrays, shapes, sums, hbm=True):
    loads = [part for _, _, parts, _ in sums for part in parts]

    def body(scal_ref, *refs):
        ins, refs = refs[: len(arrays)], refs[len(arrays) :]
        outs, refs = refs[: len(shapes)], refs[len(shapes) :]
        bufs, refs = refs[: len(loads)], refs[len(loads) :]
        res, (in_sems, out_sems) = refs[: len(sums)], refs[len(sums) :]
        copies = []
        for n, (at, index) in enumerate(loads):
            lead = index(scal_ref)
            src = ins[at].at[lead] if lead else ins[at]
            copies.append(pltpu.make_async_copy(src, bufs[n], in_sems.at[n]))
            copies[-1].start()
        stores, used = [], 0
        for n, (out, lead, parts, norm) in enumerate(sums):
            total = None
            for k in range(used, used + len(parts)):
                copies[k].wait()
                value = bufs[k][...].astype(F32)
                total = value if total is None else total + value
            used += len(parts)
            res[n][...] = (layer_norm(total) if norm else total).astype(res[n].dtype)
            dst = outs[out].at[lead] if lead else outs[out]
            stores.append(pltpu.make_async_copy(res[n], dst, out_sems.at[n]))
            stores[-1].start()
        for store in stores:
            store.wait()

    spec = pl.BlockSpec(memory_space=pltpu.HBM)
    return pl.pallas_call(
        body,
        in_specs=[pl.BlockSpec(memory_space=pltpu.SMEM)]
        + [spec if a.ndim == 6 else pl.BlockSpec(memory_space=pl.ANY) for a in arrays],
        out_specs=[spec if hbm else pl.BlockSpec(memory_space=pl.ANY)] * len(shapes),
        out_shape=[(pltpu.HBM if hbm else jax.ShapeDtypeStruct)(shape, dtype) for shape, dtype in shapes],
        scratch_shapes=[pltpu.VMEM((SLOTS, D), arrays[at].dtype) for at, _ in loads]
        + [pltpu.VMEM((SLOTS, D), shapes[out][1]) for out, _, _, _ in sums]
        + [pltpu.SemaphoreType.DMA((len(loads),)), pltpu.SemaphoreType.DMA((len(sums),))],
        compiler_params=pltpu.CompilerParams(vmem_limit_bytes=VMEM),
        cost_estimate=cost(),
        name=name,
    )(scal, *(in_hbm(a) if a.ndim == 6 else a for a in arrays))


def pack(place, tables, j):
    sums = [
        (0, (x, y), [(0, lambda s, x=x, y=y: (x, y, 1 - s[2], j))], False)
        for x in range(NX)
        for y in range(2)
    ]
    return block_sums("pack", place, [tables], [((NX, 2, SLOTS, D), BF16)], sums)[0]


def over_y(place, tables, got):
    sums = [
        (
            0,
            (x,),
            [(0, lambda s, x=x: (x, 1 - s[1], s[2], 1)), (1, lambda s, x=x: (x, 1 - s[1]))],
            False,
        )
        for x in range(NX)
    ]
    return block_sums("over_y", place, [tables, got], [((NX, SLOTS, D), BF16)], sums)[0]


def away_x(place, tables, got):
    sums = []
    for d in (1, 3, 2, 0):
        for y in range(2):
            at = lambda s, d=d: lax.rem(s[0] + d, NX)
            parts = [
                (0, lambda s, at=at, y=y: (at(s), y, s[2], 0)),
                (1, lambda s, at=at, y=y: (at(s), y)),
            ]
            sums.append((d, (y,), parts, False))
    return block_sums("away_x", place, [tables, got], [((2, SLOTS, D), BF16)] * NX, sums)


def join_x(place, away, arrived):
    arrays = [away] + list(arrived)
    sums = [
        (1, (), [(n, lambda s: (1 - s[1],)) for n in range(NX)], False),
        (0, (), [(n, lambda s: (s[1],)) for n in range(NX)], False),
    ]
    return block_sums("join_x", place, arrays, [((SLOTS, D), F32), ((SLOTS, D), BF16)], sums, False)


def join_y(place, tables, got, arrived):
    sums = []
    for d in (1, 3, 2, 0):
        at = lambda s, d=d: lax.rem(s[0] + d, NX)
        parts = [
            (0, lambda s, at=at: (at(s), s[1], s[2], 1)),
            (1, lambda s, at=at: (at(s), s[1])),
            (2, lambda s, at=at: (at(s),)),
        ]
        sums.append((d, (), parts, False))
    shapes = [((SLOTS, D), F32 if d == 0 else BF16) for d in range(NX)]
    return block_sums("join_y", place, [tables, got, arrived], shapes, sums)


def norm_sum(place, arrays):
    parts = [(n, lambda s: ()) for n in range(len(arrays))]
    return block_sums("norm_sum", place, arrays, [((SLOTS, D), BF16)], [(0, (), parts, True)], False)[0]


def norm_both(place, first, second):
    parts = [(n, lambda s: ()) for n in range(len(first) + 1)]
    sums = [(0, (1,), parts[-1:], False), (0, (0,), parts[:-1], True)]
    return block_sums("norm_both", place, list(first) + [second], [((2, SLOTS, D), BF16)], sums, False)[0]


def in_vmem(array):
    return pltpu.with_memory_space_constraint(array, pltpu.VMEM)


def kernel_call(body, name, arrays, out_shape, scratch, scalars=None, aliases=None):
    vmem = pl.BlockSpec(memory_space=pltpu.VMEM)
    in_specs, args = [vmem] * len(arrays), [in_vmem(array) for array in arrays]
    if scalars is not None:
        in_specs = [pl.BlockSpec(memory_space=pltpu.SMEM)] + in_specs
        args = [scalars] + args
    return pl.pallas_call(
        body,
        in_specs=in_specs,
        out_specs=[vmem] * len(out_shape),
        out_shape=out_shape,
        scratch_shapes=scratch,
        input_output_aliases=aliases or {},
        compiler_params=pltpu.CompilerParams(vmem_limit_bytes=VMEM),
        cost_estimate=cost(),
        name=name,
    )(*args)


def cand_kernel(owner_ref, feats_ref, w_ref, xs_ref, u_ref, q_ref, back_ref, a_ref):
    second = owner_ref[...].astype(F32)
    r_from = lax.broadcasted_iota(jnp.int32, (ROWS, ROWS), 0)
    r_to = lax.broadcasted_iota(jnp.int32, (ROWS, ROWS), 1)
    upper = jnp.where(r_from <= r_to, 1.0, 0.0).astype(BF16)
    ones_before = mm(jnp.broadcast_to(second, (8, ROWS)).astype(BF16), upper)[:1]
    index = lax.broadcasted_iota(jnp.int32, (1, ROWS), 1).astype(F32)
    n_first = ROWS - jnp.sum(second, axis=1, keepdims=True)
    place = jnp.where(second > 0.5, n_first + ones_before - 1.0, index - ones_before)
    onehot = jnp.where(r_from == place.astype(jnp.int32), 1.0, 0.0)
    back_ref[...] = onehot.T.astype(BF16)
    onehot = onehot.astype(BF16)
    x = layer_norm(feats_ref[...].astype(F32)).astype(BF16)
    xs_ref[...] = mm(onehot, x).astype(BF16)

    @pl.loop(0, D // GROUP)
    def _(g):
        cols = lambda n: pl.ds(pl.multiple_of(n * D + g * GROUP, GROUP), GROUP)
        u, v, q, k = (silu(mm(xs_ref[...], w_ref[:, cols(n)])).astype(BF16) for n in range(4))
        u_ref[:, cols(0)] = u
        q_ref[:, cols(0)] = q
        prod = q.astype(F32) * k.astype(F32)
        for h in range(GROUP // HD):
            hc = slice(h * HD, (h + 1) * HD)
            half = jnp.sum(prod[:, hc], axis=-1, keepdims=True) * HALF_SCALE
            own = (half + half * jnp.tanh(half)).astype(BF16).astype(F32)
            out_cols = pl.ds(pl.multiple_of(g * GROUP + h * HD, HD), HD)
            a_ref[:, out_cols] = own * v[:, hc].astype(F32)


def cand_project(owner_row, feats, w_in):
    rows = jax.ShapeDtypeStruct((ROWS, D), BF16)
    out_shape = [rows, rows, rows, jax.ShapeDtypeStruct((ROWS, ROWS), BF16), jax.ShapeDtypeStruct((ROWS, D), F32)]
    return kernel_call(cand_kernel, "cand_project", [owner_row, feats, w_in], out_shape, [])


def absorb_kernel(plan, scal_ref, *refs):
    pieces, first, final = plan
    count = len(pieces)
    refs = list(refs)
    take = lambda n: [refs.pop(0) for _ in range(n)]
    x_refs = take(count)
    w_ref, q_ref, a_ref = take(3)
    if not first:
        qh_ref, ah_ref = take(2)
    if final:
        uh_ref, own_ref, u_ref, xs_ref, back_ref, wo_ref, hist_ref, cand_ref = take(8)
    elif first:
        _, ah_ref, qh_ref, uh_ref = take(4)
    else:
        take(2)
    k_scr, v_scr = take(2)
    row_iota = lax.broadcasted_iota(jnp.int32, (SLOTS, 1), 0)
    ahead = lax.broadcasted_iota(jnp.int32, (SLOTS, SLOTS), 0) - lax.broadcasted_iota(
        jnp.int32, (SLOTS, SLOTS), 1
    )
    offs = [scal_ref[0, 4 + piece] for piece in pieces]
    my_off = scal_ref[0, 3]

    @pl.loop(0, D // GROUP)
    def _(g):
        cols = lambda n: pl.ds(pl.multiple_of(n * D + g * GROUP, GROUP), GROUP)
        if first:
            own = x_refs[0][...].reshape(2 * SLOTS, D)
            qh_ref[:, cols(0)] = silu(mm(own, w_ref[:, cols(2)])).astype(BF16)
            uh_ref[:, cols(0)] = silu(mm(own, w_ref[:, cols(0)])).astype(BF16)
            ah_ref[:, cols(0)] = jnp.zeros((2 * SLOTS, GROUP), F32)
        x = jnp.concatenate([ref[...].reshape(2 * SLOTS, D) for ref in x_refs], axis=0)
        k = silu(mm(x, w_ref[:, cols(3)])).astype(BF16)
        v = silu(mm(x, w_ref[:, cols(1)])).astype(BF16)
        for n in range(count):
            to = slice(n * SLOTS, (n + 1) * SLOTS)
            for user in (0, 1):
                at = slice((2 * n + user) * SLOTS, (2 * n + user + 1) * SLOTS)
                live = row_iota < scal_ref[user, 0] - offs[n]
                k_scr[user, to, :] = k[at]
                v_scr[user, to, :] = jnp.where(live, v[at], jnp.zeros_like(v[at]))

        for user in (0, 1):
            row_lo = scal_ref[user, 1]
            row_hi = scal_ref[user, 2]
            mine_rows = slice(user * SLOTS, (user + 1) * SLOTS)

            def attend(start, n_rows):
                rows = pl.ds(start, n_rows)
                index = start + lax.broadcasted_iota(jnp.int32, (n_rows, 1), 0)
                mine = (index >= row_lo) & (index < row_hi)
                for h in range(GROUP // HD):
                    hc = slice(h * HD, (h + 1) * HD)
                    oc = pl.ds(pl.multiple_of(g * GROUP + h * HD, HD), HD)
                    q = jnp.concatenate([q_ref[rows, oc], qh_ref[mine_rows, oc]], axis=0)
                    w = weights_of(q, k_scr[user, :, hc])
                    parts = []
                    for n in range(count):
                        part = w[n_rows:, n * SLOTS : (n + 1) * SLOTS]
                        parts.append(jnp.where(ahead >= offs[n] - my_off, part, 0.0).astype(BF16))
                    hist_w = jnp.concatenate(parts, axis=1)
                    w = jnp.concatenate([w[:n_rows].astype(BF16), hist_w], axis=0)
                    total = mm(w, v_scr[user, :, hc])
                    a_ref[rows, oc] += jnp.where(mine, total[:n_rows], 0.0)
                    ah_ref[mine_rows, oc] += total[n_rows:]

            start = jnp.minimum((row_lo // 16) * 16, ROWS - WINDOW)
            narrow = row_hi <= start + WINDOW

            @pl.when(narrow)
            def _():
                attend(pl.multiple_of(start, 16), WINDOW)

            @pl.when(jnp.logical_not(narrow))
            def _():
                attend(0, ROWS)

    if final:
        (y_scr,) = take(1)
        n_hist = 2 * SLOTS
        y = layer_norm(ah_ref[...]) * uh_ref[...].astype(F32)
        y_scr[:n_hist, :] = y.astype(BF16)

        @pl.loop(0, ROWS // SLOTS)
        def _(n):
            rows = pl.ds(pl.multiple_of(n * SLOTS, SLOTS), SLOTS)
            y = layer_norm(a_ref[rows, :]) * u_ref[rows, :].astype(F32)
            y_scr[pl.ds(pl.multiple_of(n_hist + n * SLOTS, SLOTS), SLOTS), :] = y.astype(BF16)

        @pl.loop(0, D // GROUP)
        def _(g):
            cols = pl.ds(pl.multiple_of(g * GROUP, GROUP), GROUP)
            res = mm(y_scr[...], wo_ref[:, cols])
            for user in (0, 1):
                out = res[user * SLOTS : (user + 1) * SLOTS] + own_ref[user, :, cols].astype(F32)
                keep = my_off + row_iota < scal_ref[user, 0]
                hist_ref[user, :, cols] = jnp.where(keep, out, 0.0).astype(BF16)
            done = (res[n_hist:] + xs_ref[:, cols].astype(F32)).astype(BF16)
            cand_ref[:, cols] = mm(back_ref[...], done).astype(BF16)


def absorb(name, scal, items, w_in, q_cand, a_cand, state=None, final=None):
    pieces = tuple(item[0] for item in items)
    arrays = [item[1] for item in items] + [w_in, q_cand, a_cand]
    a_at = len(arrays)
    scratch = [pltpu.VMEM((2, len(pieces) * SLOTS, GROUP), BF16)] * 2
    sums = jax.ShapeDtypeStruct((2 * SLOTS, D), F32)
    rows = jax.ShapeDtypeStruct((2 * SLOTS, D), BF16)
    out_shape = [jax.ShapeDtypeStruct((ROWS, D), F32), sums]
    aliases = {a_at: 0}
    first = state is None
    if first:
        out_shape += [rows, rows]
    else:
        arrays += [state[0], state[2]]
        aliases[a_at + 2] = 1
    if final is not None:
        arrays += [state[1]] + list(final)
        out_shape = [jax.ShapeDtypeStruct((2, SLOTS, D), BF16), jax.ShapeDtypeStruct((ROWS, D), BF16)]
        aliases = {}
        scratch.append(pltpu.VMEM((2 * SLOTS + ROWS, D), BF16))
    outs = kernel_call(
        functools.partial(absorb_kernel, (pieces, first, final is not None)),
        name,
        arrays,
        out_shape,
        scratch,
        scal,
        aliases,
    )
    if final is not None:
        return outs
    return outs[0], (outs[2], outs[3], outs[1]) if first else (state[0], state[1], outs[1])


def user_perm(dx, dy, dcore):
    pairs = []
    for u in range(4 * NX):
        x, y, core = u >> 2, (u >> 1) & 1, u & 1
        pairs.append((u, (((x + dx) % NX) * 2 + (y ^ dy)) * 2 + (core ^ dcore)))
    return pairs


def cand_perm(dz, dy):
    return [(c, (((c >> 1) + dz) % NZ) * 2 + ((c & 1) ^ dy)) for c in range(2 * NZ)]


def to_user(array, dx, dy, dcore):
    return lax.ppermute(array, "user", user_perm(dx, dy, dcore))


def to_cand(array, dz, dy):
    return lax.ppermute(array, "cand", cand_perm(dz, dy))


def local(pooled, cand_feats, hist_len, cand_user, w_in, w_out):
    user = lax.axis_index("user")
    cand = lax.axis_index("cand")
    x, y, core = user >> 2, (user >> 1) & 1, user & 1
    z, y_hi = cand >> 1, cand & 1
    owner = cand_user - 2 * user
    n_first = ROWS - jnp.sum(owner)
    offsets = [SLOTS * (((z + dz + NZ) % NZ) * 2 + (y_hi ^ e)) for dz in SHIFTS for e in range(2)]
    scal = jnp.stack(
        [
            jnp.stack([hist_len[0], 0 * user, n_first, cand * SLOTS] + offsets),
            jnp.stack([hist_len[1], n_first, 0 * user + ROWS, cand * SLOTS] + offsets),
        ]
    ).astype(jnp.int32)

    tables = pooled.reshape(NX, 2, 2, 2, SLOTS, D)
    place = jnp.stack([x, y, core]).astype(jnp.int32)
    with jax.named_scope("sum_core"):
        pack1 = pack(place, tables, 1)
        got1 = to_user(pack1, 0, 0, 1)
        pack0 = pack(place, after(tables, pack1), 0)
        got0 = to_user(pack0, 0, 0, 1)
    with jax.named_scope("sum_y_second"):
        over1 = over_y(place, tables, after(got1, pack0))
        y1 = to_user(over1, 0, 1, 0)
    with jax.named_scope("sum_x_first"):
        away0 = away_x(place, tables, after(got0, over1))
        x0 = [to_user(away0[d], d, 0, 0) for d in (1, 3, 2)]
    owner_row, scal = after((owner.reshape(1, ROWS), scal), away0)
    xs, u_cand, q_cand, back, a_cand = cand_project(owner_row, cand_feats, w_in)
    with jax.named_scope("sum_y_second"):
        away1 = join_y(place, tables, got1, after(y1, xs, scal))
        x1 = [to_user(away1[d], d, 0, 0) for d in (1, 3, 2)]
    with jax.named_scope("sum_x_first"):
        mine0, over0 = join_x(place, away0[0], after(x0, away1))
        y0 = to_user(over0, 0, 1, 0)
    with jax.named_scope("gather"):
        own1 = norm_sum(place, [away1[0]] + after(x1, mine0))
        own = norm_both(place, [mine0, after(y0, own1)], own1)
        near = to_cand(own, 0, 1)
        own_left, own_right = to_cand(own, 1, 0), to_cand(own, -1, 0)
    put = functools.partial(absorb, scal=scal, w_in=w_in, q_cand=q_cand)
    piece = lambda shift, e: 2 * SHIFTS.index(shift) + e
    a_cand, state = put("own_keys", items=[(piece(0, 0), own)], a_cand=a_cand)
    with jax.named_scope("gather"):
        near = after(near, a_cand)
        near_left, near_right = to_cand(near, 1, 0), to_cand(near, -1, 0)
        own_left, own_right = after((own_left, own_right), near)
        own_far = to_cand(own_left, 1, 0)
    a_cand, state = put(
        "own_sides",
        items=[(piece(-1, 0), own_left), (piece(1, 0), own_right), (piece(0, 1), near)],
        a_cand=a_cand,
        state=state,
    )
    with jax.named_scope("gather"):
        near_left, near_right = after((near_left, near_right), a_cand)
        near_far = to_cand(near_right, -1, 0)
    a_cand, state = put(
        "near_sides",
        items=[(piece(-1, 1), near_left), (piece(1, 1), near_right), (piece(2, 0), own_far)],
        a_cand=a_cand,
        state=state,
    )
    return put(
        "far_finish",
        items=[(piece(2, 1), near_far)],
        a_cand=a_cand,
        state=state,
        final=(own, u_cand, xs, back, w_out),
    )


def solution(mesh):
    placed = (
        P("user", None, "cand", None),
        P(("user", "cand"), None),
        P("user"),
        P(("user", "cand")),
        P(),
        P(),
    )
    return jax.shard_map(
        local,
        mesh=mesh,
        in_specs=placed,
        out_specs=(P("user", "cand", None), P(("user", "cand"), None)),
        check_vma=False,
    )
```

```python
import functools

import jax
import jax.numpy as jnp
from jax import lax
from jax.experimental import pallas as pl
from jax.experimental.pallas import tpu as pltpu
from jax.sharding import PartitionSpec as P

F32 = jnp.float32
BF16 = jnp.bfloat16
HEADS = 8
HD = 128
D = 1024
SLOTS = 128
ROWS = 512
NX, NZ = 4, 4
WINDOW = 320
HALF_SCALE = 0.5 / (HD**0.5)
VMEM = 20 * 1024 * 1024
GROUP = 512
SHIFTS = (0, -1, 1, 2)


def silu(v):
    half = v * 0.5
    half = half.astype(BF16)
    return half + half * jnp.tanh(half)


def layer_norm(rows):
    mean = jnp.mean(rows, axis=-1, keepdims=True)
    centered = rows - mean
    var = jnp.mean(centered * centered, axis=-1, keepdims=True)
    return centered * lax.rsqrt(var + 1e-05)


def mm(a, b):
    return jnp.dot(a, b, preferred_element_type=F32)


def weights_of(queries, keys):
    s = lax.dot_general(queries, keys, (((1,), (1,)), ((), ())), preferred_element_type=F32)
    half = (s * HALF_SCALE).astype(BF16)
    return half + half * jnp.tanh(half)


def after(value, *others):
    return lax.optimization_barrier((value, others))[0]


def in_hbm(array):
    return pltpu.with_memory_space_constraint(array, pltpu.HBM)


def cost():
    return pl.CostEstimate(flops=10**6, bytes_accessed=1 << 16, transcendentals=0)


def block_sums(name, scal, arrays, shapes, sums, hbm=True):
    loads = [part for _, _, parts, _ in sums for part in parts]

    def body(scal_ref, *refs):
        ins, refs = refs[: len(arrays)], refs[len(arrays) :]
        outs, refs = refs[: len(shapes)], refs[len(shapes) :]
        bufs, refs = refs[: len(loads)], refs[len(loads) :]
        res, (in_sems, out_sems) = refs[: len(sums)], refs[len(sums) :]
        copies = []
        for n, (at, index) in enumerate(loads):
            lead = index(scal_ref)
            src = ins[at].at[lead] if lead else ins[at]
            copies.append(pltpu.make_async_copy(src, bufs[n], in_sems.at[n]))
            copies[-1].start()
        stores, used = [], 0
        for n, (out, lead, parts, norm) in enumerate(sums):
            total = None
            for k in range(used, used + len(parts)):
                copies[k].wait()
                value = bufs[k][...].astype(F32)
                total = value if total is None else total + value
            used += len(parts)
            res[n][...] = (layer_norm(total) if norm else total).astype(res[n].dtype)
            dst = outs[out].at[lead] if lead else outs[out]
            stores.append(pltpu.make_async_copy(res[n], dst, out_sems.at[n]))
            stores[-1].start()
        for store in stores:
            store.wait()

    spec = pl.BlockSpec(memory_space=pltpu.HBM)
    return pl.pallas_call(
        body,
        in_specs=[pl.BlockSpec(memory_space=pltpu.SMEM)]
        + [spec if a.ndim == 6 else pl.BlockSpec(memory_space=pl.ANY) for a in arrays],
        out_specs=[spec if hbm else pl.BlockSpec(memory_space=pl.ANY)] * len(shapes),
        out_shape=[(pltpu.HBM if hbm else jax.ShapeDtypeStruct)(shape, dtype) for shape, dtype in shapes],
        scratch_shapes=[pltpu.VMEM((SLOTS, D), arrays[at].dtype) for at, _ in loads]
        + [pltpu.VMEM((SLOTS, D), shapes[out][1]) for out, _, _, _ in sums]
        + [pltpu.SemaphoreType.DMA((len(loads),)), pltpu.SemaphoreType.DMA((len(sums),))],
        compiler_params=pltpu.CompilerParams(vmem_limit_bytes=VMEM),
        cost_estimate=cost(),
        name=name,
    )(scal, *(in_hbm(a) if a.ndim == 6 else a for a in arrays))


def pack(place, tables):
    sums = [(0, (x,), [(0, lambda s, x=x: (x, 1 - s[1], 1 - s[2], 1))], False) for x in range(NX)]
    return block_sums("pack", place, [tables], [((NX, SLOTS, D), BF16)], sums)[0]


def pack_all(place, tables):
    sums = [
        (y, (x,), [(0, lambda s, x=x, y=y: (x, y, 1 - s[2], 0))], False)
        for x in range(NX)
        for y in range(2)
    ]
    return block_sums("pack_all", place, [tables], [((NX, SLOTS, D), BF16)] * 2, sums)


def over_y(place, tables, got):
    sums = [
        (0, (x,), [(0, lambda s, x=x: (x, 1 - s[1], s[2], 1)), (1, lambda s, x=x: (x,))], False)
        for x in range(NX)
    ]
    return block_sums("over_y", place, [tables, got], [((NX, SLOTS, D), BF16)], sums)[0]


def away_x(place, tables, got):
    sums = []
    for d in (1, 3, 2, 0):
        for y in range(2):
            at = lambda s, d=d: lax.rem(s[0] + d, NX)
            parts = [
                (0, lambda s, at=at, y=y: (at(s), y, s[2], 0)),
                (1 + y, lambda s, at=at: (at(s),)),
            ]
            sums.append((d, (y,), parts, False))
    for n in range(NX):
        sums.append((NX, (n,), [(0, lambda s, n=n: (n, s[1], 1 - s[2], 1))], False))
    shapes = [((2, SLOTS, D), BF16)] * NX + [((NX, SLOTS, D), BF16)]
    return block_sums("away_x", place, [tables] + list(got), shapes, sums)


def join_x(place, away, arrived):
    arrays = [away] + list(arrived)
    sums = [
        (1, (), [(n, lambda s: (1 - s[1],)) for n in range(NX)], False),
        (0, (), [(n, lambda s: (s[1],)) for n in range(NX)], False),
    ]
    return block_sums("join_x", place, arrays, [((SLOTS, D), F32), ((SLOTS, D), BF16)], sums, False)


def join_y(place, tables, got, arrived):
    sums = []
    for d in (1, 3, 2, 0):
        at = lambda s, d=d: lax.rem(s[0] + d, NX)
        parts = [
            (0, lambda s, at=at: (at(s), s[1], s[2], 1)),
            (1, lambda s, at=at: (at(s),)),
            (2, lambda s, at=at: (at(s),)),
        ]
        sums.append((d, (), parts, False))
    shapes = [((SLOTS, D), F32 if d == 0 else BF16) for d in range(NX)]
    return block_sums("join_y", place, [tables, got, arrived], shapes, sums)


def norm_sum(place, arrays):
    parts = [(n, lambda s: ()) for n in range(len(arrays))]
    return block_sums("norm_sum", place, arrays, [((SLOTS, D), BF16)], [(0, (), parts, True)], False)[0]


def norm_both(place, first, second):
    parts = [(n, lambda s: ()) for n in range(len(first) + 1)]
    sums = [(0, (1,), parts[-1:], False), (0, (0,), parts[:-1], True)]
    return block_sums("norm_both", place, list(first) + [second], [((2, SLOTS, D), BF16)], sums, False)[0]


def in_vmem(array):
    return pltpu.with_memory_space_constraint(array, pltpu.VMEM)


def kernel_call(body, name, arrays, out_shape, scratch, scalars=None, aliases=None):
    vmem = pl.BlockSpec(memory_space=pltpu.VMEM)
    in_specs, args = [vmem] * len(arrays), [in_vmem(array) for array in arrays]
    if scalars is not None:
        in_specs = [pl.BlockSpec(memory_space=pltpu.SMEM)] + in_specs
        args = [scalars] + args
    return pl.pallas_call(
        body,
        in_specs=in_specs,
        out_specs=[vmem] * len(out_shape),
        out_shape=out_shape,
        scratch_shapes=scratch,
        input_output_aliases=aliases or {},
        compiler_params=pltpu.CompilerParams(vmem_limit_bytes=VMEM),
        cost_estimate=cost(),
        name=name,
    )(*args)


def cand_kernel(owner_ref, feats_ref, w_ref, xs_ref, u_ref, q_ref, back_ref, a_ref):
    second = owner_ref[...].astype(F32)
    r_from = lax.broadcasted_iota(jnp.int32, (ROWS, ROWS), 0)
    r_to = lax.broadcasted_iota(jnp.int32, (ROWS, ROWS), 1)
    upper = jnp.where(r_from <= r_to, 1.0, 0.0).astype(BF16)
    ones_before = mm(jnp.broadcast_to(second, (8, ROWS)).astype(BF16), upper)[:1]
    index = lax.broadcasted_iota(jnp.int32, (1, ROWS), 1).astype(F32)
    n_first = ROWS - jnp.sum(second, axis=1, keepdims=True)
    place = jnp.where(second > 0.5, n_first + ones_before - 1.0, index - ones_before)
    onehot = jnp.where(r_from == place.astype(jnp.int32), 1.0, 0.0)
    back_ref[...] = onehot.T.astype(BF16)
    onehot = onehot.astype(BF16)
    x = layer_norm(feats_ref[...].astype(F32)).astype(BF16)
    xs_ref[...] = mm(onehot, x).astype(BF16)

    @pl.loop(0, D // GROUP)
    def _(g):
        cols = lambda n: pl.ds(pl.multiple_of(n * D + g * GROUP, GROUP), GROUP)
        u, v, q, k = (silu(mm(xs_ref[...], w_ref[:, cols(n)])).astype(BF16) for n in range(4))
        u_ref[:, cols(0)] = u
        q_ref[:, cols(0)] = q
        prod = q.astype(F32) * k.astype(F32)
        for h in range(GROUP // HD):
            hc = slice(h * HD, (h + 1) * HD)
            half = jnp.sum(prod[:, hc], axis=-1, keepdims=True) * HALF_SCALE
            own = (half + half * jnp.tanh(half)).astype(BF16).astype(F32)
            out_cols = pl.ds(pl.multiple_of(g * GROUP + h * HD, HD), HD)
            a_ref[:, out_cols] = own * v[:, hc].astype(F32)


def cand_project(owner_row, feats, w_in):
    rows = jax.ShapeDtypeStruct((ROWS, D), BF16)
    out_shape = [rows, rows, rows, jax.ShapeDtypeStruct((ROWS, ROWS), BF16), jax.ShapeDtypeStruct((ROWS, D), F32)]
    return kernel_call(cand_kernel, "cand_project", [owner_row, feats, w_in], out_shape, [])


def absorb_kernel(plan, scal_ref, *refs):
    pieces, first, final = plan
    count = len(pieces)
    refs = list(refs)
    take = lambda n: [refs.pop(0) for _ in range(n)]
    x_refs = take(count)
    w_ref, q_ref, a_ref = take(3)
    if not first:
        qh_ref, ah_ref = take(2)
    if final:
        uh_ref, own_ref, u_ref, xs_ref, back_ref, wo_ref, hist_ref, cand_ref = take(8)
    elif first:
        _, ah_ref, qh_ref, uh_ref = take(4)
    else:
        take(2)
    k_scr, v_scr = take(2)
    row_iota = lax.broadcasted_iota(jnp.int32, (SLOTS, 1), 0)
    ahead = lax.broadcasted_iota(jnp.int32, (SLOTS, SLOTS), 0) - lax.broadcasted_iota(
        jnp.int32, (SLOTS, SLOTS), 1
    )
    offs = [scal_ref[0, 4 + piece] for piece in pieces]
    my_off = scal_ref[0, 3]

    steps = D // GROUP

    def column(n, g):
        if isinstance(g, int):
            return slice(n * D + g * GROUP, n * D + (g + 1) * GROUP)
        return pl.ds(pl.multiple_of(n * D + g * GROUP, GROUP), GROUP)

    def head_column(g, h):
        if isinstance(g, int):
            return slice(g * GROUP + h * HD, g * GROUP + (h + 1) * HD)
        return pl.ds(pl.multiple_of(g * GROUP + h * HD, HD), HD)

    def project(g, slot, n):
        x = x_refs[n][...].reshape(2 * SLOTS, D)
        if first and n == 0:
            qh_ref[:, column(0, g)] = silu(mm(x, w_ref[:, column(2, g)])).astype(BF16)
            uh_ref[:, column(0, g)] = silu(mm(x, w_ref[:, column(0, g)])).astype(BF16)
            ah_ref[:, column(0, g)] = jnp.zeros((2 * SLOTS, GROUP), F32)
        k = silu(mm(x, w_ref[:, column(3, g)])).astype(BF16)
        v = silu(mm(x, w_ref[:, column(1, g)])).astype(BF16)
        to = slice(n * SLOTS, (n + 1) * SLOTS)
        for user in (0, 1):
            at = slice(user * SLOTS, (user + 1) * SLOTS)
            live = row_iota < scal_ref[user, 0] - offs[n]
            k_scr[slot, user, to, :] = k[at]
            v_scr[slot, user, to, :] = jnp.where(live, v[at], jnp.zeros_like(v[at]))

    def attend(g, slot, user, h, start, n_rows):
        rows = pl.ds(start, n_rows)
        index = start + lax.broadcasted_iota(jnp.int32, (n_rows, 1), 0)
        mine = (index >= scal_ref[user, 1]) & (index < scal_ref[user, 2])
        mine_rows = slice(user * SLOTS, (user + 1) * SLOTS)
        hc = slice(h * HD, (h + 1) * HD)
        oc = head_column(g, h)
        q = jnp.concatenate([q_ref[rows, oc], qh_ref[mine_rows, oc]], axis=0)
        w = weights_of(q, k_scr[slot, user, :, hc])
        parts = []
        for n in range(count):
            part = w[n_rows:, n * SLOTS : (n + 1) * SLOTS]
            parts.append(jnp.where(ahead >= offs[n] - my_off, part, jnp.zeros_like(part)).astype(BF16))
        w = jnp.concatenate([w[:n_rows].astype(BF16), jnp.concatenate(parts, axis=1)], axis=0)
        total = mm(w, v_scr[slot, user, :, hc])
        a_ref[rows, oc] += jnp.where(mine, total[:n_rows], 0.0)
        ah_ref[mine_rows, oc] += total[n_rows:]

    starts = [jnp.minimum((scal_ref[user, 1] // 16) * 16, ROWS - WINDOW) for user in (0, 1)]
    fits = [scal_ref[user, 2] <= starts[user] + WINDOW for user in (0, 1)]
    narrow = fits[0] & fits[1]
    pairs = [(user, h) for user in (0, 1) for h in range(GROUP // HD)]

    @pl.when(narrow)
    def _():
        at = [pl.multiple_of(start, 16) for start in starts]
        for n in range(count):
            project(0, 0, n)
        for g in range(steps):
            left = list(range(count)) if g + 1 < steps else []
            gap = max(1, len(pairs) // max(1, len(left)))
            for i, (user, h) in enumerate(pairs):
                if left and i % gap == 0:
                    project(g + 1, (g + 1) % 2, left.pop(0))
                attend(g, g % 2, user, h, at[user], WINDOW)
            for n in left:
                project(g + 1, (g + 1) % 2, n)

    @pl.when(jnp.logical_not(narrow))
    def _():
        @pl.loop(0, steps)
        def _(g):
            for n in range(count):
                project(g, 0, n)
            for user, h in pairs:
                attend(g, 0, user, h, 0, ROWS)

    if final:
        (y_scr,) = take(1)
        n_hist = 2 * SLOTS
        y = layer_norm(ah_ref[...]) * uh_ref[...].astype(F32)
        y_scr[:n_hist, :] = y.astype(BF16)

        @pl.loop(0, ROWS // SLOTS)
        def _(n):
            rows = pl.ds(pl.multiple_of(n * SLOTS, SLOTS), SLOTS)
            y = layer_norm(a_ref[rows, :]) * u_ref[rows, :].astype(F32)
            y_scr[pl.ds(pl.multiple_of(n_hist + n * SLOTS, SLOTS), SLOTS), :] = y.astype(BF16)

        @pl.loop(0, D // GROUP)
        def _(g):
            cols = pl.ds(pl.multiple_of(g * GROUP, GROUP), GROUP)
            res = mm(y_scr[...], wo_ref[:, cols])
            for user in (0, 1):
                out = res[user * SLOTS : (user + 1) * SLOTS] + own_ref[user, :, cols].astype(F32)
                keep = my_off + row_iota < scal_ref[user, 0]
                hist_ref[user, :, cols] = jnp.where(keep, out, 0.0).astype(BF16)
            done = (res[n_hist:] + xs_ref[:, cols].astype(F32)).astype(BF16)
            cand_ref[:, cols] = mm(back_ref[...], done).astype(BF16)


def absorb(name, scal, items, w_in, q_cand, a_cand, state=None, final=None):
    pieces = tuple(item[0] for item in items)
    arrays = [item[1] for item in items] + [w_in, q_cand, a_cand]
    a_at = len(arrays)
    scratch = [pltpu.VMEM((2, 2, len(pieces) * SLOTS, GROUP), BF16)] * 2
    sums = jax.ShapeDtypeStruct((2 * SLOTS, D), F32)
    rows = jax.ShapeDtypeStruct((2 * SLOTS, D), BF16)
    out_shape = [jax.ShapeDtypeStruct((ROWS, D), F32), sums]
    aliases = {a_at: 0}
    first = state is None
    if first:
        out_shape += [rows, rows]
    else:
        arrays += [state[0], state[2]]
        aliases[a_at + 2] = 1
    if final is not None:
        arrays += [state[1]] + list(final)
        out_shape = [jax.ShapeDtypeStruct((2, SLOTS, D), BF16), jax.ShapeDtypeStruct((ROWS, D), BF16)]
        aliases = {}
        scratch.append(pltpu.VMEM((2 * SLOTS + ROWS, D), BF16))
    outs = kernel_call(
        functools.partial(absorb_kernel, (pieces, first, final is not None)),
        name,
        arrays,
        out_shape,
        scratch,
        scal,
        aliases,
    )
    if final is not None:
        return outs
    return outs[0], (outs[2], outs[3], outs[1]) if first else (state[0], state[1], outs[1])


def user_perm(dx, dy, dcore):
    pairs = []
    for u in range(4 * NX):
        x, y, core = u >> 2, (u >> 1) & 1, u & 1
        pairs.append((u, (((x + dx) % NX) * 2 + (y ^ dy)) * 2 + (core ^ dcore)))
    return pairs


def cand_perm(dz, dy):
    return [(c, (((c >> 1) + dz) % NZ) * 2 + ((c & 1) ^ dy)) for c in range(2 * NZ)]


def to_user(array, dx, dy, dcore):
    return lax.ppermute(array, "user", user_perm(dx, dy, dcore))


def to_cand(array, dz, dy):
    return lax.ppermute(array, "cand", cand_perm(dz, dy))


def local(pooled, cand_feats, hist_len, cand_user, w_in, w_out):
    user = lax.axis_index("user")
    cand = lax.axis_index("cand")
    x, y, core = user >> 2, (user >> 1) & 1, user & 1
    z, y_hi = cand >> 1, cand & 1
    owner = cand_user - 2 * user
    n_first = ROWS - jnp.sum(owner)
    offsets = [SLOTS * (((z + dz + NZ) % NZ) * 2 + (y_hi ^ e)) for dz in SHIFTS for e in range(2)]
    scal = jnp.stack(
        [
            jnp.stack([hist_len[0], 0 * user, n_first, cand * SLOTS] + offsets),
            jnp.stack([hist_len[1], n_first, 0 * user + ROWS, cand * SLOTS] + offsets),
        ]
    ).astype(jnp.int32)

    tables = pooled.reshape(NX, 2, 2, 2, SLOTS, D)
    place = jnp.stack([x, y, core]).astype(jnp.int32)
    with jax.named_scope("sum_core"):
        pack1 = pack(place, tables)
        got1 = to_user(pack1, 0, 0, 1)
        pack0 = pack_all(place, after(tables, pack1))
        got0 = [to_user(part, 0, 0, 1) for part in pack0]
    with jax.named_scope("sum_y_second"):
        over1 = over_y(place, tables, after(got1, pack0))
        y1 = to_user(over1, 0, 1, 0)
    with jax.named_scope("sum_x_first"):
        *away0, pack2 = away_x(place, tables, after(got0, over1))
        x0 = [to_user(away0[d], d, 0, 0) for d in (1, 3, 2)]
    with jax.named_scope("sum_core"):
        got2 = to_user(pack2, 0, 0, 1)
    owner_row, scal = after((owner.reshape(1, ROWS), scal), pack2)
    xs, u_cand, q_cand, back, a_cand = cand_project(owner_row, cand_feats, w_in)
    with jax.named_scope("sum_y_second"):
        away1 = join_y(place, tables, got2, after(y1, xs, scal))
        x1 = [to_user(away1[d], d, 0, 0) for d in (1, 3, 2)]
    with jax.named_scope("sum_x_first"):
        mine0, over0 = join_x(place, away0[0], after(x0, away1))
        y0 = to_user(over0, 0, 1, 0)
    with jax.named_scope("gather"):
        own1 = norm_sum(place, [away1[0]] + after(x1, mine0))
        own = norm_both(place, [mine0, after(y0, own1)], own1)
        near = to_cand(own, 0, 1)
        own_left, own_right = to_cand(own, 1, 0), to_cand(own, -1, 0)
    put = functools.partial(absorb, scal=scal, w_in=w_in, q_cand=q_cand)
    piece = lambda shift, e: 2 * SHIFTS.index(shift) + e
    a_cand, state = put("own_keys", items=[(piece(0, 0), own)], a_cand=a_cand)
    with jax.named_scope("gather"):
        near = after(near, a_cand)
        near_left, near_right = to_cand(near, 1, 0), to_cand(near, -1, 0)
        own_left, own_right = after((own_left, own_right), near)
        own_far = to_cand(own_left, 1, 0)
    a_cand, state = put(
        "own_sides",
        items=[(piece(-1, 0), own_left), (piece(1, 0), own_right), (piece(0, 1), near)],
        a_cand=a_cand,
        state=state,
    )
    with jax.named_scope("gather"):
        near_left, near_right = after((near_left, near_right), a_cand)
        near_far = to_cand(near_right, -1, 0)
    a_cand, state = put(
        "near_sides",
        items=[(piece(-1, 1), near_left), (piece(1, 1), near_right)],
        a_cand=a_cand,
        state=state,
    )
    return put(
        "far_finish",
        items=[(piece(2, 0), own_far), (piece(2, 1), near_far)],
        a_cand=a_cand,
        state=state,
        final=(own, u_cand, xs, back, w_out),
    )


def solution(mesh):
    placed = (
        P("user", None, "cand", None),
        P(("user", "cand"), None),
        P("user"),
        P(("user", "cand")),
        P(),
        P(),
    )
    return jax.shard_map(
        local,
        mesh=mesh,
        in_specs=placed,
        out_specs=(P("user", "cand", None), P(("user", "cand"), None)),
        check_vma=False,
    )
```

```python
import functools

import jax
import jax.numpy as jnp
from jax import lax
from jax.experimental import pallas as pl
from jax.experimental.pallas import tpu as pltpu
from jax.sharding import PartitionSpec as P

F32 = jnp.float32
BF16 = jnp.bfloat16
HEADS = 8
HD = 128
D = 1024
SLOTS = 128
ROWS = 512
NX, NZ = 4, 4
WINDOW = 320
HALF_SCALE = 0.5 / (HD**0.5)
VMEM = 20 * 1024 * 1024
GROUP = 512
SHIFTS = (0, -1, 1, 2)
HIDE = 1 << 16
HOPS = (1, 3, 2)
SIDES = (lambda s: s[1], lambda s: 1 - s[1])


def silu(v):
    half = v * 0.5
    half = half.astype(BF16)
    return half + half * jnp.tanh(half)


def layer_norm(rows):
    mean = jnp.mean(rows, axis=-1, keepdims=True)
    centered = rows - mean
    var = jnp.mean(centered * centered, axis=-1, keepdims=True)
    return centered * lax.rsqrt(var + 1e-05)


def mm(a, b):
    return jnp.dot(a, b, preferred_element_type=F32)


def weights_of(queries, keys):
    s = lax.dot_general(queries, keys, (((1,), (1,)), ((), ())), preferred_element_type=F32)
    half = (s * HALF_SCALE).astype(BF16)
    return half + half * jnp.tanh(half)


def after(value, *others):
    return lax.optimization_barrier((value, others))[0]


def in_hbm(array):
    return pltpu.with_memory_space_constraint(array, pltpu.HBM)


def cost():
    return pl.CostEstimate(flops=10**6, bytes_accessed=1 << 16, transcendentals=0)


def block_sums(name, scal, arrays, shapes, sums, hbm=True):
    loads = [part for _, _, parts, _ in sums for part in parts]

    def body(scal_ref, *refs):
        ins, refs = refs[: len(arrays)], refs[len(arrays) :]
        outs, refs = refs[: len(shapes)], refs[len(shapes) :]
        bufs, refs = refs[: len(loads)], refs[len(loads) :]
        res, (in_sems, out_sems) = refs[: len(sums)], refs[len(sums) :]
        copies = []
        for n, (at, index) in enumerate(loads):
            lead = index(scal_ref)
            src = ins[at].at[lead] if lead else ins[at]
            copies.append(pltpu.make_async_copy(src, bufs[n], in_sems.at[n]))
            copies[-1].start()
        stores, used = [], 0
        for n, (out, lead, parts, norm) in enumerate(sums):
            members = range(used, used + len(parts))
            used += len(parts)
            for k in members:
                copies[k].wait()
            ready = bufs[members[0]]
            if len(parts) > 1:
                ready = res[n]

                @pl.loop(0, SLOTS // 32)
                def _(r):
                    rows = pl.ds(pl.multiple_of(r * 32, 32), 32)
                    total = None
                    for k in members:
                        value = bufs[k][rows, :].astype(F32)
                        total = value if total is None else total + value
                    ready[rows, :] = (layer_norm(total) if norm else total).astype(ready.dtype)

            lead = (lead(scal_ref),) if callable(lead) else lead
            dst = outs[out].at[lead] if lead else outs[out]
            stores.append(pltpu.make_async_copy(ready, dst, out_sems.at[n]))
            stores[-1].start()
        for store in stores:
            store.wait()

    spec = pl.BlockSpec(memory_space=pltpu.HBM)
    return pl.pallas_call(
        body,
        in_specs=[pl.BlockSpec(memory_space=pltpu.SMEM)]
        + [spec if a.ndim == 6 else pl.BlockSpec(memory_space=pl.ANY) for a in arrays],
        out_specs=[spec if hbm else pl.BlockSpec(memory_space=pl.ANY)] * len(shapes),
        out_shape=[(pltpu.HBM if hbm else jax.ShapeDtypeStruct)(shape, dtype) for shape, dtype in shapes],
        scratch_shapes=[pltpu.VMEM((SLOTS, D), arrays[at].dtype) for at, _ in loads]
        + [
            pltpu.VMEM((SLOTS if len(parts) > 1 else 16, D), shapes[out][1])
            for out, _, parts, _ in sums
        ]
        + [pltpu.SemaphoreType.DMA((len(loads),)), pltpu.SemaphoreType.DMA((len(sums),))],
        compiler_params=pltpu.CompilerParams(vmem_limit_bytes=VMEM),
        cost_estimate=cost(),
        name=name,
    )(scal, *(in_hbm(a) if a.ndim == 6 else a for a in arrays))


def pack(place, tables):
    sums = [(0, (x,), [(0, lambda s, x=x: (x, 1 - s[1], 1 - s[2], 1))], False) for x in range(NX)]
    return block_sums("pack", place, [tables], [((NX, SLOTS, D), BF16)], sums)[0]


def pack_all(place, tables):
    sums = [
        (n, (x,), [(0, lambda s, x=x, side=side: (x, side(s), 1 - s[2], 0))], False)
        for x in range(NX)
        for n, side in enumerate(SIDES)
    ]
    return block_sums("pack_all", place, [tables], [((NX, SLOTS, D), BF16)] * 2, sums)


def over_y(place, tables, got):
    sums = [
        (0, (x,), [(0, lambda s, x=x: (x, 1 - s[1], s[2], 1)), (1, lambda s, x=x: (x,))], False)
        for x in range(NX)
    ]
    return block_sums("over_y", place, [tables, got], [((NX, SLOTS, D), BF16)], sums)[0]


def away_x(place, tables, got):
    sums = []
    for n, d in enumerate(HOPS):
        for m, side in enumerate(SIDES):
            at = lambda s, d=d: lax.rem(s[0] + d, NX)
            parts = [
                (0, lambda s, at=at, side=side: (at(s), side(s), s[2], 0)),
                (1 + m, lambda s, at=at: (at(s),)),
            ]
            sums.append((n, side, parts, False))
    for n in range(NX):
        sums.append((3, (n,), [(0, lambda s, n=n: (n, s[1], 1 - s[2], 1))], False))
    shapes = [((2, SLOTS, D), BF16)] * 3 + [((NX, SLOTS, D), BF16)]
    return block_sums("away_x", place, [tables] + list(got), shapes, sums)


def join_x(place, tables, got, arrived):
    arrays = [tables] + list(got) + list(arrived)
    sums = []
    for n in (1, 0):
        side = SIDES[n]
        parts = [(0, lambda s, side=side: (s[0], side(s), s[2], 0)), (1 + n, lambda s: (s[0],))]
        parts += [(3 + k, lambda s, side=side: (side(s),)) for k in range(3)]
        sums.append((n, (), parts, False))
    return block_sums("join_x", place, arrays, [((SLOTS, D), F32), ((SLOTS, D), BF16)], sums, False)


def join_y(place, tables, got, arrived):
    sums = []
    for n, d in enumerate(HOPS):
        at = lambda s, d=d: lax.rem(s[0] + d, NX)
        parts = [
            (0, lambda s, at=at: (at(s), s[1], s[2], 1)),
            (1, lambda s, at=at: (at(s),)),
            (2, lambda s, at=at: (at(s),)),
        ]
        sums.append((n, (), parts, False))
    return block_sums("join_y", place, [tables, got, arrived], [((SLOTS, D), BF16)] * 3, sums)


def norm_sum(place, tables, got, side, arrived):
    parts = [
        (0, lambda s: (s[0], s[1], s[2], 1)),
        (1, lambda s: (s[0],)),
        (2, lambda s: (s[0],)),
    ] + [(3 + n, lambda s: ()) for n in range(3)]
    arrays = [tables, got, side] + list(arrived)
    return block_sums("norm_sum", place, arrays, [((SLOTS, D), BF16)], [(0, (), parts, True)], False)[0]


def norm_both(place, first, second):
    parts = [(n, lambda s: ()) for n in range(len(first) + 1)]
    sums = [(0, (1,), parts[-1:], False), (0, (0,), parts[:-1], True)]
    return block_sums("norm_both", place, list(first) + [second], [((2, SLOTS, D), BF16)], sums, False)[0]


def in_vmem(array):
    return pltpu.with_memory_space_constraint(array, pltpu.VMEM)


def kernel_call(body, name, arrays, out_shape, scratch, scalars=None, aliases=None):
    vmem = pl.BlockSpec(memory_space=pltpu.VMEM)
    in_specs, args = [vmem] * len(arrays), [in_vmem(array) for array in arrays]
    if scalars is not None:
        in_specs = [pl.BlockSpec(memory_space=pltpu.SMEM)] + in_specs
        args = [scalars] + args
    return pl.pallas_call(
        body,
        in_specs=in_specs,
        out_specs=[vmem] * len(out_shape),
        out_shape=out_shape,
        scratch_shapes=scratch,
        input_output_aliases=aliases or {},
        compiler_params=pltpu.CompilerParams(vmem_limit_bytes=VMEM),
        cost_estimate=cost(),
        name=name,
    )(*args)


def cand_kernel(owner_ref, feats_ref, w_ref, xs_ref, u_ref, q_ref, back_ref, a_ref):
    second = owner_ref[...].astype(F32)
    r_from = lax.broadcasted_iota(jnp.int32, (ROWS, ROWS), 0)
    r_to = lax.broadcasted_iota(jnp.int32, (ROWS, ROWS), 1)
    upper = jnp.where(r_from <= r_to, 1.0, 0.0).astype(BF16)
    ones_before = mm(jnp.broadcast_to(second, (8, ROWS)).astype(BF16), upper)[:1]
    index = lax.broadcasted_iota(jnp.int32, (1, ROWS), 1).astype(F32)
    n_first = ROWS - jnp.sum(second, axis=1, keepdims=True)
    place = jnp.where(second > 0.5, n_first + ones_before - 1.0, index - ones_before)
    onehot = jnp.where(r_from == place.astype(jnp.int32), 1.0, 0.0)
    back_ref[...] = onehot.T.astype(BF16)
    onehot = onehot.astype(BF16)
    x = layer_norm(feats_ref[...].astype(F32)).astype(BF16)
    xs_ref[...] = mm(onehot, x).astype(BF16)

    @pl.loop(0, D // GROUP)
    def _(g):
        cols = lambda n: pl.ds(pl.multiple_of(n * D + g * GROUP, GROUP), GROUP)
        u, v, q, k = (silu(mm(xs_ref[...], w_ref[:, cols(n)])).astype(BF16) for n in range(4))
        u_ref[:, cols(0)] = u
        q_ref[:, cols(0)] = q
        prod = q.astype(F32) * k.astype(F32)
        for h in range(GROUP // HD):
            hc = slice(h * HD, (h + 1) * HD)
            half = jnp.sum(prod[:, hc], axis=-1, keepdims=True) * HALF_SCALE
            own = (half + half * jnp.tanh(half)).astype(BF16).astype(F32)
            out_cols = pl.ds(pl.multiple_of(g * GROUP + h * HD, HD), HD)
            a_ref[:, out_cols] = own * v[:, hc].astype(F32)


def cand_project(owner_row, feats, w_in):
    rows = jax.ShapeDtypeStruct((ROWS, D), BF16)
    out_shape = [rows, rows, rows, jax.ShapeDtypeStruct((ROWS, ROWS), BF16), jax.ShapeDtypeStruct((ROWS, D), F32)]
    return kernel_call(cand_kernel, "cand_project", [owner_row, feats, w_in], out_shape, [])


def absorb_kernel(plan, scal_ref, *refs):
    pieces, first, final = plan
    count = len(pieces)
    refs = list(refs)
    take = lambda n: [refs.pop(0) for _ in range(n)]
    x_refs = take(count)
    w_ref, q_ref, a_ref = take(3)
    if not first:
        qh_ref, ah_ref = take(2)
    if final:
        uh_ref, own_ref, u_ref, xs_ref, back_ref, wo_ref, hist_ref, cand_ref = take(8)
    elif first:
        _, ah_ref, qh_ref, uh_ref = take(4)
    else:
        take(2)
    k_scr, v_scr = take(2)
    row_iota = lax.broadcasted_iota(jnp.int32, (SLOTS, 1), 0)
    ahead = lax.broadcasted_iota(jnp.int32, (SLOTS, SLOTS), 0) - lax.broadcasted_iota(
        jnp.int32, (SLOTS, SLOTS), 1
    )
    offs = [scal_ref[0, 4 + piece] for piece in pieces]
    my_off = scal_ref[0, 3]

    steps = D // GROUP

    def column(n, g):
        return slice(n * D + g * GROUP, n * D + (g + 1) * GROUP)

    def project(g, n):
        x = x_refs[n][...].reshape(2 * SLOTS, D)
        if first and n == 0:
            qh_ref[:, column(0, g)] = silu(mm(x, w_ref[:, column(2, g)])).astype(BF16)
            uh_ref[:, column(0, g)] = silu(mm(x, w_ref[:, column(0, g)])).astype(BF16)
        k = silu(mm(x, w_ref[:, column(3, g)])).astype(BF16)
        v = silu(mm(x, w_ref[:, column(1, g)])).astype(BF16)
        to = slice(n * SLOTS, (n + 1) * SLOTS)
        for user in (0, 1):
            at = slice(user * SLOTS, (user + 1) * SLOTS)
            live = row_iota < scal_ref[user, 0] - offs[n]
            k_scr[g % 2, user, to, :] = k[at]
            v_scr[g % 2, user, to, :] = jnp.where(live, v[at], jnp.zeros_like(v[at]))

    def attend(g, user, h, turn):
        row_lo, row_hi = scal_ref[user, 1], scal_ref[user, 2]
        covered = starts[user] + WINDOW
        start = pl.multiple_of(jnp.where(turn == 0, starts[user], ROWS - WINDOW), 16)
        rows = pl.ds(start, WINDOW)
        index = start + lax.broadcasted_iota(jnp.int32, (WINDOW, 1), 0)
        mine = (index >= jnp.where(turn == 0, row_lo, covered)) & (index < row_hi)
        mine_rows = slice(user * SLOTS, (user + 1) * SLOTS)
        hc = slice(h * HD, (h + 1) * HD)
        oc = slice(g * GROUP + h * HD, g * GROUP + (h + 1) * HD)
        q = jnp.concatenate([q_ref[rows, oc], qh_ref[mine_rows, oc]], axis=0)
        w = weights_of(q, k_scr[g % 2, user, :, hc])
        parts = []
        for n in range(count):
            part = w[WINDOW:, n * SLOTS : (n + 1) * SLOTS]
            seen = ahead >= offs[n] - my_off + turn * HIDE
            parts.append(jnp.where(seen, part, jnp.zeros_like(part)).astype(BF16))
        w = jnp.concatenate([w[:WINDOW].astype(BF16), jnp.concatenate(parts, axis=1)], axis=0)
        total = mm(w, v_scr[g % 2, user, :, hc])
        a_ref[rows, oc] += jnp.where(mine, total[:WINDOW], 0.0)
        ah_ref[mine_rows, oc] += total[WINDOW:]

    if first:
        ah_ref[...] = jnp.zeros((2 * SLOTS, D), F32)
    starts = [jnp.minimum((scal_ref[user, 1] // 16) * 16, ROWS - WINDOW) for user in (0, 1)]
    fits = [scal_ref[user, 2] <= starts[user] + WINDOW for user in (0, 1)]
    turns = jnp.where(fits[0] & fits[1], 1, 2)
    pairs = [(user, h) for user in (0, 1) for h in range(GROUP // HD)]

    @pl.loop(0, turns)
    def _(turn):
        for n in range(count):
            project(0, n)
        for g in range(steps):
            left = list(range(count)) if g + 1 < steps else []
            gap = max(1, len(pairs) // max(1, len(left)))
            for i, (user, h) in enumerate(pairs):
                if left and i % gap == 0:
                    project(g + 1, left.pop(0))
                attend(g, user, h, turn)
            for n in left:
                project(g + 1, n)

    if final:
        (y_scr,) = take(1)
        n_hist = 2 * SLOTS
        y = layer_norm(ah_ref[...]) * uh_ref[...].astype(F32)
        y_scr[:n_hist, :] = y.astype(BF16)

        @pl.loop(0, ROWS // SLOTS)
        def _(n):
            rows = pl.ds(pl.multiple_of(n * SLOTS, SLOTS), SLOTS)
            y = layer_norm(a_ref[rows, :]) * u_ref[rows, :].astype(F32)
            y_scr[pl.ds(pl.multiple_of(n_hist + n * SLOTS, SLOTS), SLOTS), :] = y.astype(BF16)

        @pl.loop(0, D // GROUP)
        def _(g):
            cols = pl.ds(pl.multiple_of(g * GROUP, GROUP), GROUP)
            res = mm(y_scr[...], wo_ref[:, cols])
            for user in (0, 1):
                out = res[user * SLOTS : (user + 1) * SLOTS] + own_ref[user, :, cols].astype(F32)
                keep = my_off + row_iota < scal_ref[user, 0]
                hist_ref[user, :, cols] = jnp.where(keep, out, 0.0).astype(BF16)
            done = (res[n_hist:] + xs_ref[:, cols].astype(F32)).astype(BF16)
            cand_ref[:, cols] = mm(back_ref[...], done).astype(BF16)


def absorb(name, scal, items, w_in, q_cand, a_cand, state=None, final=None):
    pieces = tuple(item[0] for item in items)
    arrays = [item[1] for item in items] + [w_in, q_cand, a_cand]
    a_at = len(arrays)
    scratch = [pltpu.VMEM((2, 2, len(pieces) * SLOTS, GROUP), BF16)] * 2
    sums = jax.ShapeDtypeStruct((2 * SLOTS, D), F32)
    rows = jax.ShapeDtypeStruct((2 * SLOTS, D), BF16)
    out_shape = [jax.ShapeDtypeStruct((ROWS, D), F32), sums]
    aliases = {a_at: 0}
    first = state is None
    if first:
        out_shape += [rows, rows]
    else:
        arrays += [state[0], state[2]]
        aliases[a_at + 2] = 1
    if final is not None:
        arrays += [state[1]] + list(final)
        out_shape = [jax.ShapeDtypeStruct((2, SLOTS, D), BF16), jax.ShapeDtypeStruct((ROWS, D), BF16)]
        aliases = {}
        scratch.append(pltpu.VMEM((2 * SLOTS + ROWS, D), BF16))
    outs = kernel_call(
        functools.partial(absorb_kernel, (pieces, first, final is not None)),
        name,
        arrays,
        out_shape,
        scratch,
        scal,
        aliases,
    )
    if final is not None:
        return outs
    return outs[0], (outs[2], outs[3], outs[1]) if first else (state[0], state[1], outs[1])


def user_perm(dx, dy, dcore):
    pairs = []
    for u in range(4 * NX):
        x, y, core = u >> 2, (u >> 1) & 1, u & 1
        pairs.append((u, (((x + dx) % NX) * 2 + (y ^ dy)) * 2 + (core ^ dcore)))
    return pairs


def cand_perm(dz, dy):
    return [(c, (((c >> 1) + dz) % NZ) * 2 + ((c & 1) ^ dy)) for c in range(2 * NZ)]


def to_user(array, dx, dy, dcore):
    return lax.ppermute(array, "user", user_perm(dx, dy, dcore))


def to_cand(array, dz, dy):
    return lax.ppermute(array, "cand", cand_perm(dz, dy))


def local(pooled, cand_feats, hist_len, cand_user, w_in, w_out):
    user = lax.axis_index("user")
    cand = lax.axis_index("cand")
    x, y, core = user >> 2, (user >> 1) & 1, user & 1
    z, y_hi = cand >> 1, cand & 1
    owner = cand_user - 2 * user
    n_first = ROWS - jnp.sum(owner)
    offsets = [SLOTS * (((z + dz + NZ) % NZ) * 2 + (y_hi ^ e)) for dz in SHIFTS for e in range(2)]
    scal = jnp.stack(
        [
            jnp.stack([hist_len[0], 0 * user, n_first, cand * SLOTS] + offsets),
            jnp.stack([hist_len[1], n_first, 0 * user + ROWS, cand * SLOTS] + offsets),
        ]
    ).astype(jnp.int32)

    tables = pooled.reshape(NX, 2, 2, 2, SLOTS, D)
    place = jnp.stack([x, y, core]).astype(jnp.int32)
    with jax.named_scope("sum_core"):
        pack1 = pack(place, tables)
        got1 = to_user(pack1, 0, 0, 1)
        pack0 = pack_all(place, after(tables, pack1))
        got0 = [to_user(part, 0, 0, 1) for part in pack0]
    with jax.named_scope("sum_y_second"):
        over1 = over_y(place, tables, after(got1, pack0))
        y1 = to_user(over1, 0, 1, 0)
    with jax.named_scope("sum_x_first"):
        *away0, pack2 = away_x(place, tables, after(got0, over1))
        x0 = [to_user(part, d, 0, 0) for part, d in zip(away0, HOPS)]
    with jax.named_scope("sum_core"):
        got2 = to_user(pack2, 0, 0, 1)
    owner_row, scal = after((owner.reshape(1, ROWS), scal), pack2)
    xs, u_cand, q_cand, back, a_cand = cand_project(owner_row, cand_feats, w_in)
    with jax.named_scope("sum_y_second"):
        y1 = after(y1, xs, scal)
        away1 = join_y(place, tables, got2, y1)
        x1 = [to_user(part, d, 0, 0) for part, d in zip(away1, HOPS)]
    with jax.named_scope("sum_x_first"):
        mine0, over0 = join_x(place, tables, got0, after(x0, away1))
        y0 = to_user(over0, 0, 1, 0)
    with jax.named_scope("gather"):
        own1 = norm_sum(place, tables, got2, y1, after(x1, mine0))
        own = norm_both(place, [mine0, after(y0, own1)], own1)
        near = to_cand(own, 0, 1)
        own_left, own_right = to_cand(own, 1, 0), to_cand(own, -1, 0)
    put = functools.partial(absorb, scal=scal, w_in=w_in, q_cand=q_cand)
    piece = lambda shift, e: 2 * SHIFTS.index(shift) + e
    a_cand, state = put("own_keys", items=[(piece(0, 0), own)], a_cand=a_cand)
    with jax.named_scope("gather"):
        near = after(near, a_cand)
        near_left, near_right = to_cand(near, 1, 0), to_cand(near, -1, 0)
        own_left, own_right = after((own_left, own_right), near)
        own_far = to_cand(own_left, 1, 0)
    a_cand, state = put(
        "own_sides",
        items=[(piece(-1, 0), own_left), (piece(1, 0), own_right), (piece(0, 1), near)],
        a_cand=a_cand,
        state=state,
    )
    with jax.named_scope("gather"):
        near_left, near_right = after((near_left, near_right), a_cand)
        near_far = to_cand(near_right, -1, 0)
    a_cand, state = put(
        "near_sides",
        items=[(piece(-1, 1), near_left), (piece(1, 1), near_right)],
        a_cand=a_cand,
        state=state,
    )
    return put(
        "far_finish",
        items=[(piece(2, 0), own_far), (piece(2, 1), near_far)],
        a_cand=a_cand,
        state=state,
        final=(own, u_cand, xs, back, w_out),
    )


def solution(mesh):
    placed = (
        P("user", None, "cand", None),
        P(("user", "cand"), None),
        P("user"),
        P(("user", "cand")),
        P(),
        P(),
    )
    return jax.shard_map(
        local,
        mesh=mesh,
        in_specs=placed,
        out_specs=(P("user", "cand", None), P(("user", "cand"), None)),
        check_vma=False,
    )
```

```python
import functools

import jax
import jax.numpy as jnp
from jax import lax
from jax.experimental import pallas as pl
from jax.experimental.pallas import tpu as pltpu
from jax.sharding import PartitionSpec as P

F32 = jnp.float32
BF16 = jnp.bfloat16
HEADS = 8
HD = 128
D = 1024
SLOTS = 128
ROWS = 512
NX, NZ = 4, 4
WINDOW = 320
HALF_SCALE = 0.5 / (HD**0.5)
VMEM = 20 * 1024 * 1024
GROUP = 512
SHIFTS = (0, -1, 1, 2)
HIDE = 1 << 16
HOPS = (1, 3, 2)
SIDES = (lambda s: s[1], lambda s: 1 - s[1])


def silu(v):
    half = v * 0.5
    half = half.astype(BF16)
    return half + half * jnp.tanh(half)


def layer_norm(rows):
    mean = jnp.mean(rows, axis=-1, keepdims=True)
    centered = rows - mean
    var = jnp.mean(centered * centered, axis=-1, keepdims=True)
    return centered * lax.rsqrt(var + 1e-05)


def mm(a, b):
    return jnp.dot(a, b, preferred_element_type=F32)


def weights_of(queries, keys):
    s = lax.dot_general(queries, keys, (((1,), (1,)), ((), ())), preferred_element_type=F32)
    half = (s * HALF_SCALE).astype(BF16)
    return half + half * jnp.tanh(half)


def after(value, *others):
    return lax.optimization_barrier((value, others))[0]


def in_hbm(array):
    return pltpu.with_memory_space_constraint(array, pltpu.HBM)


def cost():
    return pl.CostEstimate(flops=10**6, bytes_accessed=1 << 16, transcendentals=0)


def block_sums(name, scal, arrays, shapes, sums):
    added = [part for _, _, parts, _ in sums if len(parts) > 1 for part in parts]
    n_loads = sum(len(parts) for _, _, parts, _ in sums)

    def body(scal_ref, *refs):
        ins, refs = refs[: len(arrays)], refs[len(arrays) :]
        outs, refs = refs[: len(shapes)], refs[len(shapes) :]
        bufs, in_sems = list(refs[: len(added)]), refs[len(added)]
        work, count = [], 0
        for out, lead, parts, norm in sums:
            lead = (lead(scal_ref),) if callable(lead) else lead
            dst = outs[out].at[lead] if lead else outs[out]
            copies, held = [], []
            for at, index in parts:
                from_ = index(scal_ref)
                src = ins[at].at[from_] if from_ else ins[at]
                to = bufs.pop(0) if len(parts) > 1 else dst
                copies.append(pltpu.make_async_copy(src, to, in_sems.at[count]))
                copies[-1].start()
                held.append(to)
                count += 1
            work.append((dst, copies, held, norm))
        for dst, copies, held, norm in work:
            for copy in copies:
                copy.wait()
            if len(held) > 1:
                step = SLOTS if norm else SLOTS // 2

                @pl.loop(0, SLOTS // step)
                def _(r):
                    rows = pl.ds(pl.multiple_of(r * step, step), step)
                    total = None
                    for ref in held:
                        value = ref[rows, :].astype(F32)
                        total = value if total is None else total + value
                    dst[rows, :] = (layer_norm(total) if norm else total).astype(dst.dtype)

    hbm, anywhere = pl.BlockSpec(memory_space=pltpu.HBM), pl.BlockSpec(memory_space=pl.ANY)
    return pl.pallas_call(
        body,
        in_specs=[pl.BlockSpec(memory_space=pltpu.SMEM)]
        + [hbm if a.ndim == 6 else anywhere for a in arrays],
        out_specs=[pl.BlockSpec(memory_space=pltpu.VMEM)] * len(shapes),
        out_shape=[jax.ShapeDtypeStruct(shape, dtype) for shape, dtype in shapes],
        scratch_shapes=[pltpu.VMEM((SLOTS, D), arrays[at].dtype) for at, _ in added]
        + [pltpu.SemaphoreType.DMA((n_loads,))],
        compiler_params=pltpu.CompilerParams(vmem_limit_bytes=VMEM),
        cost_estimate=cost(),
        name=name,
    )(scal, *(in_hbm(a) if a.ndim == 6 else a for a in arrays))


def pack(place, tables):
    sums = [(0, (x,), [(0, lambda s, x=x: (x, 1 - s[1], 1 - s[2], 1))], False) for x in range(NX)]
    return block_sums("pack", place, [tables], [((NX, SLOTS, D), BF16)], sums)[0]


def pack_all(place, tables):
    sums = [
        (n, (x,), [(0, lambda s, x=x, side=side: (x, side(s), 1 - s[2], 0))], False)
        for x in range(NX)
        for n, side in enumerate(SIDES)
    ]
    return block_sums("pack_all", place, [tables], [((NX, SLOTS, D), BF16)] * 2, sums)


def over_y(place, tables, got):
    sums = [
        (0, (x,), [(0, lambda s, x=x: (x, 1 - s[1], s[2], 1)), (1, lambda s, x=x: (x,))], False)
        for x in range(NX)
    ]
    return block_sums("over_y", place, [tables, got], [((NX, SLOTS, D), BF16)], sums)[0]


def away_x(place, tables, got):
    sums = []
    for n, d in enumerate(HOPS):
        for m, side in enumerate(SIDES):
            at = lambda s, d=d: lax.rem(s[0] + d, NX)
            parts = [
                (0, lambda s, at=at, side=side: (at(s), side(s), s[2], 0)),
                (1 + m, lambda s, at=at: (at(s),)),
            ]
            sums.append((n, side, parts, False))
    for n in range(NX):
        sums.append((3, (n,), [(0, lambda s, n=n: (n, s[1], 1 - s[2], 1))], False))
    shapes = [((2, SLOTS, D), BF16)] * 3 + [((NX, SLOTS, D), BF16)]
    return block_sums("away_x", place, [tables] + list(got), shapes, sums)


def join_x(place, tables, got, arrived):
    arrays = [tables] + list(got) + list(arrived)
    sums = []
    for n in (1, 0):
        side = SIDES[n]
        parts = [(0, lambda s, side=side: (s[0], side(s), s[2], 0)), (1 + n, lambda s: (s[0],))]
        parts += [(3 + k, lambda s, side=side: (side(s),)) for k in range(3)]
        sums.append((n, (), parts, False))
    return block_sums("join_x", place, arrays, [((SLOTS, D), F32), ((SLOTS, D), BF16)], sums)


def join_y(place, tables, got, arrived):
    sums = []
    for n, d in enumerate(HOPS):
        at = lambda s, d=d: lax.rem(s[0] + d, NX)
        parts = [
            (0, lambda s, at=at: (at(s), s[1], s[2], 1)),
            (1, lambda s, at=at: (at(s),)),
            (2, lambda s, at=at: (at(s),)),
        ]
        sums.append((n, (), parts, False))
    return block_sums("join_y", place, [tables, got, arrived], [((SLOTS, D), BF16)] * 3, sums)


def norm_sum(place, tables, got, side, arrived):
    parts = [
        (0, lambda s: (s[0], s[1], s[2], 1)),
        (1, lambda s: (s[0],)),
        (2, lambda s: (s[0],)),
    ] + [(3 + n, lambda s: ()) for n in range(3)]
    arrays = [tables, got, side] + list(arrived)
    return block_sums("norm_sum", place, arrays, [((SLOTS, D), BF16)], [(0, (), parts, True)])[0]


def norm_both(place, first, second):
    parts = [(n, lambda s: ()) for n in range(len(first) + 1)]
    sums = [(0, (1,), parts[-1:], False), (0, (0,), parts[:-1], True)]
    return block_sums("norm_both", place, list(first) + [second], [((2, SLOTS, D), BF16)], sums)[0]


def in_vmem(array):
    return pltpu.with_memory_space_constraint(array, pltpu.VMEM)


def kernel_call(body, name, arrays, out_shape, scratch, scalars=None, aliases=None):
    vmem = pl.BlockSpec(memory_space=pltpu.VMEM)
    in_specs, args = [vmem] * len(arrays), [in_vmem(array) for array in arrays]
    if scalars is not None:
        in_specs = [pl.BlockSpec(memory_space=pltpu.SMEM)] + in_specs
        args = [scalars] + args
    return pl.pallas_call(
        body,
        in_specs=in_specs,
        out_specs=[vmem] * len(out_shape),
        out_shape=out_shape,
        scratch_shapes=scratch,
        input_output_aliases=aliases or {},
        compiler_params=pltpu.CompilerParams(vmem_limit_bytes=VMEM),
        cost_estimate=cost(),
        name=name,
    )(*args)


def cand_kernel(owner_ref, feats_ref, w_ref, xs_ref, u_ref, q_ref, back_ref, a_ref):
    second = owner_ref[...].astype(F32)
    r_from = lax.broadcasted_iota(jnp.int32, (ROWS, ROWS), 0)
    r_to = lax.broadcasted_iota(jnp.int32, (ROWS, ROWS), 1)
    upper = jnp.where(r_from <= r_to, 1.0, 0.0).astype(BF16)
    ones_before = mm(jnp.broadcast_to(second, (8, ROWS)).astype(BF16), upper)[:1]
    index = lax.broadcasted_iota(jnp.int32, (1, ROWS), 1).astype(F32)
    n_first = ROWS - jnp.sum(second, axis=1, keepdims=True)
    place = jnp.where(second > 0.5, n_first + ones_before - 1.0, index - ones_before)
    onehot = jnp.where(r_from == place.astype(jnp.int32), 1.0, 0.0)
    back_ref[...] = onehot.T.astype(BF16)
    onehot = onehot.astype(BF16)
    x = layer_norm(feats_ref[...].astype(F32)).astype(BF16)
    xs_ref[...] = mm(onehot, x).astype(BF16)

    @pl.loop(0, D // GROUP)
    def _(g):
        cols = lambda n: pl.ds(pl.multiple_of(n * D + g * GROUP, GROUP), GROUP)
        u, v, q, k = (silu(mm(xs_ref[...], w_ref[:, cols(n)])).astype(BF16) for n in range(4))
        u_ref[:, cols(0)] = u
        q_ref[:, cols(0)] = q
        prod = q.astype(F32) * k.astype(F32)
        for h in range(GROUP // HD):
            hc = slice(h * HD, (h + 1) * HD)
            half = jnp.sum(prod[:, hc], axis=-1, keepdims=True) * HALF_SCALE
            own = (half + half * jnp.tanh(half)).astype(BF16).astype(F32)
            out_cols = pl.ds(pl.multiple_of(g * GROUP + h * HD, HD), HD)
            a_ref[:, out_cols] = own * v[:, hc].astype(F32)


def cand_project(owner_row, feats, w_in):
    rows = jax.ShapeDtypeStruct((ROWS, D), BF16)
    out_shape = [rows, rows, rows, jax.ShapeDtypeStruct((ROWS, ROWS), BF16), jax.ShapeDtypeStruct((ROWS, D), F32)]
    return kernel_call(cand_kernel, "cand_project", [owner_row, feats, w_in], out_shape, [])


def absorb_kernel(plan, scal_ref, *refs):
    pieces, first, final = plan
    count = len(pieces)
    refs = list(refs)
    take = lambda n: [refs.pop(0) for _ in range(n)]
    x_refs = take(count)
    w_ref, q_ref, a_ref = take(3)
    if not first:
        qh_ref, ah_ref = take(2)
    if final:
        uh_ref, own_ref, u_ref, xs_ref, back_ref, wo_ref, hist_ref, cand_ref = take(8)
    elif first:
        _, ah_ref, qh_ref, uh_ref = take(4)
    else:
        take(2)
    k_scr, v_scr = take(2)
    row_iota = lax.broadcasted_iota(jnp.int32, (SLOTS, 1), 0)
    ahead = lax.broadcasted_iota(jnp.int32, (SLOTS, SLOTS), 0) - lax.broadcasted_iota(
        jnp.int32, (SLOTS, SLOTS), 1
    )
    offs = [scal_ref[0, 4 + piece] for piece in pieces]
    my_off = scal_ref[0, 3]

    steps = D // GROUP

    def column(n, g):
        return slice(n * D + g * GROUP, n * D + (g + 1) * GROUP)

    def project(g, n):
        x = x_refs[n][...].reshape(2 * SLOTS, D)
        if first and n == 0:
            qh_ref[:, column(0, g)] = silu(mm(x, w_ref[:, column(2, g)])).astype(BF16)
            uh_ref[:, column(0, g)] = silu(mm(x, w_ref[:, column(0, g)])).astype(BF16)
        k = silu(mm(x, w_ref[:, column(3, g)])).astype(BF16)
        v = silu(mm(x, w_ref[:, column(1, g)])).astype(BF16)
        to = slice(n * SLOTS, (n + 1) * SLOTS)
        for user in (0, 1):
            at = slice(user * SLOTS, (user + 1) * SLOTS)
            live = row_iota < scal_ref[user, 0] - offs[n]
            k_scr[g % 2, user, to, :] = k[at]
            v_scr[g % 2, user, to, :] = jnp.where(live, v[at], jnp.zeros_like(v[at]))

    def attend(g, user, h, turn):
        row_lo, row_hi = scal_ref[user, 1], scal_ref[user, 2]
        covered = starts[user] + WINDOW
        start = pl.multiple_of(jnp.where(turn == 0, starts[user], ROWS - WINDOW), 16)
        rows = pl.ds(start, WINDOW)
        index = start + lax.broadcasted_iota(jnp.int32, (WINDOW, 1), 0)
        mine = (index >= jnp.where(turn == 0, row_lo, covered)) & (index < row_hi)
        mine_rows = slice(user * SLOTS, (user + 1) * SLOTS)
        hc = slice(h * HD, (h + 1) * HD)
        oc = slice(g * GROUP + h * HD, g * GROUP + (h + 1) * HD)
        q = jnp.concatenate([q_ref[rows, oc], qh_ref[mine_rows, oc]], axis=0)
        w = weights_of(q, k_scr[g % 2, user, :, hc])
        parts = []
        for n in range(count):
            part = w[WINDOW:, n * SLOTS : (n + 1) * SLOTS]
            seen = ahead >= offs[n] - my_off + turn * HIDE
            parts.append(jnp.where(seen, part, jnp.zeros_like(part)).astype(BF16))
        w = jnp.concatenate([w[:WINDOW].astype(BF16), jnp.concatenate(parts, axis=1)], axis=0)
        total = mm(w, v_scr[g % 2, user, :, hc])
        a_ref[rows, oc] += jnp.where(mine, total[:WINDOW], 0.0)
        ah_ref[mine_rows, oc] += total[WINDOW:]

    if first:
        ah_ref[...] = jnp.zeros((2 * SLOTS, D), F32)
    starts = [jnp.minimum((scal_ref[user, 1] // 16) * 16, ROWS - WINDOW) for user in (0, 1)]
    fits = [scal_ref[user, 2] <= starts[user] + WINDOW for user in (0, 1)]
    turns = jnp.where(fits[0] & fits[1], 1, 2)
    pairs = [(user, h) for user in (0, 1) for h in range(GROUP // HD)]

    @pl.loop(0, turns)
    def _(turn):
        for n in range(count):
            project(0, n)
        for g in range(steps):
            left = list(range(count)) if g + 1 < steps else []
            gap = max(1, len(pairs) // max(1, len(left)))
            for i, (user, h) in enumerate(pairs):
                if left and i % gap == 0:
                    project(g + 1, left.pop(0))
                attend(g, user, h, turn)
            for n in left:
                project(g + 1, n)

    if final:
        (y_scr,) = take(1)
        n_hist = 2 * SLOTS
        y = layer_norm(ah_ref[...]) * uh_ref[...].astype(F32)
        y_scr[:n_hist, :] = y.astype(BF16)

        @pl.loop(0, ROWS // SLOTS)
        def _(n):
            rows = pl.ds(pl.multiple_of(n * SLOTS, SLOTS), SLOTS)
            y = layer_norm(a_ref[rows, :]) * u_ref[rows, :].astype(F32)
            y_scr[pl.ds(pl.multiple_of(n_hist + n * SLOTS, SLOTS), SLOTS), :] = y.astype(BF16)

        @pl.loop(0, D // GROUP)
        def _(g):
            cols = pl.ds(pl.multiple_of(g * GROUP, GROUP), GROUP)
            res = mm(y_scr[...], wo_ref[:, cols])
            for user in (0, 1):
                out = res[user * SLOTS : (user + 1) * SLOTS] + own_ref[user, :, cols].astype(F32)
                keep = my_off + row_iota < scal_ref[user, 0]
                hist_ref[user, :, cols] = jnp.where(keep, out, 0.0).astype(BF16)
            done = (res[n_hist:] + xs_ref[:, cols].astype(F32)).astype(BF16)
            cand_ref[:, cols] = mm(back_ref[...], done).astype(BF16)


def absorb(name, scal, items, w_in, q_cand, a_cand, state=None, final=None):
    pieces = tuple(item[0] for item in items)
    arrays = [item[1] for item in items] + [w_in, q_cand, a_cand]
    a_at = len(arrays)
    scratch = [pltpu.VMEM((2, 2, len(pieces) * SLOTS, GROUP), BF16)] * 2
    sums = jax.ShapeDtypeStruct((2 * SLOTS, D), F32)
    rows = jax.ShapeDtypeStruct((2 * SLOTS, D), BF16)
    out_shape = [jax.ShapeDtypeStruct((ROWS, D), F32), sums]
    aliases = {a_at: 0}
    first = state is None
    if first:
        out_shape += [rows, rows]
    else:
        arrays += [state[0], state[2]]
        aliases[a_at + 2] = 1
    if final is not None:
        arrays += [state[1]] + list(final)
        out_shape = [jax.ShapeDtypeStruct((2, SLOTS, D), BF16), jax.ShapeDtypeStruct((ROWS, D), BF16)]
        aliases = {}
        scratch.append(pltpu.VMEM((2 * SLOTS + ROWS, D), BF16))
    outs = kernel_call(
        functools.partial(absorb_kernel, (pieces, first, final is not None)),
        name,
        arrays,
        out_shape,
        scratch,
        scal,
        aliases,
    )
    if final is not None:
        return outs
    return outs[0], (outs[2], outs[3], outs[1]) if first else (state[0], state[1], outs[1])


def user_perm(dx, dy, dcore):
    pairs = []
    for u in range(4 * NX):
        x, y, core = u >> 2, (u >> 1) & 1, u & 1
        pairs.append((u, (((x + dx) % NX) * 2 + (y ^ dy)) * 2 + (core ^ dcore)))
    return pairs


def cand_perm(dz, dy):
    return [(c, (((c >> 1) + dz) % NZ) * 2 + ((c & 1) ^ dy)) for c in range(2 * NZ)]


def to_user(array, dx, dy, dcore):
    return lax.ppermute(array, "user", user_perm(dx, dy, dcore))


def to_cand(array, dz, dy):
    return lax.ppermute(array, "cand", cand_perm(dz, dy))


def local(pooled, cand_feats, hist_len, cand_user, w_in, w_out):
    user = lax.axis_index("user")
    cand = lax.axis_index("cand")
    x, y, core = user >> 2, (user >> 1) & 1, user & 1
    z, y_hi = cand >> 1, cand & 1
    owner = cand_user - 2 * user
    n_first = ROWS - jnp.sum(owner)
    offsets = [SLOTS * (((z + dz + NZ) % NZ) * 2 + (y_hi ^ e)) for dz in SHIFTS for e in range(2)]
    scal = jnp.stack(
        [
            jnp.stack([hist_len[0], 0 * user, n_first, cand * SLOTS] + offsets),
            jnp.stack([hist_len[1], n_first, 0 * user + ROWS, cand * SLOTS] + offsets),
        ]
    ).astype(jnp.int32)

    tables = pooled.reshape(NX, 2, 2, 2, SLOTS, D)
    place = jnp.stack([x, y, core]).astype(jnp.int32)
    with jax.named_scope("sum_core"):
        pack1 = pack(place, tables)
        got1 = to_user(pack1, 0, 0, 1)
        pack0 = pack_all(place, after(tables, pack1))
        got0 = [to_user(part, 0, 0, 1) for part in pack0]
    with jax.named_scope("sum_y_second"):
        over1 = over_y(place, tables, after(got1, pack0))
        y1 = to_user(over1, 0, 1, 0)
    with jax.named_scope("sum_x_first"):
        *away0, pack2 = away_x(place, tables, after(got0, over1))
        x0 = [to_user(part, d, 0, 0) for part, d in zip(away0, HOPS)]
    with jax.named_scope("sum_core"):
        got2 = to_user(pack2, 0, 0, 1)
    owner_row, scal = after((owner.reshape(1, ROWS), scal), pack2)
    xs, u_cand, q_cand, back, a_cand = cand_project(owner_row, cand_feats, w_in)
    with jax.named_scope("sum_y_second"):
        y1 = after(y1, xs, scal)
        away1 = join_y(place, tables, got2, y1)
        x1 = [to_user(part, d, 0, 0) for part, d in zip(away1, HOPS)]
    with jax.named_scope("sum_x_first"):
        mine0, over0 = join_x(place, tables, got0, after(x0, away1))
        y0 = to_user(over0, 0, 1, 0)
    with jax.named_scope("gather"):
        own1 = norm_sum(place, tables, got2, y1, after(x1, mine0))
        own = norm_both(place, [mine0, after(y0, own1)], own1)
        near = to_cand(own, 0, 1)
        own_left, own_right = to_cand(own, 1, 0), to_cand(own, -1, 0)
    put = functools.partial(absorb, scal=scal, w_in=w_in, q_cand=q_cand)
    piece = lambda shift, e: 2 * SHIFTS.index(shift) + e
    a_cand, state = put("own_keys", items=[(piece(0, 0), own)], a_cand=a_cand)
    with jax.named_scope("gather"):
        near = after(near, a_cand)
        near_left, near_right = to_cand(near, 1, 0), to_cand(near, -1, 0)
        own_left, own_right = after((own_left, own_right), near)
        own_far = to_cand(own_left, 1, 0)
    a_cand, state = put(
        "own_sides",
        items=[(piece(-1, 0), own_left), (piece(1, 0), own_right), (piece(0, 1), near)],
        a_cand=a_cand,
        state=state,
    )
    with jax.named_scope("gather"):
        near_left, near_right = after((near_left, near_right), a_cand)
        near_far = to_cand(near_right, -1, 0)
    a_cand, state = put(
        "near_sides",
        items=[(piece(-1, 1), near_left), (piece(1, 1), near_right)],
        a_cand=a_cand,
        state=state,
    )
    return put(
        "far_finish",
        items=[(piece(2, 0), own_far), (piece(2, 1), near_far)],
        a_cand=a_cand,
        state=state,
        final=(own, u_cand, xs, back, w_out),
    )


def solution(mesh):
    placed = (
        P("user", None, "cand", None),
        P(("user", "cand"), None),
        P("user"),
        P(("user", "cand")),
        P(),
        P(),
    )
    return jax.shard_map(
        local,
        mesh=mesh,
        in_specs=placed,
        out_specs=(P("user", "cand", None), P(("user", "cand"), None)),
        check_vma=False,
    )
```

```python
import functools

import jax
import jax.numpy as jnp
from jax import lax
from jax.experimental import pallas as pl
from jax.experimental.pallas import tpu as pltpu
from jax.sharding import PartitionSpec as P

F32 = jnp.float32
BF16 = jnp.bfloat16
HEADS = 8
HD = 128
D = 1024
SLOTS = 128
ROWS = 512
NX, NZ = 4, 4
WINDOW = 320
HALF_SCALE = 0.5 / (HD**0.5)
VMEM = 20 * 1024 * 1024
GROUP = 512
SHIFTS = (0, -1, 1, 2)
HIDE = 1 << 16
HOPS = (1, 3, 2)
SIDES = (lambda s: s[1], lambda s: 1 - s[1])


def silu(v):
    half = v * 0.5
    half = half.astype(BF16)
    return half + half * jnp.tanh(half)


def layer_norm(rows):
    mean = jnp.mean(rows, axis=-1, keepdims=True)
    centered = rows - mean
    var = jnp.mean(centered * centered, axis=-1, keepdims=True)
    return centered * lax.rsqrt(var + 1e-05)


def mm(a, b):
    return jnp.dot(a, b, preferred_element_type=F32)


def weights_of(queries, keys):
    s = lax.dot_general(queries, keys, (((1,), (1,)), ((), ())), preferred_element_type=F32)
    half = (s * HALF_SCALE).astype(BF16)
    return half + half * jnp.tanh(half)


def after(value, *others):
    return lax.optimization_barrier((value, others))[0]


def in_hbm(array):
    return pltpu.with_memory_space_constraint(array, pltpu.HBM)


def cost():
    return pl.CostEstimate(flops=10**6, bytes_accessed=1 << 16, transcendentals=0)


def block_sums(name, scal, arrays, shapes, sums):
    added = [part for _, _, parts, _ in sums if len(parts) > 1 for part in parts]
    n_loads = sum(len(parts) for _, _, parts, _ in sums)

    def body(scal_ref, *refs):
        ins, refs = refs[: len(arrays)], refs[len(arrays) :]
        outs, refs = refs[: len(shapes)], refs[len(shapes) :]
        bufs, in_sems = list(refs[: len(added)]), refs[len(added)]
        work, count = [], 0
        for out, lead, parts, norm in sums:
            lead = (lead(scal_ref),) if callable(lead) else lead
            dst = outs[out].at[lead] if lead else outs[out]
            copies, held = [], []
            for at, index in parts:
                from_ = index(scal_ref)
                src = ins[at].at[from_] if from_ else ins[at]
                to = bufs.pop(0) if len(parts) > 1 else dst
                copies.append(pltpu.make_async_copy(src, to, in_sems.at[count]))
                copies[-1].start()
                held.append(to)
                count += 1
            work.append((dst, copies, held, norm))
        for dst, copies, held, norm in work:
            for copy in copies:
                copy.wait()
            if len(held) > 1:
                step = SLOTS if norm else SLOTS // 2

                @pl.loop(0, SLOTS // step)
                def _(r):
                    rows = pl.ds(pl.multiple_of(r * step, step), step)
                    exact = len(held) == 2 and not norm and all(ref.dtype == BF16 for ref in held)
                    total = None
                    for ref in held:
                        value = ref[rows, :] if exact else ref[rows, :].astype(F32)
                        total = value if total is None else total + value
                    dst[rows, :] = (layer_norm(total) if norm else total).astype(dst.dtype)

    hbm, anywhere = pl.BlockSpec(memory_space=pltpu.HBM), pl.BlockSpec(memory_space=pl.ANY)
    return pl.pallas_call(
        body,
        in_specs=[pl.BlockSpec(memory_space=pltpu.SMEM)]
        + [hbm if a.ndim == 6 else anywhere for a in arrays],
        out_specs=[pl.BlockSpec(memory_space=pltpu.VMEM)] * len(shapes),
        out_shape=[jax.ShapeDtypeStruct(shape, dtype) for shape, dtype in shapes],
        scratch_shapes=[pltpu.VMEM((SLOTS, D), arrays[at].dtype) for at, _ in added]
        + [pltpu.SemaphoreType.DMA((n_loads,))],
        compiler_params=pltpu.CompilerParams(vmem_limit_bytes=VMEM),
        cost_estimate=cost(),
        name=name,
    )(scal, *(in_hbm(a) if a.ndim == 6 else a for a in arrays))


def pack(place, tables):
    sums = [(0, (x,), [(0, lambda s, x=x: (x, 1 - s[1], 1 - s[2], 1))], False) for x in range(NX)]
    return block_sums("pack", place, [tables], [((NX, SLOTS, D), BF16)], sums)[0]


def pack_all(place, tables):
    sums = [
        (n, (x,), [(0, lambda s, x=x, side=side: (x, side(s), 1 - s[2], 0))], False)
        for x in range(NX)
        for n, side in enumerate(SIDES)
    ]
    return block_sums("pack_all", place, [tables], [((NX, SLOTS, D), BF16)] * 2, sums)


def over_y(place, tables, got):
    sums = [
        (0, (x,), [(0, lambda s, x=x: (x, 1 - s[1], s[2], 1)), (1, lambda s, x=x: (x,))], False)
        for x in range(NX)
    ]
    return block_sums("over_y", place, [tables, got], [((NX, SLOTS, D), BF16)], sums)[0]


def away_x(place, tables, got):
    sums = []
    for n, d in enumerate(HOPS):
        for m, side in enumerate(SIDES):
            at = lambda s, d=d: lax.rem(s[0] + d, NX)
            parts = [
                (0, lambda s, at=at, side=side: (at(s), side(s), s[2], 0)),
                (1 + m, lambda s, at=at: (at(s),)),
            ]
            sums.append((n, side, parts, False))
    for n in range(NX):
        sums.append((3, (n,), [(0, lambda s, n=n: (n, s[1], 1 - s[2], 1))], False))
    shapes = [((2, SLOTS, D), BF16)] * 3 + [((NX, SLOTS, D), BF16)]
    return block_sums("away_x", place, [tables] + list(got), shapes, sums)


def join_x(place, tables, got, arrived, got1, side1):
    arrays = [tables] + list(got) + list(arrived) + [got1, side1]
    sums = []
    for n in (1, 0):
        side = SIDES[n]
        parts = [(0, lambda s, side=side: (s[0], side(s), s[2], 0)), (1 + n, lambda s: (s[0],))]
        parts += [(3 + k, lambda s, side=side: (side(s),)) for k in range(3)]
        sums.append((n, (), parts, False))
    parts = [(0, lambda s: (s[0], s[1], s[2], 1)), (6, lambda s: (s[0],)), (7, lambda s: (s[0],))]
    sums.append((2, (), parts, False))
    shapes = [((SLOTS, D), F32), ((SLOTS, D), BF16), ((SLOTS, D), F32)]
    return block_sums("join_x", place, arrays, shapes, sums)


def join_y(place, tables, got, arrived):
    sums = []
    for n, d in enumerate(HOPS):
        at = lambda s, d=d: lax.rem(s[0] + d, NX)
        parts = [
            (0, lambda s, at=at: (at(s), s[1], s[2], 1)),
            (1, lambda s, at=at: (at(s),)),
            (2, lambda s, at=at: (at(s),)),
        ]
        sums.append((n, (), parts, False))
    return block_sums("join_y", place, [tables, got, arrived], [((SLOTS, D), BF16)] * 3, sums)


def norm_sum(place, arrays):
    parts = [(n, lambda s: ()) for n in range(len(arrays))]
    return block_sums("norm_sum", place, arrays, [((SLOTS, D), BF16)], [(0, (), parts, True)])[0]


def norm_both(place, first, second):
    parts = [(n, lambda s: ()) for n in range(len(first) + 1)]
    sums = [(0, (1,), parts[-1:], False), (0, (0,), parts[:-1], True)]
    return block_sums("norm_both", place, list(first) + [second], [((2, SLOTS, D), BF16)], sums)[0]


def in_vmem(array):
    return pltpu.with_memory_space_constraint(array, pltpu.VMEM)


def kernel_call(body, name, arrays, out_shape, scratch, scalars=None, aliases=None, out=pltpu.VMEM):
    vmem = pl.BlockSpec(memory_space=pltpu.VMEM)
    in_specs, args = [vmem] * len(arrays), [in_vmem(array) for array in arrays]
    if scalars is not None:
        in_specs = [pl.BlockSpec(memory_space=pltpu.SMEM)] + in_specs
        args = [scalars] + args
    return pl.pallas_call(
        body,
        in_specs=in_specs,
        out_specs=[pl.BlockSpec(memory_space=out)] * len(out_shape),
        out_shape=out_shape,
        scratch_shapes=scratch,
        input_output_aliases=aliases or {},
        compiler_params=pltpu.CompilerParams(vmem_limit_bytes=VMEM),
        cost_estimate=cost(),
        name=name,
    )(*args)


def cand_kernel(owner_ref, feats_ref, w_ref, xs_ref, u_ref, q_ref, back_ref, a_ref):
    second = owner_ref[...].astype(F32)
    r_from = lax.broadcasted_iota(jnp.int32, (ROWS, ROWS), 0)
    r_to = lax.broadcasted_iota(jnp.int32, (ROWS, ROWS), 1)
    upper = jnp.where(r_from <= r_to, 1.0, 0.0).astype(BF16)
    ones_before = mm(jnp.broadcast_to(second, (8, ROWS)).astype(BF16), upper)[:1]
    index = lax.broadcasted_iota(jnp.int32, (1, ROWS), 1).astype(F32)
    n_first = ROWS - jnp.sum(second, axis=1, keepdims=True)
    place = jnp.where(second > 0.5, n_first + ones_before - 1.0, index - ones_before)
    onehot = jnp.where(r_from == place.astype(jnp.int32), 1.0, 0.0)
    back_ref[...] = onehot.T.astype(BF16)
    onehot = onehot.astype(BF16)
    x = layer_norm(feats_ref[...].astype(F32)).astype(BF16)
    xs_ref[...] = mm(onehot, x).astype(BF16)

    @pl.loop(0, D // GROUP)
    def _(g):
        cols = lambda n: pl.ds(pl.multiple_of(n * D + g * GROUP, GROUP), GROUP)
        u, v, q, k = (silu(mm(xs_ref[...], w_ref[:, cols(n)])).astype(BF16) for n in range(4))
        u_ref[:, cols(0)] = u
        q_ref[:, cols(0)] = q
        prod = q.astype(F32) * k.astype(F32)
        for h in range(GROUP // HD):
            hc = slice(h * HD, (h + 1) * HD)
            half = jnp.sum(prod[:, hc], axis=-1, keepdims=True) * HALF_SCALE
            own = (half + half * jnp.tanh(half)).astype(BF16).astype(F32)
            out_cols = pl.ds(pl.multiple_of(g * GROUP + h * HD, HD), HD)
            a_ref[:, out_cols] = own * v[:, hc].astype(F32)


def cand_project(owner_row, feats, w_in):
    rows = jax.ShapeDtypeStruct((ROWS, D), BF16)
    out_shape = [rows, rows, rows, jax.ShapeDtypeStruct((ROWS, ROWS), BF16), jax.ShapeDtypeStruct((ROWS, D), F32)]
    return kernel_call(cand_kernel, "cand_project", [owner_row, feats, w_in], out_shape, [])


def absorb_kernel(plan, scal_ref, *refs):
    pieces, first, final = plan
    count = len(pieces)
    refs = list(refs)
    take = lambda n: [refs.pop(0) for _ in range(n)]
    x_refs = take(count)
    w_ref, q_ref, a_ref = take(3)
    if not first:
        qh_ref, ah_ref = take(2)
    if final:
        uh_ref, own_ref, u_ref, xs_ref, back_ref, wo_ref, hist_ref, cand_ref = take(8)
    elif first:
        _, ah_ref, qh_ref, uh_ref = take(4)
    else:
        take(2)
    k_scr, v_scr = take(2)
    row_iota = lax.broadcasted_iota(jnp.int32, (SLOTS, 1), 0)
    ahead = lax.broadcasted_iota(jnp.int32, (SLOTS, SLOTS), 0) - lax.broadcasted_iota(
        jnp.int32, (SLOTS, SLOTS), 1
    )
    offs = [scal_ref[0, 4 + piece] for piece in pieces]
    my_off = scal_ref[0, 3]

    steps = D // GROUP

    def column(n, g):
        return slice(n * D + g * GROUP, n * D + (g + 1) * GROUP)

    def project(g, n):
        x = x_refs[n][...].reshape(2 * SLOTS, D)
        if first and n == 0:
            qh_ref[:, column(0, g)] = silu(mm(x, w_ref[:, column(2, g)])).astype(BF16)
            uh_ref[:, column(0, g)] = silu(mm(x, w_ref[:, column(0, g)])).astype(BF16)
        k = silu(mm(x, w_ref[:, column(3, g)])).astype(BF16)
        v = silu(mm(x, w_ref[:, column(1, g)])).astype(BF16)
        to = slice(n * SLOTS, (n + 1) * SLOTS)
        for user in (0, 1):
            at = slice(user * SLOTS, (user + 1) * SLOTS)
            live = row_iota < scal_ref[user, 0] - offs[n]
            k_scr[g % 2, user, to, :] = k[at]
            v_scr[g % 2, user, to, :] = jnp.where(live, v[at], jnp.zeros_like(v[at]))

    def attend(g, user, h, turn):
        row_lo, row_hi = scal_ref[user, 1], scal_ref[user, 2]
        covered = starts[user] + WINDOW
        start = pl.multiple_of(jnp.where(turn == 0, starts[user], ROWS - WINDOW), 16)
        rows = pl.ds(start, WINDOW)
        index = start + lax.broadcasted_iota(jnp.int32, (WINDOW, 1), 0)
        mine = (index >= jnp.where(turn == 0, row_lo, covered)) & (index < row_hi)
        mine_rows = slice(user * SLOTS, (user + 1) * SLOTS)
        hc = slice(h * HD, (h + 1) * HD)
        oc = slice(g * GROUP + h * HD, g * GROUP + (h + 1) * HD)
        q = jnp.concatenate([q_ref[rows, oc], qh_ref[mine_rows, oc]], axis=0)
        w = weights_of(q, k_scr[g % 2, user, :, hc])
        parts = []
        for n in range(count):
            part = w[WINDOW:, n * SLOTS : (n + 1) * SLOTS]
            seen = ahead >= offs[n] - my_off + turn * HIDE
            parts.append(jnp.where(seen, part, jnp.zeros_like(part)).astype(BF16))
        w = jnp.concatenate([w[:WINDOW].astype(BF16), jnp.concatenate(parts, axis=1)], axis=0)
        total = mm(w, v_scr[g % 2, user, :, hc])
        a_ref[rows, oc] += jnp.where(mine, total[:WINDOW], 0.0)
        ah_ref[mine_rows, oc] += total[WINDOW:]

    if first:
        ah_ref[...] = jnp.zeros((2 * SLOTS, D), F32)
    starts = [jnp.minimum((scal_ref[user, 1] // 16) * 16, ROWS - WINDOW) for user in (0, 1)]
    fits = [scal_ref[user, 2] <= starts[user] + WINDOW for user in (0, 1)]
    turns = jnp.where(fits[0] & fits[1], 1, 2)
    pairs = [(user, h) for user in (0, 1) for h in range(GROUP // HD)]

    @pl.loop(0, turns)
    def _(turn):
        for n in range(count):
            project(0, n)
        for g in range(steps):
            left = list(range(count)) if g + 1 < steps else []
            gap = max(1, len(pairs) // max(1, len(left)))
            for i, (user, h) in enumerate(pairs):
                if left and i % gap == 0:
                    project(g + 1, left.pop(0))
                attend(g, user, h, turn)
            for n in left:
                project(g + 1, n)

    if final:
        y_scr, hist_vm, cand_vm, sems = take(4)
        block = 2 * SLOTS
        half = D // 2

        def normed(n):
            sums, gate = (ah_ref, uh_ref) if n == 0 else (a_ref, u_ref)
            rows = slice(max(n - 1, 0) * block, (max(n - 1, 0) + 1) * block)
            y = layer_norm(sums[rows, :]) * gate[rows, :].astype(F32)
            y_scr[n * block : (n + 1) * block, :] = y.astype(BF16)

        stores = [pltpu.make_async_copy(hist_vm, hist_ref, sems.at[0])]
        for n in range(2):
            cols = slice(n * half, (n + 1) * half)
            stores.append(
                pltpu.make_async_copy(cand_vm.at[:, cols], cand_ref.at[:, cols], sems.at[1 + n])
            )
        normed(0)
        for n in range(1 + ROWS // block):
            at = slice(n * block, (n + 1) * block)
            res = mm(y_scr[at, :], wo_ref[...])
            if n < ROWS // block:
                normed(n + 1)
            if n == 0:
                res = res + own_ref[...].reshape(block, D).astype(F32)
                for user in (0, 1):
                    keep = my_off + row_iota < scal_ref[user, 0]
                    out = res[user * SLOTS : (user + 1) * SLOTS]
                    hist_vm[user] = jnp.where(keep, out, 0.0).astype(BF16)
                stores[0].start()
            else:
                rows = slice((n - 1) * block, n * block)
                y_scr[at, :] = (res + xs_ref[rows, :].astype(F32)).astype(BF16)
        for n in range(2):
            cols = slice(n * half, (n + 1) * half)
            cand_vm[:, cols] = mm(back_ref[...], y_scr[block:, cols]).astype(BF16)
            stores[1 + n].start()
        for store in stores:
            store.wait()


def absorb(name, scal, items, w_in, q_cand, a_cand, state=None, final=None):
    pieces = tuple(item[0] for item in items)
    arrays = [item[1] for item in items] + [w_in, q_cand, a_cand]
    a_at = len(arrays)
    scratch = [pltpu.VMEM((2, 2, len(pieces) * SLOTS, GROUP), BF16)] * 2
    sums = jax.ShapeDtypeStruct((2 * SLOTS, D), F32)
    rows = jax.ShapeDtypeStruct((2 * SLOTS, D), BF16)
    out_shape = [jax.ShapeDtypeStruct((ROWS, D), F32), sums]
    aliases = {a_at: 0}
    first = state is None
    if first:
        out_shape += [rows, rows]
    else:
        arrays += [state[0], state[2]]
        aliases[a_at + 2] = 1
    if final is not None:
        arrays += [state[1]] + list(final)
        out_shape = [jax.ShapeDtypeStruct((2, SLOTS, D), BF16), jax.ShapeDtypeStruct((ROWS, D), BF16)]
        aliases = {}
        scratch += [
            pltpu.VMEM((2 * SLOTS + ROWS, D), BF16),
            pltpu.VMEM((2, SLOTS, D), BF16),
            pltpu.VMEM((ROWS, D), BF16),
            pltpu.SemaphoreType.DMA((3,)),
        ]
    outs = kernel_call(
        functools.partial(absorb_kernel, (pieces, first, final is not None)),
        name,
        arrays,
        out_shape,
        scratch,
        scal,
        aliases,
        pl.ANY if final is not None else pltpu.VMEM,
    )
    if final is not None:
        return outs
    return outs[0], (outs[2], outs[3], outs[1]) if first else (state[0], state[1], outs[1])


def user_perm(dx, dy, dcore):
    pairs = []
    for u in range(4 * NX):
        x, y, core = u >> 2, (u >> 1) & 1, u & 1
        pairs.append((u, (((x + dx) % NX) * 2 + (y ^ dy)) * 2 + (core ^ dcore)))
    return pairs


def cand_perm(dz, dy):
    return [(c, (((c >> 1) + dz) % NZ) * 2 + ((c & 1) ^ dy)) for c in range(2 * NZ)]


def to_user(array, dx, dy, dcore):
    return lax.ppermute(array, "user", user_perm(dx, dy, dcore))


def to_cand(array, dz, dy):
    return lax.ppermute(array, "cand", cand_perm(dz, dy))


def local(pooled, cand_feats, hist_len, cand_user, w_in, w_out):
    user = lax.axis_index("user")
    cand = lax.axis_index("cand")
    x, y, core = user >> 2, (user >> 1) & 1, user & 1
    z, y_hi = cand >> 1, cand & 1
    owner = cand_user - 2 * user
    n_first = ROWS - jnp.sum(owner)
    offsets = [SLOTS * (((z + dz + NZ) % NZ) * 2 + (y_hi ^ e)) for dz in SHIFTS for e in range(2)]
    scal = jnp.stack(
        [
            jnp.stack([hist_len[0], 0 * user, n_first, cand * SLOTS] + offsets),
            jnp.stack([hist_len[1], n_first, 0 * user + ROWS, cand * SLOTS] + offsets),
        ]
    ).astype(jnp.int32)

    tables = pooled.reshape(NX, 2, 2, 2, SLOTS, D)
    place = jnp.stack([x, y, core]).astype(jnp.int32)
    with jax.named_scope("sum_core"):
        pack1 = pack(place, tables)
        got1 = to_user(pack1, 0, 0, 1)
        pack0 = pack_all(place, after(tables, pack1))
        got0 = [to_user(part, 0, 0, 1) for part in pack0]
    with jax.named_scope("sum_y_second"):
        over1 = over_y(place, tables, after(got1, pack0))
        y1 = to_user(over1, 0, 1, 0)
    with jax.named_scope("sum_x_first"):
        *away0, pack2 = away_x(place, tables, after(got0, over1))
        x0 = [to_user(part, d, 0, 0) for part, d in zip(away0, HOPS)]
    with jax.named_scope("sum_core"):
        got2 = to_user(pack2, 0, 0, 1)
    owner_row, scal = after((owner.reshape(1, ROWS), scal), pack2)
    xs, u_cand, q_cand, back, a_cand = cand_project(owner_row, cand_feats, w_in)
    with jax.named_scope("sum_y_second"):
        y1 = after(y1, xs, scal)
        away1 = join_y(place, tables, got2, y1)
        x1 = [to_user(part, d, 0, 0) for part, d in zip(away1, HOPS)]
    with jax.named_scope("sum_x_first"):
        mine0, over0, mine1 = join_x(place, tables, got0, after(x0, away1), got2, y1)
        y0 = to_user(over0, 0, 1, 0)
    with jax.named_scope("gather"):
        own1 = norm_sum(place, [mine1] + after(x1, mine0))
        own = norm_both(place, [mine0, after(y0, own1)], own1)
        near = to_cand(own, 0, 1)
        own_left, own_right = to_cand(own, 1, 0), to_cand(own, -1, 0)
    put = functools.partial(absorb, scal=scal, w_in=w_in, q_cand=q_cand)
    piece = lambda shift, e: 2 * SHIFTS.index(shift) + e
    a_cand, state = put("own_keys", items=[(piece(0, 0), own)], a_cand=a_cand)
    with jax.named_scope("gather"):
        near = after(near, a_cand)
        near_left, near_right = to_cand(near, 1, 0), to_cand(near, -1, 0)
        own_left, own_right = after((own_left, own_right), near)
        own_far = to_cand(own_left, 1, 0)
    a_cand, state = put(
        "own_sides",
        items=[(piece(-1, 0), own_left), (piece(1, 0), own_right), (piece(0, 1), near)],
        a_cand=a_cand,
        state=state,
    )
    with jax.named_scope("gather"):
        near_left, near_right = after((near_left, near_right), a_cand)
        near_far = to_cand(near_right, -1, 0)
    a_cand, state = put(
        "near_sides",
        items=[(piece(-1, 1), near_left), (piece(1, 1), near_right)],
        a_cand=a_cand,
        state=state,
    )
    return put(
        "far_finish",
        items=[(piece(2, 0), own_far), (piece(2, 1), near_far)],
        a_cand=a_cand,
        state=state,
        final=(own, u_cand, xs, back, w_out),
    )


def solution(mesh):
    placed = (
        P("user", None, "cand", None),
        P(("user", "cand"), None),
        P("user"),
        P(("user", "cand")),
        P(),
        P(),
    )
    return jax.shard_map(
        local,
        mesh=mesh,
        in_specs=placed,
        out_specs=(P("user", "cand", None), P(("user", "cand"), None)),
        check_vma=False,
    )
```

```python
import functools

import jax
import jax.numpy as jnp
from jax import lax
from jax.experimental import pallas as pl
from jax.experimental.pallas import tpu as pltpu
from jax.sharding import PartitionSpec as P

F32 = jnp.float32
BF16 = jnp.bfloat16
HEADS = 8
HD = 128
D = 1024
SLOTS = 128
ROWS = 512
NX, NZ = 4, 4
WINDOW = 320
HALF_SCALE = 0.5 / (HD**0.5)
VMEM = 20 * 1024 * 1024
GROUP = 512
SHIFTS = (0, -1, 1, 2)
HIDE = 1 << 16
HOPS = (1, 3, 2)
SIDES = (lambda s: s[1], lambda s: 1 - s[1])


def silu(v):
    half = v * 0.5
    half = half.astype(BF16)
    return half + half * jnp.tanh(half)


def layer_norm(rows):
    mean = jnp.mean(rows, axis=-1, keepdims=True)
    centered = rows - mean
    var = jnp.mean(centered * centered, axis=-1, keepdims=True)
    return centered * lax.rsqrt(var + 1e-05)


def mm(a, b):
    return jnp.dot(a, b, preferred_element_type=F32)


def weights_of(queries, keys):
    s = lax.dot_general(queries, keys, (((1,), (1,)), ((), ())), preferred_element_type=F32)
    half = (s * HALF_SCALE).astype(BF16)
    return half + half * jnp.tanh(half)


def after(value, *others):
    return lax.optimization_barrier((value, others))[0]


def in_hbm(array):
    return pltpu.with_memory_space_constraint(array, pltpu.HBM)


def cost():
    return pl.CostEstimate(flops=10**6, bytes_accessed=1 << 16, transcendentals=0)


def block_sums(name, scal, arrays, shapes, sums, held_in=()):
    added = [p for _, _, parts, _ in sums if len(parts) > 1 for p in parts if p[0] not in held_in]
    n_loads = sum(p[0] not in held_in for _, _, parts, _ in sums for p in parts)

    def body(scal_ref, *refs):
        ins, refs = refs[: len(arrays)], refs[len(arrays) :]
        outs, refs = refs[: len(shapes)], refs[len(shapes) :]
        bufs, in_sems = list(refs[: len(added)]), refs[len(added)]
        work, count = [], 0
        for out, lead, parts, norm in sums:
            lead = (lead(scal_ref),) if callable(lead) else lead
            dst = outs[out].at[lead] if lead else outs[out]
            copies, held = [], []
            for at, index in parts:
                from_ = index(scal_ref)
                src = ins[at].at[from_] if from_ else ins[at]
                if at in held_in:
                    held.append(src)
                    continue
                to = bufs.pop(0) if len(parts) > 1 else dst
                copies.append(pltpu.make_async_copy(src, to, in_sems.at[count]))
                copies[-1].start()
                held.append(to)
                count += 1
            work.append((dst, copies, held, norm))
        for dst, copies, held, norm in work:
            for copy in copies:
                copy.wait()
            if len(held) == 1 and not copies:
                dst[...] = held[0][...]
            if len(held) > 1:
                step = SLOTS if norm else SLOTS // 2

                @pl.loop(0, SLOTS // step)
                def _(r):
                    rows = pl.ds(pl.multiple_of(r * step, step), step)
                    exact = len(held) == 2 and not norm and all(ref.dtype == BF16 for ref in held)
                    total = None
                    for ref in held:
                        value = ref[rows, :] if exact else ref[rows, :].astype(F32)
                        total = value if total is None else total + value
                    dst[rows, :] = (layer_norm(total) if norm else total).astype(dst.dtype)

    hbm, anywhere = pl.BlockSpec(memory_space=pltpu.HBM), pl.BlockSpec(memory_space=pl.ANY)
    return pl.pallas_call(
        body,
        in_specs=[pl.BlockSpec(memory_space=pltpu.SMEM)]
        + [
            pl.BlockSpec(memory_space=pltpu.VMEM) if n in held_in else hbm if a.ndim == 6 else anywhere
            for n, a in enumerate(arrays)
        ],
        out_specs=[pl.BlockSpec(memory_space=pltpu.VMEM)] * len(shapes),
        out_shape=[jax.ShapeDtypeStruct(shape, dtype) for shape, dtype in shapes],
        scratch_shapes=[pltpu.VMEM((SLOTS, D), arrays[at].dtype) for at, _ in added]
        + [pltpu.SemaphoreType.DMA((max(n_loads, 1),))],
        compiler_params=pltpu.CompilerParams(vmem_limit_bytes=VMEM),
        cost_estimate=cost(),
        name=name,
    )(scal, *(in_hbm(a) if a.ndim == 6 else a for a in arrays))


def pack(place, tables):
    sums = [(0, (x,), [(0, lambda s, x=x: (x, 1 - s[1], 1 - s[2], 1))], False) for x in range(NX)]
    return block_sums("pack", place, [tables], [((NX, SLOTS, D), BF16)], sums)[0]


def pack_all(place, tables):
    sums = [
        (n, (x,), [(0, lambda s, x=x, side=side: (x, side(s), 1 - s[2], 0))], False)
        for x in range(NX)
        for n, side in enumerate(SIDES)
    ]
    return block_sums("pack_all", place, [tables], [((NX, SLOTS, D), BF16)] * 2, sums)


def over_y(place, tables, got):
    sums = [
        (0, (x,), [(0, lambda s, x=x: (x, 1 - s[1], s[2], 1)), (1, lambda s, x=x: (x,))], False)
        for x in range(NX)
    ]
    return block_sums("over_y", place, [tables, got], [((NX, SLOTS, D), BF16)], sums, (1,))[0]


def away_x(place, tables, got):
    sums = []
    for n, d in enumerate(HOPS):
        for m, side in enumerate(SIDES):
            at = lambda s, d=d: lax.rem(s[0] + d, NX)
            parts = [
                (0, lambda s, at=at, side=side: (at(s), side(s), s[2], 0)),
                (1 + m, lambda s, at=at: (at(s),)),
            ]
            sums.append((n, side, parts, False))
    for n in range(NX):
        sums.append((3, (n,), [(0, lambda s, n=n: (n, s[1], 1 - s[2], 1))], False))
    shapes = [((2, SLOTS, D), BF16)] * 3 + [((NX, SLOTS, D), BF16)]
    return block_sums("away_x", place, [tables] + list(got), shapes, sums, (1, 2))


def join_x(place, tables, got, arrived, got1, side1):
    arrays = [tables] + list(got) + list(arrived) + [got1, side1]
    sums = []
    for n in (1, 0):
        side = SIDES[n]
        parts = [(0, lambda s, side=side: (s[0], side(s), s[2], 0)), (1 + n, lambda s: (s[0],))]
        parts += [(3 + k, lambda s, side=side: (side(s),)) for k in range(3)]
        sums.append((n, (), parts, False))
    parts = [(0, lambda s: (s[0], s[1], s[2], 1)), (6, lambda s: (s[0],)), (7, lambda s: (s[0],))]
    sums.append((2, (), parts, False))
    shapes = [((SLOTS, D), F32), ((SLOTS, D), BF16), ((SLOTS, D), F32)]
    return block_sums("join_x", place, arrays, shapes, sums)


def join_y(place, tables, got, arrived):
    sums = []
    for n, d in enumerate(HOPS):
        at = lambda s, d=d: lax.rem(s[0] + d, NX)
        parts = [
            (0, lambda s, at=at: (at(s), s[1], s[2], 1)),
            (1, lambda s, at=at: (at(s),)),
            (2, lambda s, at=at: (at(s),)),
        ]
        sums.append((n, (), parts, False))
    return block_sums("join_y", place, [tables, got, arrived], [((SLOTS, D), BF16)] * 3, sums, (2,))


def norm_sum(place, arrays):
    parts = [(n, lambda s: ()) for n in range(len(arrays))]
    held_in = range(len(arrays))
    return block_sums("norm_sum", place, arrays, [((SLOTS, D), BF16)], [(0, (), parts, True)], held_in)[0]


def norm_both(place, first, second):
    parts = [(n, lambda s: ()) for n in range(len(first) + 1)]
    sums = [(0, (1,), parts[-1:], False), (0, (0,), parts[:-1], True)]
    arrays = list(first) + [second]
    return block_sums("norm_both", place, arrays, [((2, SLOTS, D), BF16)], sums, range(len(arrays)))[0]


def in_vmem(array):
    return pltpu.with_memory_space_constraint(array, pltpu.VMEM)


def kernel_call(body, name, arrays, out_shape, scratch, scalars=None, aliases=None, out=pltpu.VMEM):
    vmem = pl.BlockSpec(memory_space=pltpu.VMEM)
    in_specs, args = [vmem] * len(arrays), [in_vmem(array) for array in arrays]
    if scalars is not None:
        in_specs = [pl.BlockSpec(memory_space=pltpu.SMEM)] + in_specs
        args = [scalars] + args
    return pl.pallas_call(
        body,
        in_specs=in_specs,
        out_specs=[pl.BlockSpec(memory_space=out)] * len(out_shape),
        out_shape=out_shape,
        scratch_shapes=scratch,
        input_output_aliases=aliases or {},
        compiler_params=pltpu.CompilerParams(vmem_limit_bytes=VMEM),
        cost_estimate=cost(),
        name=name,
    )(*args)


def cand_kernel(owner_ref, feats_ref, w_ref, xs_ref, u_ref, q_ref, back_ref, a_ref):
    second = owner_ref[...].astype(F32)
    r_from = lax.broadcasted_iota(jnp.int32, (ROWS, ROWS), 0)
    r_to = lax.broadcasted_iota(jnp.int32, (ROWS, ROWS), 1)
    upper = jnp.where(r_from <= r_to, 1.0, 0.0).astype(BF16)
    ones_before = mm(jnp.broadcast_to(second, (8, ROWS)).astype(BF16), upper)[:1]
    index = lax.broadcasted_iota(jnp.int32, (1, ROWS), 1).astype(F32)
    n_first = ROWS - jnp.sum(second, axis=1, keepdims=True)
    place = jnp.where(second > 0.5, n_first + ones_before - 1.0, index - ones_before)
    onehot = jnp.where(r_from == place.astype(jnp.int32), 1.0, 0.0)
    back_ref[...] = onehot.T.astype(BF16)
    onehot = onehot.astype(BF16)
    x = layer_norm(feats_ref[...].astype(F32)).astype(BF16)
    xs_ref[...] = mm(onehot, x).astype(BF16)

    @pl.loop(0, D // GROUP)
    def _(g):
        cols = lambda n: pl.ds(pl.multiple_of(n * D + g * GROUP, GROUP), GROUP)
        u, v, q, k = (silu(mm(xs_ref[...], w_ref[:, cols(n)])).astype(BF16) for n in range(4))
        u_ref[:, cols(0)] = u
        q_ref[:, cols(0)] = q
        prod = q.astype(F32) * k.astype(F32)
        for h in range(GROUP // HD):
            hc = slice(h * HD, (h + 1) * HD)
            half = jnp.sum(prod[:, hc], axis=-1, keepdims=True) * HALF_SCALE
            own = (half + half * jnp.tanh(half)).astype(BF16).astype(F32)
            out_cols = pl.ds(pl.multiple_of(g * GROUP + h * HD, HD), HD)
            a_ref[:, out_cols] = own * v[:, hc].astype(F32)


def cand_project(owner_row, feats, w_in):
    rows = jax.ShapeDtypeStruct((ROWS, D), BF16)
    out_shape = [rows, rows, rows, jax.ShapeDtypeStruct((ROWS, ROWS), BF16), jax.ShapeDtypeStruct((ROWS, D), F32)]
    return kernel_call(cand_kernel, "cand_project", [owner_row, feats, w_in], out_shape, [])


def absorb_kernel(plan, scal_ref, *refs):
    pieces, first, final = plan
    count = len(pieces)
    refs = list(refs)
    take = lambda n: [refs.pop(0) for _ in range(n)]
    x_refs = take(count)
    w_ref, q_ref, a_ref = take(3)
    if not first:
        qh_ref, ah_ref = take(2)
    if final:
        uh_ref, own_ref, u_ref, xs_ref, back_ref, wo_ref, hist_ref, cand_ref = take(8)
    elif first:
        _, ah_ref, qh_ref, uh_ref = take(4)
    else:
        take(2)
    k_scr, v_scr = take(2)
    row_iota = lax.broadcasted_iota(jnp.int32, (SLOTS, 1), 0)
    ahead = lax.broadcasted_iota(jnp.int32, (SLOTS, SLOTS), 0) - lax.broadcasted_iota(
        jnp.int32, (SLOTS, SLOTS), 1
    )
    offs = [scal_ref[0, 4 + piece] for piece in pieces]
    my_off = scal_ref[0, 3]

    steps = D // GROUP

    def column(n, g):
        return slice(n * D + g * GROUP, n * D + (g + 1) * GROUP)

    def project(g, n):
        x = x_refs[n][...].reshape(2 * SLOTS, D)
        if first and n == 0:
            qh_ref[:, column(0, g)] = silu(mm(x, w_ref[:, column(2, g)])).astype(BF16)
            uh_ref[:, column(0, g)] = silu(mm(x, w_ref[:, column(0, g)])).astype(BF16)
        k = silu(mm(x, w_ref[:, column(3, g)])).astype(BF16)
        v = silu(mm(x, w_ref[:, column(1, g)])).astype(BF16)
        to = slice(n * SLOTS, (n + 1) * SLOTS)
        for user in (0, 1):
            at = slice(user * SLOTS, (user + 1) * SLOTS)
            live = row_iota < scal_ref[user, 0] - offs[n]
            k_scr[g % 2, user, to, :] = k[at]
            v_scr[g % 2, user, to, :] = jnp.where(live, v[at], jnp.zeros_like(v[at]))

    def attend(g, user, h, turn):
        row_lo, row_hi = scal_ref[user, 1], scal_ref[user, 2]
        covered = starts[user] + WINDOW
        start = pl.multiple_of(jnp.where(turn == 0, starts[user], ROWS - WINDOW), 16)
        rows = pl.ds(start, WINDOW)
        index = start + lax.broadcasted_iota(jnp.int32, (WINDOW, 1), 0)
        mine = (index >= jnp.where(turn == 0, row_lo, covered)) & (index < row_hi)
        mine_rows = slice(user * SLOTS, (user + 1) * SLOTS)
        hc = slice(h * HD, (h + 1) * HD)
        oc = slice(g * GROUP + h * HD, g * GROUP + (h + 1) * HD)
        q = jnp.concatenate([q_ref[rows, oc], qh_ref[mine_rows, oc]], axis=0)
        w = weights_of(q, k_scr[g % 2, user, :, hc])
        parts = []
        for n in range(count):
            part = w[WINDOW:, n * SLOTS : (n + 1) * SLOTS]
            seen = ahead >= offs[n] - my_off + turn * HIDE
            parts.append(jnp.where(seen, part, jnp.zeros_like(part)).astype(BF16))
        w = jnp.concatenate([w[:WINDOW].astype(BF16), jnp.concatenate(parts, axis=1)], axis=0)
        total = mm(w, v_scr[g % 2, user, :, hc])
        a_ref[rows, oc] += jnp.where(mine, total[:WINDOW], 0.0)
        ah_ref[mine_rows, oc] += total[WINDOW:]

    if first:
        ah_ref[...] = jnp.zeros((2 * SLOTS, D), F32)
    starts = [jnp.minimum((scal_ref[user, 1] // 16) * 16, ROWS - WINDOW) for user in (0, 1)]
    fits = [scal_ref[user, 2] <= starts[user] + WINDOW for user in (0, 1)]
    turns = jnp.where(fits[0] & fits[1], 1, 2)
    pairs = [(user, h) for user in (0, 1) for h in range(GROUP // HD)]

    @pl.loop(0, turns)
    def _(turn):
        for n in range(count):
            project(0, n)
        for g in range(steps):
            left = list(range(count)) if g + 1 < steps else []
            gap = max(1, len(pairs) // max(1, len(left)))
            for i, (user, h) in enumerate(pairs):
                if left and i % gap == 0:
                    project(g + 1, left.pop(0))
                attend(g, user, h, turn)
            for n in left:
                project(g + 1, n)

    if final:
        y_scr, hist_vm, cand_vm, sems = take(4)
        block = 2 * SLOTS
        half = D // 2

        def normed(n):
            sums, gate = (ah_ref, uh_ref) if n == 0 else (a_ref, u_ref)
            rows = slice(max(n - 1, 0) * block, (max(n - 1, 0) + 1) * block)
            y = layer_norm(sums[rows, :]) * gate[rows, :].astype(F32)
            y_scr[n * block : (n + 1) * block, :] = y.astype(BF16)

        stores = [pltpu.make_async_copy(hist_vm, hist_ref, sems.at[0])]
        for n in range(2):
            cols = slice(n * half, (n + 1) * half)
            stores.append(
                pltpu.make_async_copy(cand_vm.at[:, cols], cand_ref.at[:, cols], sems.at[1 + n])
            )
        normed(0)
        for n in range(1 + ROWS // block):
            at = slice(n * block, (n + 1) * block)
            res = mm(y_scr[at, :], wo_ref[...])
            if n < ROWS // block:
                normed(n + 1)
            if n == 0:
                res = res + own_ref[...].reshape(block, D).astype(F32)
                for user in (0, 1):
                    keep = my_off + row_iota < scal_ref[user, 0]
                    out = res[user * SLOTS : (user + 1) * SLOTS]
                    hist_vm[user] = jnp.where(keep, out, 0.0).astype(BF16)
                stores[0].start()
            else:
                rows = slice((n - 1) * block, n * block)
                y_scr[at, :] = (res + xs_ref[rows, :].astype(F32)).astype(BF16)
        for n in range(2):
            cols = slice(n * half, (n + 1) * half)
            cand_vm[:, cols] = mm(back_ref[...], y_scr[block:, cols]).astype(BF16)
            stores[1 + n].start()
        for store in stores:
            store.wait()


def absorb(name, scal, items, w_in, q_cand, a_cand, state=None, final=None):
    pieces = tuple(item[0] for item in items)
    arrays = [item[1] for item in items] + [w_in, q_cand, a_cand]
    a_at = len(arrays)
    scratch = [pltpu.VMEM((2, 2, len(pieces) * SLOTS, GROUP), BF16)] * 2
    sums = jax.ShapeDtypeStruct((2 * SLOTS, D), F32)
    rows = jax.ShapeDtypeStruct((2 * SLOTS, D), BF16)
    out_shape = [jax.ShapeDtypeStruct((ROWS, D), F32), sums]
    aliases = {a_at: 0}
    first = state is None
    if first:
        out_shape += [rows, rows]
    else:
        arrays += [state[0], state[2]]
        aliases[a_at + 2] = 1
    if final is not None:
        arrays += [state[1]] + list(final)
        out_shape = [jax.ShapeDtypeStruct((2, SLOTS, D), BF16), jax.ShapeDtypeStruct((ROWS, D), BF16)]
        aliases = {}
        scratch += [
            pltpu.VMEM((2 * SLOTS + ROWS, D), BF16),
            pltpu.VMEM((2, SLOTS, D), BF16),
            pltpu.VMEM((ROWS, D), BF16),
            pltpu.SemaphoreType.DMA((3,)),
        ]
    outs = kernel_call(
        functools.partial(absorb_kernel, (pieces, first, final is not None)),
        name,
        arrays,
        out_shape,
        scratch,
        scal,
        aliases,
        pl.ANY if final is not None else pltpu.VMEM,
    )
    if final is not None:
        return outs
    return outs[0], (outs[2], outs[3], outs[1]) if first else (state[0], state[1], outs[1])


def user_perm(dx, dy, dcore):
    pairs = []
    for u in range(4 * NX):
        x, y, core = u >> 2, (u >> 1) & 1, u & 1
        pairs.append((u, (((x + dx) % NX) * 2 + (y ^ dy)) * 2 + (core ^ dcore)))
    return pairs


def cand_perm(dz, dy):
    return [(c, (((c >> 1) + dz) % NZ) * 2 + ((c & 1) ^ dy)) for c in range(2 * NZ)]


def to_user(array, dx, dy, dcore):
    return lax.ppermute(array, "user", user_perm(dx, dy, dcore))


def to_cand(array, dz, dy):
    return lax.ppermute(array, "cand", cand_perm(dz, dy))


def local(pooled, cand_feats, hist_len, cand_user, w_in, w_out):
    user = lax.axis_index("user")
    cand = lax.axis_index("cand")
    x, y, core = user >> 2, (user >> 1) & 1, user & 1
    z, y_hi = cand >> 1, cand & 1
    owner = cand_user - 2 * user
    n_first = ROWS - jnp.sum(owner)
    offsets = [SLOTS * (((z + dz + NZ) % NZ) * 2 + (y_hi ^ e)) for dz in SHIFTS for e in range(2)]
    scal = jnp.stack(
        [
            jnp.stack([hist_len[0], 0 * user, n_first, cand * SLOTS] + offsets),
            jnp.stack([hist_len[1], n_first, 0 * user + ROWS, cand * SLOTS] + offsets),
        ]
    ).astype(jnp.int32)

    tables = pooled.reshape(NX, 2, 2, 2, SLOTS, D)
    place = jnp.stack([x, y, core]).astype(jnp.int32)
    with jax.named_scope("sum_core"):
        pack1 = pack(place, tables)
        got1 = to_user(pack1, 0, 0, 1)
        pack0 = pack_all(place, after(tables, pack1))
        got0 = [to_user(part, 0, 0, 1) for part in pack0]
    with jax.named_scope("sum_y_second"):
        over1 = over_y(place, tables, after(got1, pack0))
        y1 = to_user(over1, 0, 1, 0)
    with jax.named_scope("sum_x_first"):
        *away0, pack2 = away_x(place, tables, after(got0, over1))
        x0 = [to_user(part, d, 0, 0) for part, d in zip(away0, HOPS)]
    with jax.named_scope("sum_core"):
        got2 = to_user(pack2, 0, 0, 1)
    owner_row, scal = after((owner.reshape(1, ROWS), scal), pack2)
    xs, u_cand, q_cand, back, a_cand = cand_project(owner_row, cand_feats, w_in)
    with jax.named_scope("sum_y_second"):
        y1 = after(y1, xs, scal)
        away1 = join_y(place, tables, got2, y1)
        x1 = [to_user(part, d, 0, 0) for part, d in zip(away1, HOPS)]
    with jax.named_scope("sum_x_first"):
        mine0, over0, mine1 = join_x(place, tables, got0, after(x0, away1), got2, y1)
        y0 = to_user(over0, 0, 1, 0)
    with jax.named_scope("gather"):
        own1 = norm_sum(place, [mine1] + after(x1, mine0))
        own = norm_both(place, [mine0, after(y0, own1)], own1)
        near = to_cand(own, 0, 1)
        own_left, own_right = to_cand(own, 1, 0), to_cand(own, -1, 0)
    put = functools.partial(absorb, scal=scal, w_in=w_in, q_cand=q_cand)
    piece = lambda shift, e: 2 * SHIFTS.index(shift) + e
    a_cand, state = put("own_keys", items=[(piece(0, 0), own)], a_cand=a_cand)
    with jax.named_scope("gather"):
        near = after(near, a_cand)
        near_left, near_right = to_cand(near, 1, 0), to_cand(near, -1, 0)
        own_left, own_right = after((own_left, own_right), near)
        own_far = to_cand(own_left, 1, 0)
    a_cand, state = put(
        "own_sides",
        items=[(piece(-1, 0), own_left), (piece(1, 0), own_right), (piece(0, 1), near)],
        a_cand=a_cand,
        state=state,
    )
    with jax.named_scope("gather"):
        near_left, near_right = after((near_left, near_right), a_cand)
        near_far = to_cand(near_right, -1, 0)
    a_cand, state = put(
        "near_sides",
        items=[(piece(-1, 1), near_left), (piece(1, 1), near_right)],
        a_cand=a_cand,
        state=state,
    )
    return put(
        "far_finish",
        items=[(piece(2, 0), own_far), (piece(2, 1), near_far)],
        a_cand=a_cand,
        state=state,
        final=(own, u_cand, xs, back, w_out),
    )


def solution(mesh):
    placed = (
        P("user", None, "cand", None),
        P(("user", "cand"), None),
        P("user"),
        P(("user", "cand")),
        P(),
        P(),
    )
    return jax.shard_map(
        local,
        mesh=mesh,
        in_specs=placed,
        out_specs=(P("user", "cand", None), P(("user", "cand"), None)),
        check_vma=False,
    )
```

```python
import functools

import jax
import jax.numpy as jnp
from jax import lax
from jax.experimental import pallas as pl
from jax.experimental.pallas import tpu as pltpu
from jax.sharding import PartitionSpec as P

F32 = jnp.float32
BF16 = jnp.bfloat16
HEADS = 8
HD = 128
D = 1024
SLOTS = 128
ROWS = 512
NX, NZ = 4, 4
WINDOW = 320
HALF_SCALE = 0.5 / (HD**0.5)
VMEM = 20 * 1024 * 1024
GROUP = 512
SHIFTS = (0, -1, 1, 2)
HIDE = 1 << 16
HOPS = (2, 1, 3)
SIDES = (lambda s: s[1], lambda s: 1 - s[1])


def silu(v):
    half = v * 0.5
    half = half.astype(BF16)
    return half + half * jnp.tanh(half)


def layer_norm(rows):
    mean = jnp.mean(rows, axis=-1, keepdims=True)
    centered = rows - mean
    var = jnp.mean(centered * centered, axis=-1, keepdims=True)
    return centered * lax.rsqrt(var + 1e-05)


def mm(a, b):
    return jnp.dot(a, b, preferred_element_type=F32)


def weights_of(queries, keys):
    s = lax.dot_general(queries, keys, (((1,), (1,)), ((), ())), preferred_element_type=F32)
    half = (s * HALF_SCALE).astype(BF16)
    return half + half * jnp.tanh(half)


def after(value, *others):
    return lax.optimization_barrier((value, others))[0]


def in_hbm(array):
    return pltpu.with_memory_space_constraint(array, pltpu.HBM)


def cost():
    return pl.CostEstimate(flops=10**6, bytes_accessed=1 << 16, transcendentals=0)


def block_sums(name, scal, arrays, shapes, sums, held_in=()):
    added = [p for _, _, parts, _ in sums if len(parts) > 1 for p in parts if p[0] not in held_in]
    n_loads = sum(p[0] not in held_in for _, _, parts, _ in sums for p in parts)

    def body(scal_ref, *refs):
        ins, refs = refs[: len(arrays)], refs[len(arrays) :]
        outs, refs = refs[: len(shapes)], refs[len(shapes) :]
        bufs, in_sems = list(refs[: len(added)]), refs[len(added)]
        work, count = [], 0
        for out, lead, parts, norm in sums:
            lead = (lead(scal_ref),) if callable(lead) else lead
            dst = outs[out].at[lead] if lead else outs[out]
            copies, held = [], []
            for at, index in parts:
                from_ = index(scal_ref)
                src = ins[at].at[from_] if from_ else ins[at]
                if at in held_in:
                    held.append(src)
                    continue
                to = bufs.pop(0) if len(parts) > 1 else dst
                copies.append(pltpu.make_async_copy(src, to, in_sems.at[count]))
                copies[-1].start()
                held.append(to)
                count += 1
            work.append((dst, copies, held, norm))
        for dst, copies, held, norm in work:
            for copy in copies:
                copy.wait()
            if len(held) == 1 and not copies:
                dst[...] = held[0][...]
            if len(held) > 1:
                step = SLOTS if norm else SLOTS // 2

                @pl.loop(0, SLOTS // step)
                def _(r):
                    rows = pl.ds(pl.multiple_of(r * step, step), step)
                    exact = len(held) == 2 and not norm and all(ref.dtype == BF16 for ref in held)
                    total = None
                    for ref in held:
                        value = ref[rows, :] if exact else ref[rows, :].astype(F32)
                        total = value if total is None else total + value
                    dst[rows, :] = (layer_norm(total) if norm else total).astype(dst.dtype)

    hbm, anywhere = pl.BlockSpec(memory_space=pltpu.HBM), pl.BlockSpec(memory_space=pl.ANY)
    return pl.pallas_call(
        body,
        in_specs=[pl.BlockSpec(memory_space=pltpu.SMEM)]
        + [
            pl.BlockSpec(memory_space=pltpu.VMEM) if n in held_in else hbm if a.ndim == 6 else anywhere
            for n, a in enumerate(arrays)
        ],
        out_specs=[pl.BlockSpec(memory_space=pltpu.VMEM)] * len(shapes),
        out_shape=[jax.ShapeDtypeStruct(shape, dtype) for shape, dtype in shapes],
        scratch_shapes=[pltpu.VMEM((SLOTS, D), arrays[at].dtype) for at, _ in added]
        + [pltpu.SemaphoreType.DMA((max(n_loads, 1),))],
        compiler_params=pltpu.CompilerParams(vmem_limit_bytes=VMEM),
        cost_estimate=cost(),
        name=name,
    )(scal, *(in_hbm(a) if a.ndim == 6 else a for a in arrays))


def pack(place, tables):
    sums = [(0, (x,), [(0, lambda s, x=x: (x, 1 - s[1], 1 - s[2], 1))], False) for x in range(NX)]
    return block_sums("pack", place, [tables], [((NX, SLOTS, D), BF16)], sums)[0]


def pack_all(place, tables):
    sums = [
        (n, (x,), [(0, lambda s, x=x, side=side: (x, side(s), 1 - s[2], 0))], False)
        for x in range(NX)
        for n, side in enumerate(SIDES)
    ]
    return block_sums("pack_all", place, [tables], [((NX, SLOTS, D), BF16)] * 2, sums)


def over_y(place, tables, got):
    sums = [
        (0, (x,), [(0, lambda s, x=x: (x, 1 - s[1], s[2], 1)), (1, lambda s, x=x: (x,))], False)
        for x in range(NX)
    ]
    return block_sums("over_y", place, [tables, got], [((NX, SLOTS, D), BF16)], sums, (1,))[0]


def away_x(place, tables, got):
    sums = []
    for n, d in enumerate(HOPS):
        for m, side in enumerate(SIDES):
            at = lambda s, d=d: lax.rem(s[0] + d, NX)
            parts = [
                (0, lambda s, at=at, side=side: (at(s), side(s), s[2], 0)),
                (1 + m, lambda s, at=at: (at(s),)),
            ]
            sums.append((n, side, parts, False))
    for n in range(NX):
        sums.append((3, (n,), [(0, lambda s, n=n: (n, s[1], 1 - s[2], 1))], False))
    shapes = [((2, SLOTS, D), BF16)] * 3 + [((NX, SLOTS, D), BF16)]
    return block_sums("away_x", place, [tables] + list(got), shapes, sums, (1, 2))


def join_x(place, tables, got, arrived, got1, side1):
    arrays = [tables] + list(got) + list(arrived) + [got1, side1]
    sums = []
    for n in (1, 0):
        side = SIDES[n]
        parts = [(0, lambda s, side=side: (s[0], side(s), s[2], 0)), (1 + n, lambda s: (s[0],))]
        parts += [(3 + k, lambda s, side=side: (side(s),)) for k in range(3)]
        sums.append((n, (), parts, False))
    parts = [(0, lambda s: (s[0], s[1], s[2], 1)), (6, lambda s: (s[0],)), (7, lambda s: (s[0],))]
    sums.append((2, (), parts, False))
    shapes = [((SLOTS, D), F32), ((SLOTS, D), BF16), ((SLOTS, D), F32)]
    return block_sums("join_x", place, arrays, shapes, sums)


def join_y(place, tables, got, arrived):
    sums = []
    for n, d in enumerate(HOPS):
        at = lambda s, d=d: lax.rem(s[0] + d, NX)
        parts = [
            (0, lambda s, at=at: (at(s), s[1], s[2], 1)),
            (1, lambda s, at=at: (at(s),)),
            (2, lambda s, at=at: (at(s),)),
        ]
        sums.append((n, (), parts, False))
    return block_sums("join_y", place, [tables, got, arrived], [((SLOTS, D), BF16)] * 3, sums, (2,))


def norm_sum(place, arrays):
    parts = [(n, lambda s: ()) for n in range(len(arrays))]
    held_in = range(len(arrays))
    return block_sums("norm_sum", place, arrays, [((SLOTS, D), BF16)], [(0, (), parts, True)], held_in)[0]


def norm_both(place, first, second):
    parts = [(n, lambda s: ()) for n in range(len(first) + 1)]
    sums = [(0, (1,), parts[-1:], False), (0, (0,), parts[:-1], True)]
    arrays = list(first) + [second]
    return block_sums("norm_both", place, arrays, [((2, SLOTS, D), BF16)], sums, range(len(arrays)))[0]


def in_vmem(array):
    return pltpu.with_memory_space_constraint(array, pltpu.VMEM)


def kernel_call(body, name, arrays, out_shape, scratch, scalars=None, aliases=None, out=pltpu.VMEM):
    vmem = pl.BlockSpec(memory_space=pltpu.VMEM)
    in_specs, args = [vmem] * len(arrays), [in_vmem(array) for array in arrays]
    if scalars is not None:
        in_specs = [pl.BlockSpec(memory_space=pltpu.SMEM)] + in_specs
        args = [scalars] + args
    return pl.pallas_call(
        body,
        in_specs=in_specs,
        out_specs=[pl.BlockSpec(memory_space=out)] * len(out_shape),
        out_shape=out_shape,
        scratch_shapes=scratch,
        input_output_aliases=aliases or {},
        compiler_params=pltpu.CompilerParams(vmem_limit_bytes=VMEM),
        cost_estimate=cost(),
        name=name,
    )(*args)


def cand_kernel(owner_ref, feats_ref, w_ref, xs_ref, u_ref, q_ref, back_ref, a_ref):
    second = owner_ref[...].astype(F32)
    r_from = lax.broadcasted_iota(jnp.int32, (ROWS, ROWS), 0)
    r_to = lax.broadcasted_iota(jnp.int32, (ROWS, ROWS), 1)
    upper = jnp.where(r_from <= r_to, 1.0, 0.0).astype(BF16)
    ones_before = mm(jnp.broadcast_to(second, (8, ROWS)).astype(BF16), upper)[:1]
    index = lax.broadcasted_iota(jnp.int32, (1, ROWS), 1).astype(F32)
    n_first = ROWS - jnp.sum(second, axis=1, keepdims=True)
    place = jnp.where(second > 0.5, n_first + ones_before - 1.0, index - ones_before)
    onehot = jnp.where(r_from == place.astype(jnp.int32), 1.0, 0.0)
    back_ref[...] = onehot.T.astype(BF16)
    onehot = onehot.astype(BF16)
    x = layer_norm(feats_ref[...].astype(F32)).astype(BF16)
    xs_ref[...] = mm(onehot, x).astype(BF16)

    @pl.loop(0, D // GROUP)
    def _(g):
        cols = lambda n: pl.ds(pl.multiple_of(n * D + g * GROUP, GROUP), GROUP)
        u, v, q, k = (silu(mm(xs_ref[...], w_ref[:, cols(n)])).astype(BF16) for n in range(4))
        u_ref[:, cols(0)] = u
        q_ref[:, cols(0)] = q
        prod = q.astype(F32) * k.astype(F32)
        for h in range(GROUP // HD):
            hc = slice(h * HD, (h + 1) * HD)
            half = jnp.sum(prod[:, hc], axis=-1, keepdims=True) * HALF_SCALE
            own = (half + half * jnp.tanh(half)).astype(BF16).astype(F32)
            out_cols = pl.ds(pl.multiple_of(g * GROUP + h * HD, HD), HD)
            a_ref[:, out_cols] = own * v[:, hc].astype(F32)


def cand_project(owner_row, feats, w_in):
    rows = jax.ShapeDtypeStruct((ROWS, D), BF16)
    out_shape = [rows, rows, rows, jax.ShapeDtypeStruct((ROWS, ROWS), BF16), jax.ShapeDtypeStruct((ROWS, D), F32)]
    return kernel_call(cand_kernel, "cand_project", [owner_row, feats, w_in], out_shape, [])


def absorb_kernel(plan, scal_ref, *refs):
    pieces, first, final = plan
    count = len(pieces)
    refs = list(refs)
    take = lambda n: [refs.pop(0) for _ in range(n)]
    x_refs = take(count)
    w_ref, q_ref, a_ref = take(3)
    if not first:
        qh_ref, ah_ref = take(2)
    if final:
        uh_ref, own_ref, u_ref, xs_ref, back_ref, wo_ref, hist_ref, cand_ref = take(8)
    elif first:
        _, ah_ref, qh_ref, uh_ref = take(4)
    else:
        take(2)
    k_scr, v_scr = take(2)
    row_iota = lax.broadcasted_iota(jnp.int32, (SLOTS, 1), 0)
    ahead = lax.broadcasted_iota(jnp.int32, (SLOTS, SLOTS), 0) - lax.broadcasted_iota(
        jnp.int32, (SLOTS, SLOTS), 1
    )
    offs = [scal_ref[0, 4 + piece] for piece in pieces]
    my_off = scal_ref[0, 3]

    steps = D // GROUP

    def column(n, g):
        return slice(n * D + g * GROUP, n * D + (g + 1) * GROUP)

    def project(g, n):
        x = x_refs[n][...].reshape(2 * SLOTS, D)
        if first and n == 0:
            qh_ref[:, column(0, g)] = silu(mm(x, w_ref[:, column(2, g)])).astype(BF16)
            uh_ref[:, column(0, g)] = silu(mm(x, w_ref[:, column(0, g)])).astype(BF16)
        k = silu(mm(x, w_ref[:, column(3, g)])).astype(BF16)
        v = silu(mm(x, w_ref[:, column(1, g)])).astype(BF16)
        to = slice(n * SLOTS, (n + 1) * SLOTS)
        for user in (0, 1):
            at = slice(user * SLOTS, (user + 1) * SLOTS)
            live = row_iota < scal_ref[user, 0] - offs[n]
            k_scr[g % 2, user, to, :] = k[at]
            v_scr[g % 2, user, to, :] = jnp.where(live, v[at], jnp.zeros_like(v[at]))

    def attend(g, user, h, turn):
        row_lo, row_hi = scal_ref[user, 1], scal_ref[user, 2]
        covered = starts[user] + WINDOW
        start = pl.multiple_of(jnp.where(turn == 0, starts[user], ROWS - WINDOW), 16)
        rows = pl.ds(start, WINDOW)
        index = start + lax.broadcasted_iota(jnp.int32, (WINDOW, 1), 0)
        mine = (index >= jnp.where(turn == 0, row_lo, covered)) & (index < row_hi)
        mine_rows = slice(user * SLOTS, (user + 1) * SLOTS)
        hc = slice(h * HD, (h + 1) * HD)
        oc = slice(g * GROUP + h * HD, g * GROUP + (h + 1) * HD)
        q = jnp.concatenate([q_ref[rows, oc], qh_ref[mine_rows, oc]], axis=0)
        w = weights_of(q, k_scr[g % 2, user, :, hc])
        parts = []
        for n in range(count):
            part = w[WINDOW:, n * SLOTS : (n + 1) * SLOTS]
            seen = ahead >= offs[n] - my_off + turn * HIDE
            parts.append(jnp.where(seen, part, jnp.zeros_like(part)).astype(BF16))
        w = jnp.concatenate([w[:WINDOW].astype(BF16), jnp.concatenate(parts, axis=1)], axis=0)
        total = mm(w, v_scr[g % 2, user, :, hc])
        a_ref[rows, oc] += jnp.where(mine, total[:WINDOW], 0.0)
        ah_ref[mine_rows, oc] += total[WINDOW:]

    if first:
        ah_ref[...] = jnp.zeros((2 * SLOTS, D), F32)
    starts = [jnp.minimum((scal_ref[user, 1] // 16) * 16, ROWS - WINDOW) for user in (0, 1)]
    fits = [scal_ref[user, 2] <= starts[user] + WINDOW for user in (0, 1)]
    turns = jnp.where(fits[0] & fits[1], 1, 2)
    pairs = [(user, h) for user in (0, 1) for h in range(GROUP // HD)]

    @pl.loop(0, turns)
    def _(turn):
        for n in range(count):
            project(0, n)
        for g in range(steps):
            left = list(range(count)) if g + 1 < steps else []
            gap = max(1, len(pairs) // max(1, len(left)))
            for i, (user, h) in enumerate(pairs):
                if left and i % gap == 0:
                    project(g + 1, left.pop(0))
                attend(g, user, h, turn)
            for n in left:
                project(g + 1, n)

    if final:
        y_scr, hist_vm, cand_vm, sems = take(4)
        block = 2 * SLOTS
        half = D // 2

        def normed(n):
            sums, gate = (ah_ref, uh_ref) if n == 0 else (a_ref, u_ref)
            rows = slice(max(n - 1, 0) * block, (max(n - 1, 0) + 1) * block)
            y = layer_norm(sums[rows, :]) * gate[rows, :].astype(F32)
            y_scr[n * block : (n + 1) * block, :] = y.astype(BF16)

        stores = [pltpu.make_async_copy(hist_vm, hist_ref, sems.at[0])]
        for n in range(2):
            cols = slice(n * half, (n + 1) * half)
            stores.append(
                pltpu.make_async_copy(cand_vm.at[:, cols], cand_ref.at[:, cols], sems.at[1 + n])
            )
        normed(0)
        for n in range(1 + ROWS // block):
            at = slice(n * block, (n + 1) * block)
            res = mm(y_scr[at, :], wo_ref[...])
            if n < ROWS // block:
                normed(n + 1)
            if n == 0:
                res = res + own_ref[...].reshape(block, D).astype(F32)
                for user in (0, 1):
                    keep = my_off + row_iota < scal_ref[user, 0]
                    out = res[user * SLOTS : (user + 1) * SLOTS]
                    hist_vm[user] = jnp.where(keep, out, 0.0).astype(BF16)
                stores[0].start()
            else:
                rows = slice((n - 1) * block, n * block)
                y_scr[at, :] = (res + xs_ref[rows, :].astype(F32)).astype(BF16)
        for n in range(2):
            cols = slice(n * half, (n + 1) * half)
            cand_vm[:, cols] = mm(back_ref[...], y_scr[block:, cols]).astype(BF16)
            stores[1 + n].start()
        for store in stores:
            store.wait()


def absorb(name, scal, items, w_in, q_cand, a_cand, state=None, final=None):
    pieces = tuple(item[0] for item in items)
    arrays = [item[1] for item in items] + [w_in, q_cand, a_cand]
    a_at = len(arrays)
    scratch = [pltpu.VMEM((2, 2, len(pieces) * SLOTS, GROUP), BF16)] * 2
    sums = jax.ShapeDtypeStruct((2 * SLOTS, D), F32)
    rows = jax.ShapeDtypeStruct((2 * SLOTS, D), BF16)
    out_shape = [jax.ShapeDtypeStruct((ROWS, D), F32), sums]
    aliases = {a_at: 0}
    first = state is None
    if first:
        out_shape += [rows, rows]
    else:
        arrays += [state[0], state[2]]
        aliases[a_at + 2] = 1
    if final is not None:
        arrays += [state[1]] + list(final)
        out_shape = [jax.ShapeDtypeStruct((2, SLOTS, D), BF16), jax.ShapeDtypeStruct((ROWS, D), BF16)]
        aliases = {}
        scratch += [
            pltpu.VMEM((2 * SLOTS + ROWS, D), BF16),
            pltpu.VMEM((2, SLOTS, D), BF16),
            pltpu.VMEM((ROWS, D), BF16),
            pltpu.SemaphoreType.DMA((3,)),
        ]
    outs = kernel_call(
        functools.partial(absorb_kernel, (pieces, first, final is not None)),
        name,
        arrays,
        out_shape,
        scratch,
        scal,
        aliases,
        pl.ANY if final is not None else pltpu.VMEM,
    )
    if final is not None:
        return outs
    return outs[0], (outs[2], outs[3], outs[1]) if first else (state[0], state[1], outs[1])


def user_perm(dx, dy, dcore):
    pairs = []
    for u in range(4 * NX):
        x, y, core = u >> 2, (u >> 1) & 1, u & 1
        pairs.append((u, (((x + dx) % NX) * 2 + (y ^ dy)) * 2 + (core ^ dcore)))
    return pairs


def cand_perm(dz, dy):
    return [(c, (((c >> 1) + dz) % NZ) * 2 + ((c & 1) ^ dy)) for c in range(2 * NZ)]


def to_user(array, dx, dy, dcore):
    return lax.ppermute(array, "user", user_perm(dx, dy, dcore))


def to_cand(array, dz, dy):
    return lax.ppermute(array, "cand", cand_perm(dz, dy))


def local(pooled, cand_feats, hist_len, cand_user, w_in, w_out):
    user = lax.axis_index("user")
    cand = lax.axis_index("cand")
    x, y, core = user >> 2, (user >> 1) & 1, user & 1
    z, y_hi = cand >> 1, cand & 1
    owner = cand_user - 2 * user
    n_first = ROWS - jnp.sum(owner)
    offsets = [SLOTS * (((z + dz + NZ) % NZ) * 2 + (y_hi ^ e)) for dz in SHIFTS for e in range(2)]
    scal = jnp.stack(
        [
            jnp.stack([hist_len[0], 0 * user, n_first, cand * SLOTS] + offsets),
            jnp.stack([hist_len[1], n_first, 0 * user + ROWS, cand * SLOTS] + offsets),
        ]
    ).astype(jnp.int32)

    tables = pooled.reshape(NX, 2, 2, 2, SLOTS, D)
    place = jnp.stack([x, y, core]).astype(jnp.int32)
    with jax.named_scope("sum_core"):
        pack1 = pack(place, tables)
        got1 = to_user(pack1, 0, 0, 1)
        pack0 = pack_all(place, after(tables, pack1))
        got0 = [to_user(part, 0, 0, 1) for part in pack0]
    with jax.named_scope("sum_y_second"):
        over1 = over_y(place, tables, after(got1, pack0))
        y1 = to_user(over1, 0, 1, 0)
    with jax.named_scope("sum_x_first"):
        *away0, pack2 = away_x(place, tables, after(got0, over1))
        x0 = [to_user(part, d, 0, 0) for part, d in zip(away0, HOPS)]
    with jax.named_scope("sum_core"):
        got2 = to_user(pack2, 0, 0, 1)
    owner_row, scal = after((owner.reshape(1, ROWS), scal), pack2)
    xs, u_cand, q_cand, back, a_cand = cand_project(owner_row, cand_feats, w_in)
    with jax.named_scope("sum_y_second"):
        y1 = after(y1, xs, scal)
        away1 = join_y(place, tables, got2, y1)
        x1 = [to_user(part, d, 0, 0) for part, d in zip(away1, HOPS)]
    with jax.named_scope("sum_x_first"):
        mine0, over0, mine1 = join_x(place, tables, got0, after(x0, away1), got2, y1)
        y0 = to_user(over0, 0, 1, 0)
    with jax.named_scope("gather"):
        own1 = norm_sum(place, [mine1] + after(x1, mine0))
        own = norm_both(place, [mine0, after(y0, own1)], own1)
        near = to_cand(own, 0, 1)
        own_left, own_right = to_cand(own, 1, 0), to_cand(own, -1, 0)
    put = functools.partial(absorb, scal=scal, w_in=w_in, q_cand=q_cand)
    piece = lambda shift, e: 2 * SHIFTS.index(shift) + e
    a_cand, state = put("own_keys", items=[(piece(0, 0), own)], a_cand=a_cand)
    with jax.named_scope("gather"):
        near = after(near, a_cand)
        near_left, near_right = to_cand(near, 1, 0), to_cand(near, -1, 0)
        own_left, own_right = after((own_left, own_right), near)
        own_far = to_cand(own_left, 1, 0)
    a_cand, state = put(
        "own_sides",
        items=[(piece(-1, 0), own_left), (piece(1, 0), own_right), (piece(0, 1), near)],
        a_cand=a_cand,
        state=state,
    )
    with jax.named_scope("gather"):
        near_left, near_right = after((near_left, near_right), a_cand)
        near_far = to_cand(near_right, -1, 0)
    a_cand, state = put(
        "near_sides",
        items=[(piece(-1, 1), near_left), (piece(1, 1), near_right)],
        a_cand=a_cand,
        state=state,
    )
    return put(
        "far_finish",
        items=[(piece(2, 0), own_far), (piece(2, 1), near_far)],
        a_cand=a_cand,
        state=state,
        final=(own, u_cand, xs, back, w_out),
    )


def solution(mesh):
    placed = (
        P("user", None, "cand", None),
        P(("user", "cand"), None),
        P("user"),
        P(("user", "cand")),
        P(),
        P(),
    )
    return jax.shard_map(
        local,
        mesh=mesh,
        in_specs=placed,
        out_specs=(P("user", "cand", None), P(("user", "cand"), None)),
        check_vma=False,
    )
```

```python
import functools

import jax
import jax.numpy as jnp
from jax import lax
from jax.experimental import pallas as pl
from jax.experimental.pallas import tpu as pltpu
from jax.sharding import PartitionSpec as P

F32 = jnp.float32
BF16 = jnp.bfloat16
HEADS = 8
HD = 128
D = 1024
SLOTS = 128
ROWS = 512
NX, NZ = 4, 4
WINDOW = 320
HALF_SCALE = 0.5 / (HD**0.5)
VMEM = 20 * 1024 * 1024
GROUP = 512
SHIFTS = (0, -1, 1, 2)
HIDE = 1 << 16
HOPS = (1, 3, 2)
SIDES = (lambda s: s[1], lambda s: 1 - s[1])


def silu(v):
    half = v * 0.5
    half = half.astype(BF16)
    return half + half * jnp.tanh(half)


def layer_norm(rows):
    mean = jnp.mean(rows, axis=-1, keepdims=True)
    centered = rows - mean
    var = jnp.mean(centered * centered, axis=-1, keepdims=True)
    return centered * lax.rsqrt(var + 1e-05)


def mm(a, b):
    return jnp.dot(a, b, preferred_element_type=F32)


def weights_of(queries, keys):
    s = lax.dot_general(queries, keys, (((1,), (1,)), ((), ())), preferred_element_type=F32)
    half = (s * HALF_SCALE).astype(BF16)
    return half + half * jnp.tanh(half)


def after(value, *others):
    return lax.optimization_barrier((value, others))[0]


def in_hbm(array):
    return pltpu.with_memory_space_constraint(array, pltpu.HBM)


def cost():
    return pl.CostEstimate(flops=10**6, bytes_accessed=1 << 16, transcendentals=0)


def block_sums(name, scal, arrays, shapes, sums, held_in=()):
    added = [p for _, _, parts, _ in sums if len(parts) > 1 for p in parts if p[0] not in held_in]
    n_loads = sum(p[0] not in held_in for _, _, parts, _ in sums for p in parts)

    def body(scal_ref, *refs):
        ins, refs = refs[: len(arrays)], refs[len(arrays) :]
        outs, refs = refs[: len(shapes)], refs[len(shapes) :]
        bufs, in_sems = list(refs[: len(added)]), refs[len(added)]
        work, count = [], 0
        for out, lead, parts, norm in sums:
            lead = (lead(scal_ref),) if callable(lead) else lead
            dst = outs[out].at[lead] if lead else outs[out]
            copies, held = [], []
            for at, index in parts:
                from_ = index(scal_ref)
                src = ins[at].at[from_] if from_ else ins[at]
                if at in held_in:
                    held.append(src)
                    continue
                to = bufs.pop(0) if len(parts) > 1 else dst
                copies.append(pltpu.make_async_copy(src, to, in_sems.at[count]))
                copies[-1].start()
                held.append(to)
                count += 1
            work.append((dst, copies, held, norm))
        for dst, copies, held, norm in work:
            for copy in copies:
                copy.wait()
            if len(held) == 1 and not copies:
                dst[...] = held[0][...]
            if len(held) > 1:
                exact = len(held) == 2 and not norm and all(ref.dtype == BF16 for ref in held)
                total = None
                for ref in held:
                    value = ref[...] if exact else ref[...].astype(F32)
                    total = value if total is None else total + value
                dst[...] = (layer_norm(total) if norm else total).astype(dst.dtype)

    hbm, anywhere = pl.BlockSpec(memory_space=pltpu.HBM), pl.BlockSpec(memory_space=pl.ANY)
    return pl.pallas_call(
        body,
        in_specs=[pl.BlockSpec(memory_space=pltpu.SMEM)]
        + [
            pl.BlockSpec(memory_space=pltpu.VMEM) if n in held_in else hbm if a.ndim == 6 else anywhere
            for n, a in enumerate(arrays)
        ],
        out_specs=[pl.BlockSpec(memory_space=pltpu.VMEM)] * len(shapes),
        out_shape=[jax.ShapeDtypeStruct(shape, dtype) for shape, dtype in shapes],
        scratch_shapes=[pltpu.VMEM((SLOTS, D), arrays[at].dtype) for at, _ in added]
        + [pltpu.SemaphoreType.DMA((max(n_loads, 1),))],
        compiler_params=pltpu.CompilerParams(vmem_limit_bytes=VMEM),
        cost_estimate=cost(),
        name=name,
    )(scal, *(in_hbm(a) if a.ndim == 6 else a for a in arrays))


def pack(place, tables):
    sums = [(0, (x,), [(0, lambda s, x=x: (x, 1 - s[1], 1 - s[2], 1))], False) for x in range(NX)]
    return block_sums("pack", place, [tables], [((NX, SLOTS, D), BF16)], sums)[0]


def pack_all(place, tables):
    sums = [
        (n, (x,), [(0, lambda s, x=x, side=side: (x, side(s), 1 - s[2], 0))], False)
        for x in range(NX)
        for n, side in enumerate(SIDES)
    ]
    return block_sums("pack_all", place, [tables], [((NX, SLOTS, D), BF16)] * 2, sums)


def over_y(place, tables, got):
    sums = [
        (0, (x,), [(0, lambda s, x=x: (x, 1 - s[1], s[2], 1)), (1, lambda s, x=x: (x,))], False)
        for x in range(NX)
    ]
    return block_sums("over_y", place, [tables, got], [((NX, SLOTS, D), BF16)], sums, (1,))[0]


def away_x(place, tables, got):
    sums = []
    for n, d in enumerate(HOPS):
        for m, side in enumerate(SIDES):
            at = lambda s, d=d: lax.rem(s[0] + d, NX)
            parts = [
                (0, lambda s, at=at, side=side: (at(s), side(s), s[2], 0)),
                (1 + m, lambda s, at=at: (at(s),)),
            ]
            sums.append((n, side, parts, False))
    for n in range(NX):
        sums.append((3, (n,), [(0, lambda s, n=n: (n, s[1], 1 - s[2], 1))], False))
    shapes = [((2, SLOTS, D), BF16)] * 3 + [((NX, SLOTS, D), BF16)]
    return block_sums("away_x", place, [tables] + list(got), shapes, sums, (1, 2))


def join_x(place, tables, got, arrived, got1, side1):
    arrays = [tables] + list(got) + list(arrived) + [got1, side1]
    sums = []
    for n in (1, 0):
        side = SIDES[n]
        parts = [(0, lambda s, side=side: (s[0], side(s), s[2], 0)), (1 + n, lambda s: (s[0],))]
        parts += [(3 + k, lambda s, side=side: (side(s),)) for k in range(3)]
        sums.append((n, (), parts, False))
    parts = [(0, lambda s: (s[0], s[1], s[2], 1)), (6, lambda s: (s[0],)), (7, lambda s: (s[0],))]
    sums.append((2, (), parts, False))
    shapes = [((SLOTS, D), F32), ((SLOTS, D), BF16), ((SLOTS, D), F32)]
    return block_sums("join_x", place, arrays, shapes, sums)


def join_y(place, tables, got, arrived):
    sums = []
    for n, d in enumerate(HOPS):
        at = lambda s, d=d: lax.rem(s[0] + d, NX)
        parts = [
            (0, lambda s, at=at: (at(s), s[1], s[2], 1)),
            (1, lambda s, at=at: (at(s),)),
            (2, lambda s, at=at: (at(s),)),
        ]
        sums.append((n, (), parts, False))
    return block_sums("join_y", place, [tables, got, arrived], [((SLOTS, D), BF16)] * 3, sums, (2,))


def norm_sum(place, arrays):
    parts = [(n, lambda s: ()) for n in range(len(arrays))]
    held_in = range(len(arrays))
    return block_sums("norm_sum", place, arrays, [((SLOTS, D), BF16)], [(0, (), parts, True)], held_in)[0]


def norm_both(place, first, second):
    parts = [(n, lambda s: ()) for n in range(len(first) + 1)]
    sums = [(0, (1,), parts[-1:], False), (0, (0,), parts[:-1], True)]
    arrays = list(first) + [second]
    return block_sums("norm_both", place, arrays, [((2, SLOTS, D), BF16)], sums, range(len(arrays)))[0]


def in_vmem(array):
    return pltpu.with_memory_space_constraint(array, pltpu.VMEM)


def kernel_call(body, name, arrays, out_shape, scratch, scalars=None, aliases=None, out=pltpu.VMEM):
    vmem = pl.BlockSpec(memory_space=pltpu.VMEM)
    in_specs, args = [vmem] * len(arrays), [in_vmem(array) for array in arrays]
    if scalars is not None:
        in_specs = [pl.BlockSpec(memory_space=pltpu.SMEM)] + in_specs
        args = [scalars] + args
    return pl.pallas_call(
        body,
        in_specs=in_specs,
        out_specs=[pl.BlockSpec(memory_space=out)] * len(out_shape),
        out_shape=out_shape,
        scratch_shapes=scratch,
        input_output_aliases=aliases or {},
        compiler_params=pltpu.CompilerParams(vmem_limit_bytes=VMEM),
        cost_estimate=cost(),
        name=name,
    )(*args)


def cand_kernel(owner_ref, feats_ref, w_ref, xs_ref, u_ref, q_ref, back_ref, a_ref):
    second = owner_ref[...].astype(F32)
    r_from = lax.broadcasted_iota(jnp.int32, (ROWS, ROWS), 0)
    r_to = lax.broadcasted_iota(jnp.int32, (ROWS, ROWS), 1)
    upper = jnp.where(r_from <= r_to, 1.0, 0.0).astype(BF16)
    ones_before = mm(jnp.broadcast_to(second, (8, ROWS)).astype(BF16), upper)[:1]
    index = lax.broadcasted_iota(jnp.int32, (1, ROWS), 1).astype(F32)
    n_first = ROWS - jnp.sum(second, axis=1, keepdims=True)
    place = jnp.where(second > 0.5, n_first + ones_before - 1.0, index - ones_before)
    onehot = jnp.where(r_from == place.astype(jnp.int32), 1.0, 0.0)
    back_ref[...] = onehot.T.astype(BF16)
    onehot = onehot.astype(BF16)
    x = layer_norm(feats_ref[...].astype(F32)).astype(BF16)
    xs_ref[...] = mm(onehot, x).astype(BF16)

    @pl.loop(0, D // GROUP)
    def _(g):
        cols = lambda n: pl.ds(pl.multiple_of(n * D + g * GROUP, GROUP), GROUP)
        u, v, q, k = (silu(mm(xs_ref[...], w_ref[:, cols(n)])).astype(BF16) for n in range(4))
        u_ref[:, cols(0)] = u
        q_ref[:, cols(0)] = q
        prod = q.astype(F32) * k.astype(F32)
        for h in range(GROUP // HD):
            hc = slice(h * HD, (h + 1) * HD)
            half = jnp.sum(prod[:, hc], axis=-1, keepdims=True) * HALF_SCALE
            own = (half + half * jnp.tanh(half)).astype(BF16).astype(F32)
            out_cols = pl.ds(pl.multiple_of(g * GROUP + h * HD, HD), HD)
            a_ref[:, out_cols] = own * v[:, hc].astype(F32)


def cand_project(owner_row, feats, w_in):
    rows = jax.ShapeDtypeStruct((ROWS, D), BF16)
    out_shape = [rows, rows, rows, jax.ShapeDtypeStruct((ROWS, ROWS), BF16), jax.ShapeDtypeStruct((ROWS, D), F32)]
    return kernel_call(cand_kernel, "cand_project", [owner_row, feats, w_in], out_shape, [])


def absorb_kernel(plan, scal_ref, *refs):
    pieces, first, final = plan
    count = len(pieces)
    refs = list(refs)
    take = lambda n: [refs.pop(0) for _ in range(n)]
    x_refs = take(count)
    w_ref, q_ref, a_ref = take(3)
    if not first:
        qh_ref, ah_ref = take(2)
    if final:
        uh_ref, own_ref, u_ref, xs_ref, back_ref, wo_ref, hist_ref, cand_ref = take(8)
    elif first:
        _, ah_ref, qh_ref, uh_ref = take(4)
    else:
        take(2)
    k_scr, v_scr = take(2)
    row_iota = lax.broadcasted_iota(jnp.int32, (SLOTS, 1), 0)
    ahead = lax.broadcasted_iota(jnp.int32, (SLOTS, SLOTS), 0) - lax.broadcasted_iota(
        jnp.int32, (SLOTS, SLOTS), 1
    )
    offs = [scal_ref[0, 4 + piece] for piece in pieces]
    my_off = scal_ref[0, 3]

    steps = D // GROUP

    def column(n, g):
        return slice(n * D + g * GROUP, n * D + (g + 1) * GROUP)

    def project(g, n):
        x = x_refs[n][...].reshape(2 * SLOTS, D)
        if first and n == 0:
            qh_ref[:, column(0, g)] = silu(mm(x, w_ref[:, column(2, g)])).astype(BF16)
            uh_ref[:, column(0, g)] = silu(mm(x, w_ref[:, column(0, g)])).astype(BF16)
        k = silu(mm(x, w_ref[:, column(3, g)])).astype(BF16)
        v = silu(mm(x, w_ref[:, column(1, g)])).astype(BF16)
        to = slice(n * SLOTS, (n + 1) * SLOTS)
        for user in (0, 1):
            at = slice(user * SLOTS, (user + 1) * SLOTS)
            live = row_iota < scal_ref[user, 0] - offs[n]
            k_scr[g % 2, user, to, :] = k[at]
            v_scr[g % 2, user, to, :] = jnp.where(live, v[at], jnp.zeros_like(v[at]))

    def attend(g, user, h, turn):
        row_lo, row_hi = scal_ref[user, 1], scal_ref[user, 2]
        covered = starts[user] + WINDOW
        start = pl.multiple_of(jnp.where(turn == 0, starts[user], ROWS - WINDOW), 16)
        rows = pl.ds(start, WINDOW)
        index = start + lax.broadcasted_iota(jnp.int32, (WINDOW, 1), 0)
        mine = (index >= jnp.where(turn == 0, row_lo, covered)) & (index < row_hi)
        mine_rows = slice(user * SLOTS, (user + 1) * SLOTS)
        hc = slice(h * HD, (h + 1) * HD)
        oc = slice(g * GROUP + h * HD, g * GROUP + (h + 1) * HD)
        q = jnp.concatenate([q_ref[rows, oc], qh_ref[mine_rows, oc]], axis=0)
        w = weights_of(q, k_scr[g % 2, user, :, hc])
        parts = []
        for n in range(count):
            part = w[WINDOW:, n * SLOTS : (n + 1) * SLOTS]
            seen = ahead >= offs[n] - my_off + turn * HIDE
            parts.append(jnp.where(seen, part, jnp.zeros_like(part)).astype(BF16))
        w = jnp.concatenate([w[:WINDOW].astype(BF16), jnp.concatenate(parts, axis=1)], axis=0)
        total = mm(w, v_scr[g % 2, user, :, hc])
        a_ref[rows, oc] += jnp.where(mine, total[:WINDOW], 0.0)
        ah_ref[mine_rows, oc] += total[WINDOW:]

    if first:
        ah_ref[...] = jnp.zeros((2 * SLOTS, D), F32)
    starts = [jnp.minimum((scal_ref[user, 1] // 16) * 16, ROWS - WINDOW) for user in (0, 1)]
    fits = [scal_ref[user, 2] <= starts[user] + WINDOW for user in (0, 1)]
    turns = jnp.where(fits[0] & fits[1], 1, 2)
    pairs = [(user, h) for user in (0, 1) for h in range(GROUP // HD)]

    @pl.loop(0, turns)
    def _(turn):
        for n in range(count):
            project(0, n)
        for g in range(steps):
            left = list(range(count)) if g + 1 < steps else []
            gap = max(1, len(pairs) // max(1, len(left)))
            for i, (user, h) in enumerate(pairs):
                if left and i % gap == 0:
                    project(g + 1, left.pop(0))
                attend(g, user, h, turn)
            for n in left:
                project(g + 1, n)

    if final:
        y_scr, hist_vm, cand_vm, sems = take(4)
        block = 2 * SLOTS
        half = D // 2

        def normed(n):
            sums, gate = (ah_ref, uh_ref) if n == 0 else (a_ref, u_ref)
            rows = slice(max(n - 1, 0) * block, (max(n - 1, 0) + 1) * block)
            y = layer_norm(sums[rows, :]) * gate[rows, :].astype(F32)
            y_scr[n * block : (n + 1) * block, :] = y.astype(BF16)

        stores = [pltpu.make_async_copy(hist_vm, hist_ref, sems.at[0])]
        for n in range(2):
            cols = slice(n * half, (n + 1) * half)
            stores.append(
                pltpu.make_async_copy(cand_vm.at[:, cols], cand_ref.at[:, cols], sems.at[1 + n])
            )
        normed(0)
        for n in range(1 + ROWS // block):
            at = slice(n * block, (n + 1) * block)
            res = mm(y_scr[at, :], wo_ref[...])
            if n < ROWS // block:
                normed(n + 1)
            if n == 0:
                res = res + own_ref[...].reshape(block, D).astype(F32)
                for user in (0, 1):
                    keep = my_off + row_iota < scal_ref[user, 0]
                    out = res[user * SLOTS : (user + 1) * SLOTS]
                    hist_vm[user] = jnp.where(keep, out, 0.0).astype(BF16)
                stores[0].start()
            else:
                rows = slice((n - 1) * block, n * block)
                y_scr[at, :] = (res + xs_ref[rows, :].astype(F32)).astype(BF16)
        for n in range(2):
            cols = slice(n * half, (n + 1) * half)
            cand_vm[:, cols] = mm(back_ref[...], y_scr[block:, cols]).astype(BF16)
            stores[1 + n].start()
        for store in stores:
            store.wait()


def absorb(name, scal, items, w_in, q_cand, a_cand, state=None, final=None):
    pieces = tuple(item[0] for item in items)
    arrays = [item[1] for item in items] + [w_in, q_cand, a_cand]
    a_at = len(arrays)
    scratch = [pltpu.VMEM((2, 2, len(pieces) * SLOTS, GROUP), BF16)] * 2
    sums = jax.ShapeDtypeStruct((2 * SLOTS, D), F32)
    rows = jax.ShapeDtypeStruct((2 * SLOTS, D), BF16)
    out_shape = [jax.ShapeDtypeStruct((ROWS, D), F32), sums]
    aliases = {a_at: 0}
    first = state is None
    if first:
        out_shape += [rows, rows]
    else:
        arrays += [state[0], state[2]]
        aliases[a_at + 2] = 1
    if final is not None:
        arrays += [state[1]] + list(final)
        out_shape = [jax.ShapeDtypeStruct((2, SLOTS, D), BF16), jax.ShapeDtypeStruct((ROWS, D), BF16)]
        aliases = {}
        scratch += [
            pltpu.VMEM((2 * SLOTS + ROWS, D), BF16),
            pltpu.VMEM((2, SLOTS, D), BF16),
            pltpu.VMEM((ROWS, D), BF16),
            pltpu.SemaphoreType.DMA((3,)),
        ]
    outs = kernel_call(
        functools.partial(absorb_kernel, (pieces, first, final is not None)),
        name,
        arrays,
        out_shape,
        scratch,
        scal,
        aliases,
        pl.ANY if final is not None else pltpu.VMEM,
    )
    if final is not None:
        return outs
    return outs[0], (outs[2], outs[3], outs[1]) if first else (state[0], state[1], outs[1])


def user_perm(dx, dy, dcore):
    pairs = []
    for u in range(4 * NX):
        x, y, core = u >> 2, (u >> 1) & 1, u & 1
        pairs.append((u, (((x + dx) % NX) * 2 + (y ^ dy)) * 2 + (core ^ dcore)))
    return pairs


def cand_perm(dz, dy):
    return [(c, (((c >> 1) + dz) % NZ) * 2 + ((c & 1) ^ dy)) for c in range(2 * NZ)]


def to_user(array, dx, dy, dcore):
    return lax.ppermute(array, "user", user_perm(dx, dy, dcore))


def to_cand(array, dz, dy):
    return lax.ppermute(array, "cand", cand_perm(dz, dy))


def local(pooled, cand_feats, hist_len, cand_user, w_in, w_out):
    user = lax.axis_index("user")
    cand = lax.axis_index("cand")
    x, y, core = user >> 2, (user >> 1) & 1, user & 1
    z, y_hi = cand >> 1, cand & 1
    owner = cand_user - 2 * user
    n_first = ROWS - jnp.sum(owner)
    offsets = [SLOTS * (((z + dz + NZ) % NZ) * 2 + (y_hi ^ e)) for dz in SHIFTS for e in range(2)]
    scal = jnp.stack(
        [
            jnp.stack([hist_len[0], 0 * user, n_first, cand * SLOTS] + offsets),
            jnp.stack([hist_len[1], n_first, 0 * user + ROWS, cand * SLOTS] + offsets),
        ]
    ).astype(jnp.int32)

    tables = pooled.reshape(NX, 2, 2, 2, SLOTS, D)
    place = jnp.stack([x, y, core]).astype(jnp.int32)
    with jax.named_scope("sum_core"):
        pack1 = pack(place, tables)
        got1 = to_user(pack1, 0, 0, 1)
        pack0 = pack_all(place, after(tables, pack1))
        got0 = [to_user(part, 0, 0, 1) for part in pack0]
    with jax.named_scope("sum_y_second"):
        over1 = over_y(place, tables, after(got1, pack0))
        y1 = to_user(over1, 0, 1, 0)
    with jax.named_scope("sum_x_first"):
        *away0, pack2 = away_x(place, tables, after(got0, over1))
        x0 = [to_user(part, d, 0, 0) for part, d in zip(away0, HOPS)]
    with jax.named_scope("sum_core"):
        got2 = to_user(pack2, 0, 0, 1)
    owner_row, scal = after((owner.reshape(1, ROWS), scal), pack2)
    xs, u_cand, q_cand, back, a_cand = cand_project(owner_row, cand_feats, w_in)
    with jax.named_scope("sum_y_second"):
        y1 = after(y1, xs, scal)
        away1 = join_y(place, tables, got2, y1)
        x1 = [to_user(part, d, 0, 0) for part, d in zip(away1, HOPS)]
    with jax.named_scope("sum_x_first"):
        mine0, over0, mine1 = join_x(place, tables, got0, after(x0, away1), got2, y1)
        y0 = to_user(over0, 0, 1, 0)
    with jax.named_scope("gather"):
        own1 = norm_sum(place, [mine1] + after(x1, mine0))
        own = norm_both(place, [mine0, after(y0, own1)], own1)
        near = to_cand(own, 0, 1)
        own_left, own_right = to_cand(own, 1, 0), to_cand(own, -1, 0)
    put = functools.partial(absorb, scal=scal, w_in=w_in, q_cand=q_cand)
    piece = lambda shift, e: 2 * SHIFTS.index(shift) + e
    a_cand, state = put("own_keys", items=[(piece(0, 0), own)], a_cand=a_cand)
    with jax.named_scope("gather"):
        near = after(near, a_cand)
        near_left, near_right = to_cand(near, 1, 0), to_cand(near, -1, 0)
        own_left, own_right = after((own_left, own_right), near)
        own_far = to_cand(own_left, 1, 0)
    a_cand, state = put(
        "own_sides",
        items=[(piece(-1, 0), own_left), (piece(1, 0), own_right), (piece(0, 1), near)],
        a_cand=a_cand,
        state=state,
    )
    with jax.named_scope("gather"):
        near_left, near_right = after((near_left, near_right), a_cand)
        near_far = to_cand(near_right, -1, 0)
    a_cand, state = put(
        "near_sides",
        items=[(piece(-1, 1), near_left), (piece(1, 1), near_right)],
        a_cand=a_cand,
        state=state,
    )
    return put(
        "far_finish",
        items=[(piece(2, 0), own_far), (piece(2, 1), near_far)],
        a_cand=a_cand,
        state=state,
        final=(own, u_cand, xs, back, w_out),
    )


def solution(mesh):
    placed = (
        P("user", None, "cand", None),
        P(("user", "cand"), None),
        P("user"),
        P(("user", "cand")),
        P(),
        P(),
    )
    return jax.shard_map(
        local,
        mesh=mesh,
        in_specs=placed,
        out_specs=(P("user", "cand", None), P(("user", "cand"), None)),
        check_vma=False,
    )
```
